256 devices in a mesh: section: 8 (over y_hi, x), dp: 32 (over y_lo, z, core).
Axes of the slice: x: 4, y: 4 (y_hi: 2, y_lo: 2; y = y_hi * 2 + y_lo), z: 8, core: 2. Of those that a mesh axis runs over, the one named last changes fastest.
Arguments:
- section_inputs: bfloat16 [8, 4096, 2048], P('section', 'dp'), as said below
- section_weights: bfloat16 [8, 2048, 2048], P('section'), may hold values from -0.125 to 0.125
- memory_weights: bfloat16 [8, 2048, 2048], P('section', 'dp'), may hold values from -0.125 to 0.125
- norm_gains: float32 [8, 2048], P('section'), may hold values from 0.1 to 1.9
- memory: bfloat16 [4096, 2048], P('dp'), may hold values from -5 to 5
- cotangent: bfloat16 [4096, 2048], P('dp'), may hold values from -3 to 3
- lengths: int32 [32], P('dp'), may hold values from 32 to 128, as said below
Outputs:
- input_grads: bfloat16 [8, 4096, 2048], P('section', 'dp')
- weight_grads: float32 [8, 2048, 2048], P('section', 'dp')
- gain_grads: float32 [8, 2048], P('section', 'dp')
The draws below stay inside these ranges and needn't reach their ends.
Inputs may be any that keep to these rules, and one draw needn't show every extreme that they name: `section_inputs`: saved activations with uneven scales over tokens and features. `lengths`: tokens of a sequence at positions below its entry are live, the rest padding; some sequence is full and some has 32 live tokens.
All inputs are finite; a program needn't handle non-finite values.
Results may differ from the reference program's by a relative error of at most 0.035.
Values may be sent and summed in bfloat16 or wider, within the bound.
A program may use at most 128 MiB of HBM per device.

```python
import math
import jax
import jax.numpy as jnp
from jax import lax

D = 2048
LEN = 128
SECTIONS = 8
HALF = 4
TOK_DEV = 128
TOKENS = 4096
SEQS = 32
N_DP = 32


def draw_section_inputs(key, part):
    key = jax.random.fold_in(key, 11)
    key_base, key_rows, key_cols = jax.random.split(key, 3)
    shape = (SECTIONS, TOKENS, D)
    col_scale = jnp.exp(jax.random.uniform(key_cols, (SECTIONS, 1, D), jnp.float32, math.log(0.4), math.log(4.0)))
    row_scale = jnp.exp(jax.random.uniform(key_rows, (SECTIONS, TOKENS, 1), jnp.float32, math.log(0.3), math.log(3.0)))
    base = jax.random.normal(key_base, shape, jnp.float32)
    values = row_scale * col_scale * base
    return values.astype(jnp.bfloat16)


def draw_lengths(key, part):
    key = jax.random.fold_in(key, 23)
    key_len, key_top, key_low = jax.random.split(key, 3)
    drawn = jax.random.randint(key_len, (SEQS,), LEN // 4, LEN + 1)
    top_index = jax.random.randint(key_top, (), 0, SEQS)
    low_index = (top_index + 1 + jax.random.randint(key_low, (), 0, SEQS - 1)) % SEQS
    places = jnp.arange(SEQS, dtype=jnp.int32)
    drawn = jnp.where(places == top_index, LEN, drawn)
    drawn = jnp.where(places == low_index, LEN // 4, drawn)
    return drawn.astype(jnp.int32)


def strengthened(entries, key, source, target, blocks, factor):
    owner, partner = [(jnp.arange(entries.shape[dim]) // (entries.shape[dim] // blocks)).reshape([-1 if axis == dim else 1 for axis in range(entries.ndim)]) for dim in (source, target)]
    chosen = jax.random.permutation(key, blocks)[partner]
    strong = (owner == chosen) | (owner == (partner + blocks // 2) % blocks)
    return jnp.where(strong, factor * entries, entries)


def block_levels(rng, extent, cuts, least, top_value):
    level, own = 1.0, jax.random.fold_in(rng, 6)
    for dim, parts in cuts:
        steps = jnp.exp(jax.random.uniform(jax.random.fold_in(own, dim), (parts,), jnp.float32, least / len(cuts), top_value / len(cuts)))
        level = level * jnp.repeat(steps, extent[dim] // parts).reshape([-1 if axis == dim else 1 for axis in range(len(extent))])
    return level


def scatter_about(stream_key, shape, deviation, most, cuts=(), kind=jnp.bfloat16):
    level = block_levels(stream_key, shape, cuts, -0.22, 0.18) if cuts else 1.0
    values = jax.random.normal(stream_key, shape, jnp.float32) * deviation * level
    return jnp.minimum(jnp.maximum(values, -most), most).astype(kind)


def gaussian_with(key, extent, spread, most, pieces, heavy, held_as=jnp.bfloat16):
    entries = spread * jax.random.normal(key, extent, jnp.float32)
    if pieces:
        entries = entries * block_levels(key, extent, pieces, -0.22, 0.18)
    return jnp.clip(strengthened(entries, jax.random.fold_in(key, 3), *heavy), -most, most).astype(held_as)


def setup_inputs(seed: int = 0) -> dict:
    key_of = jax.random.split(jax.random.key(seed), 8)
    section_inputs = draw_section_inputs(jax.random.fold_in(key_of[7], 71), 0)
    section_weights = scatter_about(key_of[1], (SECTIONS, D, D), D ** -0.5, 0.125, ((0, 8),))
    memory_weights = scatter_about(key_of[2], (SECTIONS, D, D), D ** -0.5, 0.125, ((0, 8), (1, 32)))
    norm_gains = jnp.clip(1.0 + 0.18 * jax.random.normal(key_of[3], (SECTIONS, D), jnp.float32), 0.1, 1.9)
    memory = scatter_about(key_of[4], (TOKENS, D), 1.0, 5.0, ((0, 32),))
    cotangent = gaussian_with(key_of[5], (TOKENS, D), 0.5, 3.0, ((0, 32),), (0, 1, 32, 2.75))
    lengths = draw_lengths(jax.random.fold_in(key_of[7], 71), 0)
    return dict(section_inputs=section_inputs, section_weights=section_weights, memory_weights=memory_weights, norm_gains=norm_gains, memory=memory, cotangent=cotangent, lengths=lengths)


epsilon = 1e-06

def section_backward(activations, weight, gain_row, gate_values, incoming):
    wide = activations.astype(jnp.float32)
    inv_rms = lax.rsqrt(lax.optimization_barrier(jnp.mean(wide * wide, axis=1, keepdims=True)) + epsilon)
    normed = wide * inv_rms
    scaled = (normed * gain_row).astype(jnp.bfloat16)
    preact = jnp.dot(scaled, weight, preferred_element_type=jnp.float32)
    sigmoid_vals = jax.nn.sigmoid(preact)
    activation = preact * sigmoid_vals
    slope_vals = sigmoid_vals * (1.0 + preact * (1.0 - sigmoid_vals))
    slope_gate = slope_vals * gate_values
    upstream = incoming.astype(jnp.float32)
    grad_pre = (upstream * slope_gate).astype(jnp.bfloat16)
    grad_scaled = jnp.dot(grad_pre, weight.T, preferred_element_type=jnp.float32)
    grad_normed = grad_scaled * gain_row
    center = lax.optimization_barrier(jnp.mean(grad_normed * normed, axis=1, keepdims=True))
    grad_input = (upstream + inv_rms * (grad_normed - normed * center)).astype(jnp.bfloat16)
    gain_terms = grad_scaled * normed
    grad_gate = (upstream * activation).astype(jnp.bfloat16)
    return (grad_input, grad_pre, gain_terms, grad_gate, scaled)

def replica_sums(scaled, grad_pre, gain_terms):

    def accumulate(totals, index):
        start = (index * TOK_DEV).astype(jnp.int32)
        scaled_part = lax.dynamic_slice_in_dim(scaled, start, TOK_DEV, 0)
        pre_part = lax.dynamic_slice_in_dim(grad_pre, start, TOK_DEV, 0)
        gain_part = lax.dynamic_slice_in_dim(gain_terms, start, TOK_DEV, 0)
        weight_part = jnp.dot(scaled_part.T, pre_part, preferred_element_type=jnp.float32)
        gain_sum = lax.optimization_barrier(jnp.sum(gain_part, axis=0))
        weight_part = lax.optimization_barrier(weight_part.astype(jnp.bfloat16)).astype(jnp.float32)
        gain_sum = lax.optimization_barrier(gain_sum.astype(jnp.bfloat16)).astype(jnp.float32)
        return ((totals[0] + weight_part, totals[1] + gain_sum), None)
    start_totals = (jnp.zeros((D, D), jnp.float32), jnp.zeros((D,), jnp.float32))
    totals, _ = lax.scan(accumulate, start_totals, jnp.arange(N_DP, dtype=jnp.int32))
    return (totals[0] / N_DP, totals[1] / N_DP)

def reference(section_inputs, section_weights, memory_weights, norm_gains, memory, cotangent, lengths):
    position = jnp.arange(TOKENS, dtype=jnp.int32)
    limits = lengths[position // LEN]
    valid_mask = (position % LEN < limits).astype(jnp.bfloat16)
    incoming = cotangent * valid_mask[:, None]
    encoder_gate = jnp.ones((TOKENS, D), jnp.float32)
    memory_grad = jnp.zeros((TOKENS, D), jnp.float32)
    input_list = [None] * SECTIONS
    weight_list = [None] * SECTIONS
    gain_list = [None] * SECTIONS
    for section_num in range(SECTIONS - 1, -1, -1):
        if section_num == HALF - 1:
            incoming = memory_grad.astype(jnp.bfloat16)
        if section_num >= HALF:
            gate_values = jnp.dot(memory, memory_weights[section_num], preferred_element_type=jnp.float32)
        else:
            gate_values = encoder_gate
        grad_input, grad_pre, gain_terms, grad_gate, scaled = section_backward(section_inputs[section_num], section_weights[section_num], norm_gains[section_num], gate_values, incoming)
        if section_num >= HALF:
            memory_grad = memory_grad + jnp.dot(grad_gate, memory_weights[section_num].T, preferred_element_type=jnp.float32)
        input_list[section_num] = grad_input
        weight_mean, gain_mean = replica_sums(scaled, grad_pre, gain_terms)
        weight_list[section_num] = weight_mean
        gain_list[section_num] = gain_mean
        incoming = grad_input
    return (jnp.stack(input_list), jnp.stack(weight_list), jnp.stack(gain_list))
```

```python
import functools

import jax
import jax.numpy as jnp
from jax import lax
from jax.experimental import pallas as pl
from jax.experimental.pallas import tpu as pltpu
from jax.sharding import PartitionSpec as P

epsilon = 1e-06
BF = jnp.bfloat16
F32 = jnp.float32
CH = 16
TILE = 256
COLS = 128


class Gather:
    def __init__(self, block, rows, place, send_sems, recv_sems, both_cores):
        self.block, self.rows = block, rows
        self.y, self.z, self.c, self.nz, self.device = place
        self.far = self.nz // 2
        self.ss, self.rs = send_sems, recv_sems
        self.both = both_cores

    @staticmethod
    def count(nz, both):
        ids = 1 + 2 * (nz // 2) * 3 + 1 + 2 * (nz // 2)
        return 2 * ids + 1 if both else ids

    @property
    def ids(self):
        return self.count(self.nz, False)

    def copy(self, q, start, size, ident, dev):
        ref = self.block(q, start, size)
        return pltpu.make_async_remote_copy(
            src_ref=ref, dst_ref=ref, send_sem=self.ss.at[ident], recv_sem=self.rs.at[ident],
            device_id=dev, device_id_type=pl.DeviceIdType.MESH)

    def turn(self, z):
        return lax.rem(z + 2 * self.nz, self.nz)

    def z_id(self, way, d, m):
        return 1 + (way * self.far + d - 1) * 3 + m

    def y_id(self, way, d):
        base = 1 + 2 * self.far * 3
        return base if d == 0 else base + 1 + way * self.far + d - 1

    def span(self, way, d, m):
        half = self.rows // 2
        start, size = (half if m == 1 else 0), half
        if d == self.far:
            size = half // 2
            start = start + way * size
        return start, size

    def z_copy(self, way, d, m, sending):
        sign = 1 - 2 * way
        src = self.turn(self.z - sign * (d - 1 if sending else d))
        y = 1 - self.y if m == 2 else self.y
        start, size = self.span(way, d, m)
        dev = self.device(self.y, self.turn(self.z + sign), self.c)
        return self.copy(y * self.nz + src, start, size, self.z_id(way, d, m), dev)

    def y_copy(self, way, d, sending):
        src = self.turn(self.z - (1 - 2 * way) * d)
        y = self.y if sending else 1 - self.y
        start, size = self.span(way, d, 1)
        dev = self.device(1 - self.y, self.z, self.c)
        return self.copy(y * self.nz + src, start, size, self.y_id(way, d), dev)

    def first_copy(self, sending):
        y = self.y if sending else 1 - self.y
        dev = self.device(1 - self.y, self.z, self.c)
        return self.copy(y * self.nz + self.z, 0, self.rows // 2, 0, dev)

    def pair(self, ident, sending):
        dev = self.device(self.y, self.z, 1 - self.c)
        owner = self.c if sending else 1 - self.c
        other = Gather(functools.partial(self.block, lane=owner), self.rows,
                       (self.y, self.z, self.c, self.nz, self.device), self.ss, self.rs, False)
        kind, args = ident
        if kind == "own":
            return other.copy(self.y * self.nz + self.z, 0, self.rows, 2 * self.ids, dev)
        if kind == "first":
            return other.copy((1 - self.y) * self.nz + self.z, 0, self.rows // 2, self.ids, dev)
        if kind == "z":
            way, d, m = args
            src = self.turn(self.z - (1 - 2 * way) * d)
            y = 1 - self.y if m == 2 else self.y
            start, size = self.span(way, d, m)
            return other.copy(y * self.nz + src, start, size, self.ids + self.z_id(way, d, m), dev)
        way, d = args
        src = self.turn(self.z - (1 - 2 * way) * d)
        start, size = self.span(way, d, 1)
        return other.copy((1 - self.y) * self.nz + src, start, size, self.ids + self.y_id(way, d), dev)

    def hand(self, kind, args=()):
        if self.both:
            self.pair((kind, args), True).start()

    def begin(self):
        self.first_copy(True).start()
        for m in (0, 1):
            for way in (0, 1):
                self.z_copy(way, 1, m, True).start()
        self.y_copy(0, 0, True).start()
        self.hand("own")

    def begin_other(self):
        self.first_copy(False).wait_recv()
        for way in (0, 1):
            self.z_copy(way, 1, 2, True).start()
        self.hand("first")

    def step(self, d):
        for m in (0, 1, 2):
            for way in (0, 1):
                self.z_copy(way, d, m, False).wait_recv()
                if d < self.far:
                    self.z_copy(way, d + 1, m, True).start()
                if m == 1:
                    self.y_copy(way, d, True).start()
                self.hand("z", (way, d, m))

    def ways(self, d):
        return (0,) if d == 0 else (0, 1)

    def collect(self, d):
        for way in self.ways(d):
            self.y_copy(way, d, False).wait_recv()
            self.hand("y", (way, d))
        if self.both:
            if d == 0:
                self.pair(("own", ()), False).wait_recv()
                self.pair(("first", ()), False).wait_recv()
            else:
                for way in (0, 1):
                    for m in (0, 1, 2):
                        self.pair(("z", (way, d, m)), False).wait_recv()
            for way in self.ways(d):
                self.pair(("y", (way, d)), False).wait_recv()

    def sent(self):
        self.first_copy(True).wait_send()
        for d in range(1, self.far + 1):
            for way in (0, 1):
                for m in (0, 1, 2):
                    self.z_copy(way, d, m, True).wait_send()
        for d in range(self.far + 1):
            for way in self.ways(d):
                self.y_copy(way, d, True).wait_send()
        if self.both:
            self.pair(("own", ()), True).wait_send()
            self.pair(("first", ()), True).wait_send()
            for d in range(self.far + 1):
                for way in self.ways(d):
                    self.pair(("y", (way, d)), True).wait_send()
                    if d:
                        for m in (0, 1, 2):
                            self.pair(("z", (way, d, m)), True).wait_send()

    def sources(self, d):
        spots = {0: (0,), self.far: (self.far,)}.get(d, (d, -d))
        return [y * self.nz + self.turn(self.z + o) for o in spots for y in (0, 1)]


def relay_kernel(n_sec, n_dp,
                 x_ref, w_hbm, mw_hbm, gain_ref, mem_ref, cot_ref, len_ref,
                 gin_ref, dw_ref, gg_ref,
                 wv, wt, mwv, mwt, sg, normed, slope, act, inv, gbuf, tbuf, tsend,
                 gpv, gacc, gs, gpg, gpt, dws, dwp, dwo, og, gnl, gnp,
                 load_sem, wag_s, wag_r, sag_s, sag_r, g_s, g_r, t_s, t_r, late_s, late_r, tail_s, tail_r):
    s = lax.axis_index("section")
    j = lax.axis_index("dp")
    half = n_sec // 2
    nq = n_dp // 2
    nz = nq // 2
    c = lax.rem(j, 2)
    q0 = j // 2
    y, z = q0 // nz, lax.rem(q0, nz)
    toks, feats = x_ref.shape
    rw = mw_hbm.shape[0]
    n_ch = toks // CH
    tiles = feats // TILE
    decoder = s >= half
    encoder = s < half
    MESH = pl.DeviceIdType.MESH

    def device(yy, zz, cc):
        return {"dp": (yy * nz + zz) * 2 + cc}

    load_w = pltpu.make_async_copy(w_hbm, wv, load_sem.at[0])
    load_w.start()
    load_m = pltpu.make_async_copy(
        mw_hbm, mwv.at[pl.ds(pl.multiple_of(j * rw, rw), rw)], load_sem.at[1])
    load_m.start()

    barrier = pltpu.get_barrier_semaphore()

    def greet(i, carry):
        q = lax.rem(q0 + i, nq)
        pl.semaphore_signal(barrier, inc=1, device_id={"dp": q * 2 + c}, device_id_type=MESH)
        return carry

    lax.fori_loop(1, nq, greet, 0)
    pl.semaphore_signal(barrier, inc=1, device_id={"dp": q0 * 2 + 1 - c}, device_id_type=MESH)

    @pl.when(s > 0)
    def _():
        pl.semaphore_signal(barrier, inc=1, device_id={"section": s - 1}, device_id_type=MESH)

    @pl.when(s < n_sec - 1)
    def _():
        pl.semaphore_signal(barrier, inc=1, device_id={"section": s + 1}, device_id_type=MESH)

    ends = (s == 0) | (s == n_sec - 1)
    pl.semaphore_wait(barrier, nq + jnp.where(ends, 1, 2))

    place = (y, z, c, nz, device)

    def w_block(q, start, size, lane=None):
        lane = c if lane is None else lane
        return mwv.at[pl.ds(pl.multiple_of((q * 2 + lane) * rw + start, 16), size)]

    def s_block(q, start, size):
        return sg.at[q, pl.ds(start, size)]

    wag = Gather(w_block, rw, place, wag_s, wag_r, True)
    sag = Gather(s_block, toks, place, sag_s, sag_r, False)
    far = wag.far

    load_m.wait()

    @pl.when(decoder)
    def _():
        wag.begin()

    def rows_of(k):
        return pl.ds(pl.multiple_of(k * CH, CH), CH)

    def norm_rows(k, carry):
        rows = rows_of(k)
        wide = x_ref[rows, :].astype(F32)
        scale = lax.rsqrt(jnp.mean(wide * wide, axis=1, keepdims=True) + epsilon)
        inv[rows, :] = jnp.broadcast_to(scale, (CH, 128))
        value = wide * scale
        normed[rows, :] = value
        sg[q0, rows, :] = (value * gain_ref[...]).astype(BF)
        return carry

    lax.fori_loop(0, n_ch, norm_rows, 0)

    @pl.when(encoder)
    def _():
        sag.begin()

    load_w.wait()

    def cols_of(t):
        return pl.ds(pl.multiple_of(t * TILE, TILE), TILE)

    def preact_tile(t, carry):
        cols = cols_of(t)
        p = jnp.dot(sg[q0], wv[:, cols], preferred_element_type=F32)
        sig = jax.nn.sigmoid(p)
        act[:, cols] = p * sig
        slope[:, cols] = sig * (1.0 + p * (1.0 - sig))
        return carry

    lax.fori_loop(0, tiles, preact_tile, 0)

    def turn_w(lo, hi):
        def body(i, carry):
            a, b = i // tiles, lax.rem(i, tiles)
            wt[cols_of(b), cols_of(a)] = wv[cols_of(a), cols_of(b)].T
            return carry

        lax.fori_loop(lo, hi, body, 0)

    def turn_m(d):
        for q in wag.sources(d):
            at = pl.ds(pl.multiple_of(q * 2 * rw, 2 * rw), 2 * rw)

            def body(t, carry, at=at):
                mwt[cols_of(t), at] = mwv[at, cols_of(t)].T
                return carry

            lax.fori_loop(0, tiles, body, 0)

    cut = tiles * tiles // 2

    @pl.when(decoder)
    def _():
        wag.begin_other()
        wag.step(1)
        wag.collect(0)
        turn_w(0, cut)
        turn_m(0)
        wag.step(2)
        wag.collect(1)
        turn_w(cut, 2 * cut)
        turn_m(1)
        wag.step(3)
        wag.collect(2)
        turn_m(2)
        wag.step(4)
        wag.collect(3)
        turn_m(3)
        wag.collect(4)

        def gate_tile(t, carry):
            cols = cols_of(t)
            g = jnp.dot(mem_ref[...], mwv[:, cols], preferred_element_type=F32)
            slope[:, cols] = slope[:, cols] * g
            return carry

        lax.fori_loop(0, tiles, gate_tile, 0)
        sag.begin()
        turn_m(4)

    @pl.when(encoder)
    def _():
        sag.begin_other()
        turn_w(0, cut)
        sag.step(1)
        turn_w(cut, 2 * cut)
        sag.step(2)
        sag.step(3)

    @pl.when(s == n_sec - 1)
    def _():
        live = lax.broadcasted_iota(jnp.int32, (toks, TILE), 0) < len_ref[...]

        def body(t, carry):
            cols = cols_of(t)
            gbuf[:, cols] = jnp.where(live, cot_ref[:, cols], jnp.zeros((), BF))
            return carry

        lax.fori_loop(0, tiles, body, 0)

    gacc[...] = jnp.zeros_like(gacc)

    def down(src, dst, k, send_sems, recv_sems):
        rows = rows_of(k)
        return pltpu.make_async_remote_copy(
            src_ref=src.at[rows], dst_ref=dst.at[rows], send_sem=send_sems.at[k], recv_sem=recv_sems.at[k],
            device_id={"section": s - 1}, device_id_type=MESH)

    def late(g, q, size=2 * CH):
        rows = pl.ds(pl.multiple_of(g * 2 * CH, 2 * CH), size)
        return pltpu.make_async_remote_copy(
            src_ref=gpv.at[rows, pl.ds(pl.multiple_of(q * COLS, COLS), COLS)], dst_ref=gpg.at[q0, rows],
            send_sem=late_s.at[g], recv_sem=late_r.at[g], device_id={"dp": q * 2 + c}, device_id_type=MESH)

    def late_send(g, size=2 * CH):
        def body(i, carry):
            late(g, lax.rem(q0 + i, nq), size).start()
            return carry

        lax.fori_loop(1, nq, body, 0)

    def late_done(g, size=2 * CH):
        ref = gpg.at[pl.ds(0, nq - 1), pl.ds(g * 2 * CH, size)]
        whole = pltpu.make_async_remote_copy(
            src_ref=ref, dst_ref=ref, send_sem=late_s.at[g], recv_sem=late_r.at[g],
            device_id={"dp": q0 * 2 + 1 - c}, device_id_type=MESH)
        whole.wait_send()
        whole.wait_recv()

    def term(k):
        rows = rows_of(k)
        up = gbuf[rows, :].astype(F32)
        grad_gate = (up * act[rows, :]).astype(BF)

        @pl.when(s < n_sec - 1)
        def _():
            down(tsend, tbuf, k, t_s, t_r).wait_recv()

        first = jnp.where(s < n_sec - 1, 1.0, 0.0)
        for t in range(tiles):
            cols = slice(t * TILE, (t + 1) * TILE)
            p = jnp.dot(grad_gate, mwt[:, cols], preferred_element_type=F32)
            tsend[rows, cols] = (p + jnp.where(first > 0, tbuf[rows, cols].astype(F32), 0.0)).astype(BF)

    def chunk(k, carry):
        rows = rows_of(k)

        @pl.when(s < n_sec - 1)
        def _():
            down(gin_ref, gbuf, k, g_s, g_r).wait_recv()

        @pl.when(s == half)
        def _():
            term(k)
            down(tsend, gbuf, k, t_s, g_r).start()

        gpv[rows, :] = (gbuf[rows, :].astype(F32) * slope[rows, :]).astype(BF)
        grad_pre = gpv[rows, :]
        total = jnp.zeros((CH, 128), F32)
        for t in range(tiles):
            cols = slice(t * TILE, (t + 1) * TILE)
            p = jnp.dot(grad_pre, wt[:, cols], preferred_element_type=F32)
            both = p * normed[rows, cols]
            gacc[:, cols] += both
            h = p * gain_ref[:, cols]
            gs[:, cols] = h
            weighted = both * gain_ref[:, cols]
            for i in range(TILE // 128):
                total = total + weighted[:, i * 128:(i + 1) * 128]
        center = jnp.sum(total, axis=1, keepdims=True) * (1.0 / feats)
        scale = inv[rows, 0:1]
        for t in range(tiles):
            cols = slice(t * TILE, (t + 1) * TILE)
            gin_ref[rows, cols] = (
                gbuf[rows, cols].astype(F32) + scale * (gs[:, cols] - normed[rows, cols] * center)
            ).astype(BF)

        @pl.when((s > 0) & (s != half))
        def _():
            down(gin_ref, gbuf, k, g_s, g_r).start()

        @pl.when(s > half)
        def _():
            term(k)
            down(tsend, tbuf, k, t_s, t_r).start()

        @pl.when((lax.rem(k, 2) == 1) & (k < n_ch - 1))
        def _():
            late_send(k // 2)

        @pl.when(encoder & (k == n_ch - 3))
        def _():
            sag.step(4)
            for d in range(far + 1):
                sag.collect(d)

        @pl.when(decoder & (k == jnp.maximum(s - half - 1, 0)))
        def _():
            sag.begin_other()

        @pl.when(decoder & (k == s - half + 1))
        def _():
            sag.step(1)

        @pl.when(decoder & (k == s - half + 5))
        def _():
            sag.step(2)

        return carry

    lax.fori_loop(0, n_ch, chunk, 0)

    gpv[toks:toks + CH, :] = gacc[...].astype(BF)
    groups = n_ch // 2
    late_send(groups - 1, 3 * CH)

    def own(g, carry):
        gpg[q0, rows_of(g), :] = gpv[rows_of(g), pl.ds(pl.multiple_of(q0 * COLS, COLS), COLS)]
        return carry

    lax.fori_loop(0, n_ch + 1, own, 0)

    @pl.when(decoder)
    def _():
        @pl.when(s == n_sec - 1)
        def _():
            sag.step(2)

        sag.step(3)
        sag.step(4)
        for d in range(far + 1):
            sag.collect(d)

    for g in range(groups):
        late_done(g, 3 * CH if g == groups - 1 else 2 * CH)

    gain_sum = jnp.zeros((8, COLS), F32)
    for q in range(nq):
        gpt[:, q * toks:(q + 1) * toks] = gpg[q, 0:toks, :].T
        part = gpg[q, toks:toks + CH, :].astype(F32)
        gain_sum = gain_sum + part[0:8] + part[8:16]
    gnl[...] = gain_sum

    other = {"dp": q0 * 2 + 1 - c}
    gain_copy = pltpu.make_async_remote_copy(
        src_ref=gnl, dst_ref=gnp, send_sem=tail_s.at[0], recv_sem=tail_r.at[0], device_id=other, device_id_type=MESH)
    gain_copy.start()

    per = TILE // (2 * rw)

    def product(t, carry):
        cols = cols_of(t)
        p = jnp.dot(gpt[...], sg[:, :, cols].reshape(nq * toks, TILE), preferred_element_type=F32)
        dws[pl.ds(t * per, per)] = p.T.astype(BF).reshape(per, 2, rw, COLS)
        return carry

    lax.fori_loop(0, tiles, product, 0)
    swap = pltpu.make_async_remote_copy(
        src_ref=dws.at[:, 1 - c], dst_ref=dwp, send_sem=tail_s.at[1], recv_sem=tail_r.at[1],
        device_id=other, device_id_type=MESH)
    swap.start()
    gain_copy.wait()
    gains = jnp.sum(gnl[...] + gnp[...], axis=0, keepdims=True) * (1.0 / n_dp)
    gg_ref[...] = jnp.where(c == 0, gains[:, 0:rw], gains[:, rw:2 * rw])
    swap.wait()

    def add_block(i, carry):
        q = lax.rem(q0 + 1 + i, nq)
        dwo[q] = (dws[q, c].astype(F32) + dwp[q].astype(F32)).astype(BF)

        @pl.when(i < nq - 1)
        def _():
            pltpu.make_async_remote_copy(
                src_ref=dwo.at[q], dst_ref=og.at[q0], send_sem=tail_s.at[2], recv_sem=tail_r.at[2],
                device_id={"dp": q * 2 + c}, device_id_type=MESH).start()

        return carry

    lax.fori_loop(0, nq, add_block, 0)
    og[q0] = dwo[q0]

    for k in range(n_ch):
        @pl.when((s > 0) & (s != half))
        def _(k=k):
            down(gin_ref, gbuf, k, g_s, g_r).wait_send()

        @pl.when(decoder)
        def _(k=k):
            down(tsend, tbuf, k, t_s, t_r).wait_send()

    sag.sent()

    @pl.when(decoder)
    def _():
        wag.sent()

    whole = pltpu.make_async_remote_copy(
        src_ref=dwo.at[pl.ds(0, nq - 1)], dst_ref=og.at[pl.ds(0, nq - 1)], send_sem=tail_s.at[2],
        recv_sem=tail_r.at[2], device_id=other, device_id_type=MESH)
    whole.wait_send()
    whole.wait_recv()
    for q in range(nq):
        dw_ref[:, q * COLS:(q + 1) * COLS] = og[q].astype(F32) * (1.0 / n_dp)


def local(section_inputs, section_weights, memory_weights, norm_gains, memory, cotangent, lengths):
    n_sec, n_dp = lax.axis_size("section"), lax.axis_size("dp")
    toks, feats = section_inputs.shape[1:]
    rw = memory_weights.shape[1]
    nq = n_dp // 2
    nz = nq // 2
    n_ch = toks // CH
    vmem = pl.BlockSpec(memory_space=pltpu.VMEM)
    hbm = pl.BlockSpec(memory_space=pl.ANY)
    square = pltpu.VMEM((feats, feats), BF)
    wide = pltpu.VMEM((toks, feats), F32)
    narrow = pltpu.VMEM((toks, feats), BF)
    blocks = pltpu.VMEM((nq, rw, COLS), BF)
    dma = pltpu.SemaphoreType.DMA
    gin, dw, gg = pl.pallas_call(
        functools.partial(relay_kernel, n_sec, n_dp),
        out_shape=(
            jax.ShapeDtypeStruct((toks, feats), BF),
            jax.ShapeDtypeStruct((rw, feats), F32),
            jax.ShapeDtypeStruct((1, rw), F32),
        ),
        in_specs=[vmem, hbm, hbm, vmem, vmem, vmem, vmem],
        out_specs=(vmem, vmem, vmem),
        scratch_shapes=[
            square, square, square, square,
            pltpu.VMEM((nq, toks, feats), BF),
            wide, wide, wide,
            pltpu.VMEM((toks, 128), F32),
            narrow, narrow, narrow,
            pltpu.VMEM((toks + CH, feats), BF),
            pltpu.VMEM((CH, feats), F32),
            pltpu.VMEM((CH, feats), F32),
            pltpu.VMEM((nq, toks + CH, COLS), BF),
            pltpu.VMEM((COLS, nq * toks), BF),
            pltpu.VMEM((nq, 2, rw, COLS), BF),
            blocks, blocks, blocks,
            pltpu.VMEM((8, COLS), F32),
            pltpu.VMEM((8, COLS), F32),
            dma((2,)),
            dma((Gather.count(nz, True),)), dma((Gather.count(nz, True),)),
            dma((Gather.count(nz, False),)), dma((Gather.count(nz, False),)),
            dma((n_ch,)), dma((n_ch,)), dma((n_ch,)), dma((n_ch,)),
            dma((n_ch // 2,)), dma((n_ch // 2,)),
            dma((3,)), dma((3,)),
        ],
        compiler_params=pltpu.CompilerParams(
            collective_id=0, has_side_effects=True, vmem_limit_bytes=60 * 1024 * 1024
        ),
    )(
        section_inputs[0], section_weights[0], memory_weights[0], norm_gains, memory, cotangent,
        lengths[:, None],
    )
    return gin[None], dw[None], gg


def solution(mesh):
    return jax.shard_map(
        local,
        mesh=mesh,
        in_specs=(
            P("section", "dp", None),
            P("section", None, None),
            P("section", "dp", None),
            P("section", None),
            P("dp", None),
            P("dp", None),
            P("dp"),
        ),
        out_specs=(P("section", "dp", None), P("section", "dp", None), P("section", "dp")),
        check_vma=False,
    )
```

```python
import functools

import jax
import jax.numpy as jnp
from jax import lax
from jax.experimental import pallas as pl
from jax.experimental.pallas import tpu as pltpu
from jax.sharding import PartitionSpec as P

epsilon = 1e-06
BF = jnp.bfloat16
F32 = jnp.float32
CH = 16
TILE = 256


class Gather:
    def __init__(self, block, rows, place, send_sems, recv_sems, both_cores):
        self.block, self.rows = block, rows
        self.y, self.z, self.c, self.nz, self.device = place
        self.far = self.nz // 2
        self.ss, self.rs = send_sems, recv_sems
        self.both = both_cores

    @staticmethod
    def count(nz, both):
        ids = 1 + 2 * (nz // 2) * 3 + 1 + 2 * (nz // 2)
        return 2 * ids + 1 if both else ids

    @property
    def ids(self):
        return self.count(self.nz, False)

    def copy(self, q, start, size, ident, dev):
        ref = self.block(q, start, size)
        return pltpu.make_async_remote_copy(
            src_ref=ref, dst_ref=ref, send_sem=self.ss.at[ident], recv_sem=self.rs.at[ident],
            device_id=dev, device_id_type=pl.DeviceIdType.MESH)

    def turn(self, z):
        return lax.rem(z + 2 * self.nz, self.nz)

    def z_id(self, way, d, m):
        return 1 + (way * self.far + d - 1) * 3 + m

    def y_id(self, way, d):
        base = 1 + 2 * self.far * 3
        return base if d == 0 else base + 1 + way * self.far + d - 1

    def span(self, way, d, m):
        half = self.rows // 2
        start, size = (half if m == 1 else 0), half
        if d == self.far:
            size = half // 2
            start = start + way * size
        return start, size

    def z_copy(self, way, d, m, sending):
        sign = 1 - 2 * way
        src = self.turn(self.z - sign * (d - 1 if sending else d))
        y = 1 - self.y if m == 2 else self.y
        start, size = self.span(way, d, m)
        dev = self.device(self.y, self.turn(self.z + sign), self.c)
        return self.copy(y * self.nz + src, start, size, self.z_id(way, d, m), dev)

    def y_copy(self, way, d, sending):
        src = self.turn(self.z - (1 - 2 * way) * d)
        y = self.y if sending else 1 - self.y
        start, size = self.span(way, d, 1)
        dev = self.device(1 - self.y, self.z, self.c)
        return self.copy(y * self.nz + src, start, size, self.y_id(way, d), dev)

    def first_copy(self, sending):
        y = self.y if sending else 1 - self.y
        dev = self.device(1 - self.y, self.z, self.c)
        return self.copy(y * self.nz + self.z, 0, self.rows // 2, 0, dev)

    def pair(self, ident, sending):
        dev = self.device(self.y, self.z, 1 - self.c)
        owner = self.c if sending else 1 - self.c
        other = Gather(functools.partial(self.block, lane=owner), self.rows,
                       (self.y, self.z, self.c, self.nz, self.device), self.ss, self.rs, False)
        kind, args = ident
        if kind == "own":
            return other.copy(self.y * self.nz + self.z, 0, self.rows, 2 * self.ids, dev)
        if kind == "first":
            return other.copy((1 - self.y) * self.nz + self.z, 0, self.rows // 2, self.ids, dev)
        if kind == "z":
            way, d, m = args
            src = self.turn(self.z - (1 - 2 * way) * d)
            y = 1 - self.y if m == 2 else self.y
            start, size = self.span(way, d, m)
            return other.copy(y * self.nz + src, start, size, self.ids + self.z_id(way, d, m), dev)
        way, d = args
        src = self.turn(self.z - (1 - 2 * way) * d)
        start, size = self.span(way, d, 1)
        return other.copy((1 - self.y) * self.nz + src, start, size, self.ids + self.y_id(way, d), dev)

    def hand(self, kind, args=()):
        if self.both:
            self.pair((kind, args), True).start()

    def begin(self):
        self.first_copy(True).start()
        for m in (0, 1):
            for way in (0, 1):
                self.z_copy(way, 1, m, True).start()
        self.y_copy(0, 0, True).start()
        self.hand("own")

    def begin_other(self):
        self.first_copy(False).wait_recv()
        for way in (0, 1):
            self.z_copy(way, 1, 2, True).start()
        self.hand("first")

    def pair_step(self, i):
        d, m = i // 3 + 1, i % 3
        for way in (0, 1):
            self.z_copy(way, d, m, False).wait_recv()
            if d < self.far:
                self.z_copy(way, d + 1, m, True).start()
            if m == 1:
                self.y_copy(way, d, True).start()
            self.hand("z", (way, d, m))

    def ways(self, d):
        return (0,) if d == 0 else (0, 1)

    def collect(self, d):
        for way in self.ways(d):
            self.y_copy(way, d, False).wait_recv()
            self.hand("y", (way, d))
        if self.both:
            if d == 0:
                self.pair(("own", ()), False).wait_recv()
                self.pair(("first", ()), False).wait_recv()
            else:
                for way in (0, 1):
                    for m in (0, 1, 2):
                        self.pair(("z", (way, d, m)), False).wait_recv()
            for way in self.ways(d):
                self.pair(("y", (way, d)), False).wait_recv()

    def sent(self):
        self.first_copy(True).wait_send()
        for d in range(1, self.far + 1):
            for way in (0, 1):
                for m in (0, 1, 2):
                    self.z_copy(way, d, m, True).wait_send()
        for d in range(self.far + 1):
            for way in self.ways(d):
                self.y_copy(way, d, True).wait_send()
        if self.both:
            self.pair(("own", ()), True).wait_send()
            self.pair(("first", ()), True).wait_send()
            for d in range(self.far + 1):
                for way in self.ways(d):
                    self.pair(("y", (way, d)), True).wait_send()
                    if d:
                        for m in (0, 1, 2):
                            self.pair(("z", (way, d, m)), True).wait_send()

    def sources(self, d):
        spots = {0: (0,), self.far: (self.far,)}.get(d, (d, -d))
        return [y * self.nz + self.turn(self.z + o) for o in spots for y in (0, 1)]


class HalfGather:
    def __init__(self, buf, place, send_sems, recv_sems):
        self.buf, self.ss, self.rs = buf, send_sems, recv_sems
        self.y, self.z, self.c, self.nz, self.device = place
        self.far = self.nz // 2
        self.rows = buf.shape[1]

    @staticmethod
    def count(nz):
        return 1 + 2 * (nz // 2) * 2

    def turn(self, z):
        return lax.rem(z + 2 * self.nz, self.nz)

    def cross(self, src):
        return pltpu.make_async_remote_copy(
            src_ref=src, dst_ref=self.buf.at[self.y * self.nz + self.z], send_sem=self.ss.at[0],
            recv_sem=self.rs.at[0], device_id=self.device(1 - self.y, self.z, self.c),
            device_id_type=pl.DeviceIdType.MESH)

    def z_copy(self, way, d, m, sending):
        sign = 1 - 2 * way
        src = self.turn(self.z - sign * (d - 1 if sending else d))
        y = 1 - self.y if m else self.y
        size = self.rows // 2 if d == self.far else self.rows
        ref = self.buf.at[y * self.nz + src, pl.ds(way * size if d == self.far else 0, size)]
        ident = 1 + (way * self.far + d - 1) * 2 + m
        return pltpu.make_async_remote_copy(
            src_ref=ref, dst_ref=ref, send_sem=self.ss.at[ident], recv_sem=self.rs.at[ident],
            device_id=self.device(self.y, self.turn(self.z + sign), self.c), device_id_type=pl.DeviceIdType.MESH)

    def begin(self, src):
        self.cross(src).start()
        for way in (0, 1):
            self.z_copy(way, 1, 0, True).start()

    def begin_other(self, src):
        self.cross(src).wait_recv()
        for way in (0, 1):
            self.z_copy(way, 1, 1, True).start()

    def pair_step(self, i):
        d, m = i // 2 + 1, i % 2
        for way in (0, 1):
            self.z_copy(way, d, m, False).wait_recv()
            if d < self.far:
                self.z_copy(way, d + 1, m, True).start()

    def sent(self, src):
        self.cross(src).wait_send()
        for d in range(1, self.far + 1):
            for way in (0, 1):
                for m in (0, 1):
                    self.z_copy(way, d, m, True).wait_send()


def relay_kernel(n_sec, n_dp,
                 x_hbm, w_hbm, mw_hbm, gain_ref, mem_hbm, cot_hbm, len_ref,
                 gin_hbm, dw_ref, gg_ref,
                 x_ref, mem_ref, cot_ref, gin_ref,
                 wv, wt, mwv, mwt, sc, sg, normed, slope, act, gate, dwt, inv, gbuf, tbuf, tsend,
                 gpv, gacc, gs, gpg, gpt, dws, dwp, dwo, og, gnv, gng, gnl, gnp,
                 load_sem, wag_s, wag_r, sag_s, sag_r, g_s, g_r, t_s, t_r, late_s, late_r, pass_s, pass_r, swap_s, swap_r,
                 tail_s, tail_r):
    s = lax.axis_index("section")
    j = lax.axis_index("dp")
    half = n_sec // 2
    nq = n_dp // 2
    nz = nq // 2
    c = lax.rem(j, 2)
    q0 = j // 2
    y, z = q0 // nz, lax.rem(q0, nz)
    toks, feats = x_ref.shape
    rw = mw_hbm.shape[0]
    n_ch = toks // CH
    tiles = feats // TILE
    decoder = s >= half
    encoder = s < half
    above = n_sec - 1 - s
    MESH = pl.DeviceIdType.MESH

    def device(yy, zz, cc):
        return {"dp": (yy * nz + zz) * 2 + cc}

    def load(src, dst, i):
        copy = pltpu.make_async_copy(src, dst, load_sem.at[i])
        copy.start()
        return copy

    barrier = pltpu.get_barrier_semaphore()

    def greet(i, carry):
        q = lax.rem(q0 + i, nq)
        pl.semaphore_signal(barrier, inc=1, device_id={"dp": q * 2 + c}, device_id_type=MESH)
        return carry

    lax.fori_loop(1, nq, greet, 0)
    pl.semaphore_signal(barrier, inc=1, device_id={"dp": q0 * 2 + 1 - c}, device_id_type=MESH)

    @pl.when(s > 0)
    def _():
        pl.semaphore_signal(barrier, inc=1, device_id={"section": s - 1}, device_id_type=MESH)

    @pl.when(s < n_sec - 1)
    def _():
        pl.semaphore_signal(barrier, inc=1, device_id={"section": s + 1}, device_id_type=MESH)

    load_m = load(mw_hbm, mwv.at[pl.ds(pl.multiple_of(j * rw, rw), rw)], 1)
    load_x = load(x_hbm, x_ref, 2)
    load_w = load(w_hbm, wv, 0)
    load_mem = load(mem_hbm, mem_ref, 3)
    load_cot = load(cot_hbm, cot_ref, 4)

    ends = (s == 0) | (s == n_sec - 1)
    pl.semaphore_wait(barrier, nq + jnp.where(ends, 1, 2))

    place = (y, z, c, nz, device)

    def w_block(q, start, size, lane=None):
        lane = c if lane is None else lane
        return mwv.at[pl.ds(pl.multiple_of((q * 2 + lane) * rw + start, 16), size)]

    wag = Gather(w_block, rw, place, wag_s, wag_r, True)
    sag = HalfGather(sg, place, sag_s, sag_r)
    far = wag.far
    last_pair = 2 * far
    width = feats // 2
    cols_z = feats // nz
    mine, theirs = (pl.ds(pl.multiple_of(v * width, width), width) for v in (y, 1 - y))
    crossing = sc.at[:, theirs]

    load_m.wait()

    @pl.when(decoder)
    def _():
        wag.begin()

    def rows_of(k):
        return pl.ds(pl.multiple_of(k * CH, CH), CH)

    def norm_rows(k, carry):
        rows = rows_of(k)
        wide = x_ref[rows, :].astype(F32)
        scale = lax.rsqrt(jnp.mean(wide * wide, axis=1, keepdims=True) + epsilon)
        inv[rows, :] = jnp.broadcast_to(scale, (CH, 128))
        value = wide * scale
        normed[rows, :] = value
        sc[rows, :] = (value * gain_ref[...]).astype(BF)
        sg[q0, rows, :] = sc[rows, mine]
        return carry

    load_x.wait()
    lax.fori_loop(0, n_ch, norm_rows, 0)

    @pl.when(encoder)
    def _():
        sag.begin(crossing)

    load_w.wait()

    def cols_of(t):
        return pl.ds(pl.multiple_of(t * TILE, TILE), TILE)

    def preact_tile(t, carry):
        cols = cols_of(t)
        p = jnp.dot(sc[...], wv[:, cols], preferred_element_type=F32)
        sig = jax.nn.sigmoid(p)
        act[:, cols] = p * sig
        slope[:, cols] = sig * (1.0 + p * (1.0 - sig))
        return carry

    lax.fori_loop(0, tiles, preact_tile, 0)
    load_mem.wait()
    load_cot.wait()

    def turn_w(piece, pieces):
        def body(i, carry):
            a, b = i // tiles, lax.rem(i, tiles)
            wt[cols_of(b), cols_of(a)] = wv[cols_of(a), cols_of(b)].T
            return carry

        size = tiles * tiles // pieces
        lax.fori_loop(piece * size, (piece + 1) * size, body, 0, unroll=4)

    def chip_rows(q):
        return pl.ds(pl.multiple_of(q * 2 * rw, 2 * rw), 2 * rw)

    def turn_m(d):
        spots = [chip_rows(q) for q in wag.sources(d)]

        def body(t, carry):
            for at in spots:
                mwt[cols_of(t), at] = mwv[at, cols_of(t)].T
            return carry

        lax.fori_loop(0, tiles, body, 0, unroll=2)

    def gate_part(d):
        spots = [chip_rows(q) for q in wag.sources(d)]
        left = jnp.concatenate([mem_ref[:, at] for at in spots], axis=1)

        def body(t, carry):
            cols = cols_of(t)
            right = jnp.concatenate([mwv[at, cols] for at in spots], axis=0)
            p = jnp.dot(left, right, preferred_element_type=F32)
            if d == 0:
                gate[:, cols] = p
            elif d < far:
                gate[:, cols] += p
            else:
                slope[:, cols] = slope[:, cols] * (gate[:, cols] + p)
            return carry

        lax.fori_loop(0, tiles, body, 0, unroll=4)

    @pl.when(decoder)
    def _():
        wag.begin_other()
        wag.pair_step(0)
        turn_w(0, 4)
        wag.pair_step(1)
        turn_w(1, 4)
        wag.pair_step(2)
        wag.collect(0)
        gate_part(0)
        wag.pair_step(3)
        turn_m(0)
        wag.pair_step(4)
        turn_w(2, 4)
        wag.pair_step(5)
        wag.collect(1)
        gate_part(1)
        wag.pair_step(6)
        turn_m(1)
        wag.pair_step(7)
        turn_w(3, 4)
        wag.pair_step(8)
        wag.collect(2)
        gate_part(2)
        wag.pair_step(9)
        turn_m(2)
        wag.pair_step(10)
        wag.pair_step(11)
        wag.collect(3)
        gate_part(3)
        turn_m(3)
        wag.collect(4)
        gate_part(4)
        sag.begin(crossing)
        turn_m(4)

        @pl.when(above >= 1)
        def _():
            sag.begin_other(crossing)

        @pl.when(above >= 2)
        def _():
            sag.pair_step(0)

        @pl.when(above >= 3)
        def _():
            sag.pair_step(1)

    @pl.when(encoder)
    def _():
        turn_w(0, 4)
        sag.begin_other(crossing)
        turn_w(1, 4)
        sag.pair_step(0)
        turn_w(2, 4)
        sag.pair_step(1)
        turn_w(3, 4)
        for i in range(2, last_pair):
            sag.pair_step(i)

    @pl.when(s == n_sec - 1)
    def _():
        live = lax.broadcasted_iota(jnp.int32, (toks, TILE), 0) < len_ref[0]

        def body(t, carry):
            cols = cols_of(t)
            gbuf[:, cols] = jnp.where(live, cot_ref[:, cols], jnp.zeros((), BF))
            return carry

        lax.fori_loop(0, tiles, body, 0)

    gacc[...] = jnp.zeros_like(gacc)

    def down(src, dst, k, send_sems, recv_sems):
        rows = rows_of(k)
        return pltpu.make_async_remote_copy(
            src_ref=src.at[rows], dst_ref=dst.at[rows], send_sem=send_sems.at[k], recv_sem=recv_sems.at[k],
            device_id={"section": s - 1}, device_id_type=MESH)

    groups = [(i * 2 * CH, 2 * CH) for i in range(n_ch // 2 - 1)] + [(toks - 2 * CH, CH), (toks - CH, CH)]

    def late_send(g):
        start, size = groups[g]
        rows = pl.ds(start, size)

        def send(yy, zz):
            pltpu.make_async_remote_copy(
                src_ref=gpv.at[rows, pl.ds(pl.multiple_of(zz * cols_z, cols_z), cols_z)], dst_ref=gpg.at[q0, rows],
                send_sem=late_s.at[g], recv_sem=late_r.at[g], device_id=device(yy, zz, c), device_id_type=MESH).start()

        def body(i, carry):
            zz = lax.rem(z + i, nz)
            send(y, zz)

            @pl.when(encoder)
            def _():
                send(1 - y, zz)

            return carry

        lax.fori_loop(1, nz, body, 0)

        @pl.when(encoder)
        def _():
            send(1 - y, z)

    def late_done(g, count):
        start, size = groups[g]
        ref = gpg.at[pl.ds(0, count), pl.ds(start, size)]
        return pltpu.make_async_remote_copy(
            src_ref=ref, dst_ref=ref, send_sem=late_s.at[g], recv_sem=late_r.at[g],
            device_id={"dp": q0 * 2 + 1 - c}, device_id_type=MESH)

    def late_recv(g):
        @pl.when(encoder)
        def _():
            late_done(g, nq - 1).wait_recv()

        @pl.when(decoder)
        def _():
            late_done(g, nz - 1).wait_recv()

    def late_pass(g):
        start, size = groups[g]
        ref = gpg.at[pl.ds(pl.multiple_of(y * nz, nz), nz), pl.ds(start, size)]
        return pltpu.make_async_remote_copy(
            src_ref=ref, dst_ref=ref, send_sem=pass_s.at[g], recv_sem=pass_r.at[g],
            device_id=device(1 - y, z, c), device_id_type=MESH)

    def term(k):
        rows = rows_of(k)
        up = gbuf[rows, :].astype(F32)
        grad_gate = (up * act[rows, :]).astype(BF)

        @pl.when(s < n_sec - 1)
        def _():
            down(tsend, tbuf, k, t_s, t_r).wait_recv()

        first = jnp.where(s < n_sec - 1, 1.0, 0.0)
        for t in range(tiles):
            cols = slice(t * TILE, (t + 1) * TILE)
            p = jnp.dot(grad_gate, mwt[:, cols], preferred_element_type=F32)
            tsend[rows, cols] = (p + jnp.where(first > 0, tbuf[rows, cols].astype(F32), 0.0)).astype(BF)

    def chunk(k, carry):
        rows = rows_of(k)

        @pl.when(s < n_sec - 1)
        def _():
            down(gin_ref, gbuf, k, g_s, g_r).wait_recv()

        @pl.when(s == half)
        def _():
            term(k)
            down(tsend, gbuf, k, t_s, g_r).start()

        gpv[rows, :] = (gbuf[rows, :].astype(F32) * slope[rows, :]).astype(BF)
        grad_pre = gpv[rows, :]
        total = jnp.zeros((CH, 128), F32)
        for t in range(tiles):
            cols = slice(t * TILE, (t + 1) * TILE)
            p = jnp.dot(grad_pre, wt[:, cols], preferred_element_type=F32)
            both = p * normed[rows, cols]
            gacc[:, cols] += both
            h = p * gain_ref[:, cols]
            gs[:, cols] = h
            weighted = both * gain_ref[:, cols]
            for i in range(TILE // 128):
                total = total + weighted[:, i * 128:(i + 1) * 128]
        center = jnp.sum(total, axis=1, keepdims=True) * (1.0 / feats)
        scale = inv[rows, 0:1]
        for t in range(tiles):
            cols = slice(t * TILE, (t + 1) * TILE)
            gin_ref[rows, cols] = (
                gbuf[rows, cols].astype(F32) + scale * (gs[:, cols] - normed[rows, cols] * center)
            ).astype(BF)

        @pl.when((s > 0) & (s != half))
        def _():
            down(gin_ref, gbuf, k, g_s, g_r).start()

        @pl.when(s > half)
        def _():
            term(k)
            down(tsend, tbuf, k, t_s, t_r).start()

        for g, (start, size) in enumerate(groups[:-1]):
            @pl.when(k == (start + size) // CH - 1)
            def _(g=g):
                late_send(g)

        @pl.when((s == n_sec - 1) & (k == 1))
        def _():
            sag.begin_other(crossing)

        for i in range(0, 6):
            @pl.when(decoder & (lax.rem(k, 2) == 1) & ((k + 1) // 2 + above == i + 2))
            def _(i=i):
                sag.pair_step(i)

        return carry

    lax.fori_loop(0, n_ch, chunk, 0)

    late_send(len(groups) - 1)
    part = gacc[...]
    for q in range(nq):
        gnv[q] = part[0:8, q * 128:(q + 1) * 128] + part[8:16, q * 128:(q + 1) * 128]

    def gain_send(i, carry):
        q = lax.rem(q0 + i, nq)
        pltpu.make_async_remote_copy(
            src_ref=gnv.at[q], dst_ref=gng.at[q0], send_sem=tail_s.at[2], recv_sem=tail_r.at[2],
            device_id={"dp": q * 2 + c}, device_id_type=MESH).start()
        return carry

    lax.fori_loop(1, nq, gain_send, 0)
    gng[q0] = gnv[q0]
    store_gin = load(gin_ref, gin_hbm, 5)
    mine_z = pl.ds(pl.multiple_of(z * cols_z, cols_z), cols_z)

    def own(g, carry):
        gpg[q0, rows_of(g), :] = gpv[rows_of(g), mine_z]
        return carry

    lax.fori_loop(0, n_ch, own, 0)

    @pl.when(decoder)
    def _():
        for g in range(len(groups)):
            late_recv(g)
            late_pass(g).start()
        for i in range(3, last_pair):
            @pl.when(i >= 3 + above)
            def _(i=i):
                sag.pair_step(i)
        for g in range(len(groups)):
            late_pass(g).wait_recv()

    @pl.when(encoder)
    def _():
        for g in range(len(groups) - 1):
            late_recv(g)

    most = toks - CH
    kk = nq * most
    parts = width // TILE
    gpt[:, 0:kk] = gpg[:, 0:most, :].reshape(kk, cols_z).T

    def product(t, carry):
        cols = cols_of(t)
        dwt[:, cols] = jnp.dot(gpt[:, 0:kk], sg[:, 0:most, cols].reshape(kk, TILE), preferred_element_type=F32)
        return carry

    lax.fori_loop(0, parts, product, 0, unroll=2)

    @pl.when(encoder)
    def _():
        late_recv(len(groups) - 1)

    gpt[:, kk:nq * toks] = gpg[:, most:toks, :].reshape(nq * CH, cols_z).T

    other = {"dp": q0 * 2 + 1 - c}
    per = TILE // (2 * rw)
    first_part = z // per

    def swap(t):
        spots = pl.ds(t * per, per)
        return pltpu.make_async_remote_copy(
            src_ref=dws.at[spots, 1 - c], dst_ref=dwp.at[spots], send_sem=swap_s.at[t], recv_sem=swap_r.at[t],
            device_id=other, device_id_type=MESH)

    def finish(i, carry):
        t = lax.rem(first_part + i, parts)
        cols = cols_of(t)
        p = dwt[:, cols] + jnp.dot(
            gpt[:, kk:nq * toks], sg[:, most:toks, cols].reshape(nq * CH, TILE), preferred_element_type=F32)
        dws[pl.ds(t * per, per)] = p.T.astype(BF).reshape(per, 2, rw, cols_z)
        swap(t).start()
        return carry

    lax.fori_loop(0, parts, finish, 0, unroll=2)

    def deliver(i, carry):
        t = lax.rem(first_part + i, parts)
        swap(t).wait_recv()
        for e in range(per):
            zz = t * per + e
            dwo[zz] = (dws[zz, c].astype(F32) + dwp[zz].astype(F32)).astype(BF)

            @pl.when(zz != z)
            def _(zz=zz):
                pltpu.make_async_remote_copy(
                    src_ref=dwo.at[zz], dst_ref=og.at[z], send_sem=tail_s.at[1], recv_sem=tail_r.at[1],
                    device_id=device(y, zz, c), device_id_type=MESH).start()

        return carry

    lax.fori_loop(0, parts, deliver, 0)
    og[z] = dwo[z]

    gain_all = pltpu.make_async_remote_copy(
        src_ref=gng.at[pl.ds(0, nq - 1)], dst_ref=gng.at[pl.ds(0, nq - 1)], send_sem=tail_s.at[2],
        recv_sem=tail_r.at[2], device_id=other, device_id_type=MESH)
    gain_all.wait()
    gnl[...] = jnp.sum(gng[...], axis=0)
    gain_copy = pltpu.make_async_remote_copy(
        src_ref=gnl, dst_ref=gnp, send_sem=tail_s.at[0], recv_sem=tail_r.at[0], device_id=other, device_id_type=MESH)
    gain_copy.start()

    for g in range(len(groups)):
        @pl.when(encoder)
        def _(g=g):
            late_done(g, nq - 1).wait_send()

        @pl.when(decoder)
        def _(g=g):
            late_done(g, nz - 1).wait_send()
            late_pass(g).wait_send()
    for k in range(n_ch):
        @pl.when((s > 0) & (s != half))
        def _(k=k):
            down(gin_ref, gbuf, k, g_s, g_r).wait_send()

        @pl.when(decoder)
        def _(k=k):
            down(tsend, tbuf, k, t_s, t_r).wait_send()

    sag.sent(crossing)

    @pl.when(decoder)
    def _():
        wag.sent()

    for t in range(parts):
        swap(t).wait_send()
    store_gin.wait()
    gain_copy.wait()
    gains = jnp.sum(gnl[...] + gnp[...], axis=0, keepdims=True) * (1.0 / n_dp)
    gg_ref[...] = jnp.where(c == 0, gains[:, 0:rw], gains[:, rw:2 * rw])

    whole = pltpu.make_async_remote_copy(
        src_ref=dwo.at[pl.ds(0, nz - 1)], dst_ref=og.at[pl.ds(0, nz - 1)], send_sem=tail_s.at[1],
        recv_sem=tail_r.at[1], device_id=other, device_id_type=MESH)
    whole.wait_recv()
    for zz in range(nz):
        dw_ref[:, zz * cols_z:(zz + 1) * cols_z] = og[zz].astype(F32) * (1.0 / n_dp)
    whole.wait_send()


def publish_kernel(a, b, c, a_out, b_out, c_out):
    a_out[...] = a[...]
    b_out[...] = b[...]
    c_out[...] = c[...]


def local(section_inputs, section_weights, memory_weights, norm_gains, memory, cotangent, lengths):
    n_sec, n_dp = lax.axis_size("section"), lax.axis_size("dp")
    toks, feats = section_inputs.shape[1:]
    rw = memory_weights.shape[1]
    nq = n_dp // 2
    nz = nq // 2
    n_ch = toks // CH
    vmem = pl.BlockSpec(memory_space=pltpu.VMEM)
    hbm = pl.BlockSpec(memory_space=pl.ANY)
    square = pltpu.VMEM((feats, feats), BF)
    wide = pltpu.VMEM((toks, feats), F32)
    narrow = pltpu.VMEM((toks, feats), BF)
    cols_z = feats // nz
    blocks = pltpu.VMEM((nz, rw, cols_z), BF)
    dma = pltpu.SemaphoreType.DMA
    gin, dw, gg = pl.pallas_call(
        functools.partial(relay_kernel, n_sec, n_dp),
        out_shape=(
            jax.ShapeDtypeStruct((toks, feats), BF),
            jax.ShapeDtypeStruct((rw, feats), F32),
            jax.ShapeDtypeStruct((1, rw), F32),
        ),
        in_specs=[hbm, hbm, hbm, vmem, hbm, hbm, pl.BlockSpec(memory_space=pltpu.SMEM)],
        out_specs=(hbm, vmem, vmem),
        scratch_shapes=[
            narrow, narrow, narrow, narrow,
            square, square, square, square, narrow,
            pltpu.VMEM((nq, toks, feats // 2), BF),
            wide, wide, wide, wide,
            pltpu.VMEM((cols_z, feats // 2), F32),
            pltpu.VMEM((toks, 128), F32),
            narrow, narrow, narrow,
            narrow,
            pltpu.VMEM((CH, feats), F32),
            pltpu.VMEM((CH, feats), F32),
            pltpu.VMEM((nq, toks, cols_z), BF),
            pltpu.VMEM((cols_z, nq * toks), BF),
            pltpu.VMEM((nz, 2, rw, cols_z), BF),
            blocks, blocks, blocks,
            pltpu.VMEM((nq, 8, 128), F32),
            pltpu.VMEM((nq, 8, 128), F32),
            pltpu.VMEM((8, 128), F32),
            pltpu.VMEM((8, 128), F32),
            dma((6,)),
            dma((Gather.count(nz, True),)), dma((Gather.count(nz, True),)),
            dma((HalfGather.count(nz),)), dma((HalfGather.count(nz),)),
            dma((n_ch,)), dma((n_ch,)), dma((n_ch,)), dma((n_ch,)),
            dma((n_ch // 2 + 1,)), dma((n_ch // 2 + 1,)),
            dma((n_ch // 2 + 1,)), dma((n_ch // 2 + 1,)),
            dma((feats // 2 // TILE,)), dma((feats // 2 // TILE,)),
            dma((3,)), dma((3,)),
        ],
        compiler_params=pltpu.CompilerParams(
            collective_id=0, has_side_effects=True, vmem_limit_bytes=60 * 1024 * 1024
        ),
    )(
        section_inputs[0], section_weights[0], memory_weights[0], norm_gains, memory, cotangent,
        lengths,
    )
    gin, dw, gg = pl.pallas_call(
        publish_kernel,
        out_shape=tuple(jax.ShapeDtypeStruct(v.shape, v.dtype) for v in (gin, dw, gg)),
        in_specs=[vmem] * 3,
        out_specs=(vmem,) * 3,
    )(gin, dw, gg)
    return gin[None], dw[None], gg


def solution(mesh):
    return jax.shard_map(
        local,
        mesh=mesh,
        in_specs=(
            P("section", "dp", None),
            P("section", None, None),
            P("section", "dp", None),
            P("section", None),
            P("dp", None),
            P("dp", None),
            P("dp"),
        ),
        out_specs=(P("section", "dp", None), P("section", "dp", None), P("section", "dp")),
        check_vma=False,
    )
```

```python
import functools

import jax
import jax.numpy as jnp
from jax import lax
from jax.experimental import pallas as pl
from jax.experimental.pallas import tpu as pltpu
from jax.sharding import PartitionSpec as P

epsilon = 1e-06
BF = jnp.bfloat16
F32 = jnp.float32
CH = 16
TILE = 256


class Gather:
    def __init__(self, block, rows, place, send_sems, recv_sems, lane=None):
        self.block, self.rows, self.lane = block, rows, lane
        self.place = place
        self.y, self.z, self.c, self.nz, self.device = place
        self.far = self.nz // 2
        self.ss, self.rs = send_sems, recv_sems

    @staticmethod
    def count(nz):
        far = nz // 2
        return 2 * (2 + 10 * far) + 1 + 2 * far

    @property
    def ids(self):
        return 2 + 10 * self.far

    def copy(self, q, start, size, ident, dev):
        ref = self.block(q, start, size, self.lane)
        return pltpu.make_async_remote_copy(
            src_ref=ref, dst_ref=ref, send_sem=self.ss.at[ident], recv_sem=self.rs.at[ident],
            device_id=dev, device_id_type=pl.DeviceIdType.MESH)

    def turn(self, z):
        return lax.rem(z + 2 * self.nz, self.nz)

    def source(self, way, d):
        return self.turn(self.z - (1 - 2 * way) * d)

    def number(self, way, d):
        return way * self.far + d - 1

    def ways(self, d, m=0):
        return (0,) if d == 0 or (d == self.far and m in (1, 3)) else (0, 1)

    def span(self, way, d, m):
        half, quarter = self.rows // 2, self.rows // 4
        if m in (1, 3):
            return (half if m == 1 else half + quarter), quarter
        return (way * quarter, quarter) if d == self.far else (0, half)

    def z_copy(self, way, d, m, sending):
        sign = 1 - 2 * way
        src = self.source(way, d - 1 if sending else d)
        y = 1 - self.y if m == 2 else self.y
        start, size = self.span(way, d, m)
        dev = self.device(self.y, self.turn(self.z + sign), self.c)
        return self.copy(y * self.nz + src, start, size, 1 + 3 * self.number(way, d) + m, dev)

    def y_copy(self, way, d, m, sending):
        y = self.y if sending else 1 - self.y
        base = 1 + 6 * self.far
        start, size = self.span(way, d, m)
        if d == 0:
            start, size, ident = self.rows // 2, self.rows // 2, base
        else:
            ident = base + 1 + (2 * self.far if m == 3 else 0) + self.number(way, d)
        dev = self.device(1 - self.y, self.z, self.c)
        return self.copy(y * self.nz + self.source(way, d), start, size, ident, dev)

    def first_copy(self, sending):
        y = self.y if sending else 1 - self.y
        dev = self.device(1 - self.y, self.z, self.c)
        return self.copy(y * self.nz + self.z, 0, self.rows // 2, 0, dev)

    def pair(self, kind, args, sending):
        dev = self.device(self.y, self.z, 1 - self.c)
        other = Gather(self.block, self.rows, self.place, self.ss, self.rs, self.c if sending else 1 - self.c)
        ids = self.ids
        if kind == "own":
            return other.copy(self.y * self.nz + self.z, 0, self.rows, 2 * ids, dev)
        if kind == "first":
            return other.copy((1 - self.y) * self.nz + self.z, 0, self.rows // 2, ids, dev)
        way, d, m = args
        src = self.source(way, d)
        start, size = self.span(way, d, m)
        if kind == "z":
            y = 1 - self.y if m == 2 else self.y
            return other.copy(y * self.nz + src, start, size, ids + 1 + 3 * self.number(way, d) + m, dev)
        if kind == "back":
            return other.copy(self.y * self.nz + src, start, size, 2 * ids + 1 + self.number(way, d), dev)
        base = ids + 1 + 6 * self.far
        if d == 0:
            start, size, ident = self.rows // 2, self.rows // 2, base
        else:
            ident = base + 1 + (2 * self.far if m == 3 else 0) + self.number(way, d)
        return other.copy((1 - self.y) * self.nz + src, start, size, ident, dev)

    def begin(self):
        self.first_copy(True).start()
        for m in (1, 0):
            for way in (0, 1):
                self.z_copy(way, 1, m, True).start()
        self.y_copy(0, 0, 1, True).start()
        self.pair("own", (), True).start()

    def begin_other(self):
        self.first_copy(False).wait_recv()
        for way in (0, 1):
            self.z_copy(way, 1, 2, True).start()
        self.pair("first", (), True).start()

    def pair_step(self, i):
        d, m = i // 3 + 1, (1, 0, 2)[i % 3]
        for way in self.ways(d, m):
            self.z_copy(way, d, m, False).wait_recv()
            if way in self.ways(d + 1, m) and d < self.far:
                self.z_copy(way, d + 1, m, True).start()
            if m == 1:
                self.y_copy(way, d, 1, True).start()
            self.pair("z", (way, d, m), True).start()

    def back_step(self, d, back):
        for way in self.ways(d, 3):
            back(way, d).wait_recv()
            self.y_copy(way, d, 3, True).start()
            self.pair("back", (way, d, 3), True).start()

    def crossed(self, d):
        return [(0, 0, 1)] if d == 0 else [(way, d, m) for m in (1, 3) for way in self.ways(d, m)]

    def handed(self, d):
        if d == 0:
            return [("own", ()), ("first", ()), ("y", (0, 0, 1))]
        came = [("z", (way, d, m)) for m in (0, 1, 2) for way in self.ways(d, m)]
        came += [("back", (way, d, 3)) for way in self.ways(d, 3)]
        return came + [("y", args) for args in self.crossed(d)]

    def collect(self, d):
        for args in self.crossed(d):
            self.y_copy(*args, False).wait_recv()
            self.pair("y", args, True).start()
        for kind, args in self.handed(d):
            self.pair(kind, args, False).wait_recv()

    def sent(self):
        self.first_copy(True).wait_send()
        for d in range(self.far + 1):
            for args in self.crossed(d):
                self.y_copy(*args, True).wait_send()
            for kind, args in self.handed(d):
                self.pair(kind, args, True).wait_send()
                if kind == "z":
                    self.z_copy(*args, True).wait_send()

    def sources(self, d):
        spots = {0: (0,), self.far: (self.far,)}.get(d, (d, -d))
        return [y * self.nz + self.turn(self.z + o) for o in spots for y in (0, 1)]


class Relay:
    def __init__(self, gather, section, half, sems):
        self.g, self.ss, self.rs = gather, *sems
        decoder = section >= half
        g = gather
        self.partner = {
            "section": jnp.where(decoder, section - half, section + half),
            "dp": ((1 - g.y) * g.nz + g.z) * 2 + g.c,
        }

    def copy(self, y, src, ident, dev):
        g = self.g
        start, size = g.span(0, 1, 3)
        ref = g.block(y * g.nz + src, start, size, None)
        return pltpu.make_async_remote_copy(
            src_ref=ref, dst_ref=ref, send_sem=self.ss.at[ident], recv_sem=self.rs.at[ident],
            device_id=dev, device_id_type=pl.DeviceIdType.MESH)

    @staticmethod
    def count(nz):
        return 1 + 4 * (nz // 2)

    def up(self, sending):
        y = self.g.y if sending else 1 - self.g.y
        return self.copy(y, self.g.z, 0, self.partner)

    def ring(self, way, d, sending):
        g = self.g
        src = g.source(way, d - 1 if sending else d)
        dev = g.device(g.y, g.turn(g.z + 1 - 2 * way), g.c)
        return self.copy(1 - g.y, src, 1 + g.number(way, d), dev)

    def back(self, way, d, sending=False):
        g = self.g
        y = 1 - g.y if sending else g.y
        return self.copy(y, g.source(way, d), 1 + 2 * g.far + g.number(way, d), self.partner)

    def begin(self):
        self.up(False).wait_recv()
        for way in (0, 1):
            self.ring(way, 1, True).start()

    def step(self, d):
        g = self.g
        for way in g.ways(d, 3):
            self.ring(way, d, False).wait_recv()
            if d < g.far and way in g.ways(d + 1, 3):
                self.ring(way, d + 1, True).start()
            self.back(way, d, True).start()

    def sent(self):
        for d in range(1, self.g.far + 1):
            for way in self.g.ways(d, 3):
                self.ring(way, d, True).wait_send()
                self.back(way, d, True).wait_send()


class HalfGather:
    def __init__(self, buf, place, send_sems, recv_sems):
        self.buf, self.ss, self.rs = buf, send_sems, recv_sems
        self.y, self.z, self.c, self.nz, self.device = place
        self.far = self.nz // 2
        self.rows = buf.shape[1]

    @staticmethod
    def count(nz):
        return 1 + 2 * (nz // 2) * 2

    def turn(self, z):
        return lax.rem(z + 2 * self.nz, self.nz)

    def cross(self, src):
        return pltpu.make_async_remote_copy(
            src_ref=src, dst_ref=self.buf.at[self.y * self.nz + self.z], send_sem=self.ss.at[0],
            recv_sem=self.rs.at[0], device_id=self.device(1 - self.y, self.z, self.c),
            device_id_type=pl.DeviceIdType.MESH)

    def z_copy(self, way, d, m, sending):
        sign = 1 - 2 * way
        src = self.turn(self.z - sign * (d - 1 if sending else d))
        y = 1 - self.y if m else self.y
        size = self.rows // 2 if d == self.far else self.rows
        ref = self.buf.at[y * self.nz + src, pl.ds(way * size if d == self.far else 0, size)]
        ident = 1 + (way * self.far + d - 1) * 2 + m
        return pltpu.make_async_remote_copy(
            src_ref=ref, dst_ref=ref, send_sem=self.ss.at[ident], recv_sem=self.rs.at[ident],
            device_id=self.device(self.y, self.turn(self.z + sign), self.c), device_id_type=pl.DeviceIdType.MESH)

    def begin(self):
        for way in (0, 1):
            self.z_copy(way, 1, 0, True).start()

    def begin_other(self, src):
        self.cross(src).wait_recv()
        for way in (0, 1):
            self.z_copy(way, 1, 1, True).start()

    def pair_step(self, i):
        d, m = i // 2 + 1, i % 2
        for way in (0, 1):
            self.z_copy(way, d, m, False).wait_recv()
            if d < self.far:
                self.z_copy(way, d + 1, m, True).start()

    def sent(self, src):
        self.cross(src).wait_send()
        for d in range(1, self.far + 1):
            for way in (0, 1):
                for m in (0, 1):
                    self.z_copy(way, d, m, True).wait_send()


def relay_kernel(n_sec, n_dp,
                 x_hbm, w_hbm, mw_hbm, gain_ref, mem_hbm, cot_hbm, len_ref,
                 gin_hbm, og, gg_ref,
                 x_ref, mem_ref, cot_ref, gin_ref,
                 wv, wt, mwv, mwt, sc, sg, normed, slope, act, gate, dwt, inv, gbuf, tbuf, tsend,
                 gpv, gacc, gs, ts, gpg, gpt, dws, dwp, dwo, gnv, gng, gnl, gnp,
                 load_sem, wag_s, wag_r, rel_s, rel_r, sag_s, sag_r, g_s, g_r, t_s, t_r, late_s, late_r, pass_s, pass_r, swap_s, swap_r,
                 tail_s, tail_r):
    s = lax.axis_index("section")
    j = lax.axis_index("dp")
    half = n_sec // 2
    nq = n_dp // 2
    nz = nq // 2
    c = lax.rem(j, 2)
    q0 = j // 2
    y, z = q0 // nz, lax.rem(q0, nz)
    toks, feats = x_ref.shape
    rw = mw_hbm.shape[0]
    n_ch = toks // CH
    tiles = feats // TILE
    decoder = s >= half
    encoder = s < half
    above = n_sec - 1 - s
    MESH = pl.DeviceIdType.MESH

    def device(yy, zz, cc):
        return {"dp": (yy * nz + zz) * 2 + cc}

    def load(src, dst, i):
        copy = pltpu.make_async_copy(src, dst, load_sem.at[i])
        copy.start()
        return copy

    barrier = pltpu.get_barrier_semaphore()

    def greet(i, carry):
        q = lax.rem(q0 + i, nq)
        pl.semaphore_signal(barrier, inc=1, device_id={"dp": q * 2 + c}, device_id_type=MESH)
        return carry

    lax.fori_loop(1, nq, greet, 0)
    pl.semaphore_signal(barrier, inc=1, device_id={"dp": q0 * 2 + 1 - c}, device_id_type=MESH)

    @pl.when(s > 0)
    def _():
        pl.semaphore_signal(barrier, inc=1, device_id={"section": s - 1}, device_id_type=MESH)

    @pl.when(s < n_sec - 1)
    def _():
        pl.semaphore_signal(barrier, inc=1, device_id={"section": s + 1}, device_id_type=MESH)

    load_m = load(mw_hbm, mwv.at[pl.ds(pl.multiple_of(j * rw, rw), rw)], 1)
    load_x = load(x_hbm, x_ref, 2)
    load_w = load(w_hbm, wv, 0)
    load_mem = load(mem_hbm, mem_ref, 3)
    load_cot = load(cot_hbm, cot_ref, 4)

    pl.semaphore_signal(
        barrier, inc=1, device_id={"section": lax.rem(s + half, n_sec), "dp": ((1 - y) * nz + z) * 2 + c},
        device_id_type=MESH)
    ends = (s == 0) | (s == n_sec - 1)
    pl.semaphore_wait(barrier, nq + jnp.where(ends, 2, 3))

    place = (y, z, c, nz, device)

    def w_block(q, start, size, lane=None):
        lane = c if lane is None else lane
        return mwv.at[pl.ds(pl.multiple_of((q * 2 + lane) * rw + start, 16), size)]

    wag = Gather(w_block, rw, place, wag_s, wag_r)
    relay = Relay(wag, s, half, (rel_s, rel_r))
    sag = HalfGather(sg, place, sag_s, sag_r)
    far = wag.far
    last_pair = 2 * far
    width = feats // 2
    cols_z = feats // nz
    mine, theirs = (pl.ds(pl.multiple_of(v * width, width), width) for v in (y, 1 - y))
    crossing = sc.at[:, theirs]
    mine_z = pl.ds(pl.multiple_of(z * cols_z, cols_z), cols_z)

    load_m.wait()

    @pl.when(decoder)
    def _():
        relay.up(True).start()
        wag.begin()

    def rows_of(k):
        return pl.ds(pl.multiple_of(k * CH, CH), CH)

    def norm_rows(k, carry):
        rows = rows_of(k)
        wide = x_ref[rows, :].astype(F32)
        scale = lax.rsqrt(jnp.mean(wide * wide, axis=1, keepdims=True) + epsilon)
        inv[rows, :] = jnp.broadcast_to(scale, (CH, 128))
        value = wide * scale
        normed[rows, :] = value
        sc[rows, :] = (value * gain_ref[...]).astype(BF)
        sg[q0, rows, :] = sc[rows, mine]
        return carry

    load_x.wait()
    lax.fori_loop(0, n_ch, norm_rows, 0)

    @pl.when(encoder)
    def _():
        sag.cross(crossing).start()
        relay.begin()

    load_w.wait()

    def cols_of(t):
        return pl.ds(pl.multiple_of(t * TILE, TILE), TILE)

    def preact_tile(t, carry):
        cols = cols_of(t)
        p = jnp.dot(sc[...], wv[:, cols], preferred_element_type=F32)
        sig = jax.nn.sigmoid(p)
        act[:, cols] = p * sig
        slope[:, cols] = sig * (1.0 + p * (1.0 - sig))
        return carry

    lax.fori_loop(0, tiles // 2, preact_tile, 0)

    @pl.when(encoder)
    def _():
        relay.step(1)

    lax.fori_loop(tiles // 2, tiles, preact_tile, 0)
    load_mem.wait()
    load_cot.wait()

    def turn_w(piece, pieces):
        def body(i, carry):
            a, b = i // tiles, lax.rem(i, tiles)
            wt[cols_of(b), cols_of(a)] = wv[cols_of(a), cols_of(b)].T
            return carry

        size = tiles * tiles // pieces
        lax.fori_loop(piece * size, (piece + 1) * size, body, 0, unroll=4)

    def chip_rows(q):
        return pl.ds(pl.multiple_of(q * 2 * rw, 2 * rw), 2 * rw)

    def turn_m(d):
        spots = [chip_rows(q) for q in wag.sources(d)]

        def body(t, carry):
            for at in spots:
                mwt[cols_of(t), at] = mwv[at, cols_of(t)].T
            return carry

        lax.fori_loop(0, tiles, body, 0, unroll=2)

    def gate_part(d):
        spots = [chip_rows(q) for q in wag.sources(d)]
        left = jnp.concatenate([mem_ref[:, at] for at in spots], axis=1)

        def body(t, carry):
            cols = cols_of(t)
            right = jnp.concatenate([mwv[at, cols] for at in spots], axis=0)
            p = jnp.dot(left, right, preferred_element_type=F32)
            if d == 0:
                gate[:, cols] = p
            elif d < far:
                gate[:, cols] += p
            else:
                slope[:, cols] = slope[:, cols] * (gate[:, cols] + p)
            return carry

        lax.fori_loop(0, tiles, body, 0, unroll=4)

    @pl.when(decoder)
    def _():
        wag.begin_other()
        wag.pair_step(0)
        turn_w(0, 4)
        wag.pair_step(1)
        turn_w(1, 4)
        wag.pair_step(2)
        wag.back_step(1, relay.back)
        wag.collect(0)
        gate_part(0)
        wag.pair_step(3)
        turn_m(0)
        wag.pair_step(4)
        turn_w(2, 4)
        wag.pair_step(5)
        wag.back_step(2, relay.back)
        wag.collect(1)
        gate_part(1)
        wag.pair_step(6)
        turn_m(1)
        wag.pair_step(7)
        turn_w(3, 4)
        wag.pair_step(8)
        wag.back_step(3, relay.back)
        wag.collect(2)
        gate_part(2)
        wag.pair_step(9)
        turn_m(2)
        wag.pair_step(10)
        wag.back_step(4, relay.back)
        sag.cross(crossing).start()
        wag.pair_step(11)
        wag.collect(3)
        gate_part(3)
        turn_m(3)
        wag.collect(4)
        gate_part(4)
        sag.begin()
        turn_m(4)

        @pl.when(above >= 2)
        def _():
            sag.begin_other(crossing)
            sag.pair_step(0)

        @pl.when(above >= 3)
        def _():
            sag.pair_step(1)

    @pl.when(encoder)
    def _():
        relay.step(2)
        turn_w(0, 4)
        relay.step(3)
        turn_w(1, 4)
        relay.step(4)
        sag.begin()
        sag.begin_other(crossing)
        turn_w(2, 4)
        turn_w(3, 4)
        for i in range(last_pair - 2):
            sag.pair_step(i)

    @pl.when(s == n_sec - 1)
    def _():
        live = lax.broadcasted_iota(jnp.int32, (toks, TILE), 0) < len_ref[0]

        def body(t, carry):
            cols = cols_of(t)
            gbuf[:, cols] = jnp.where(live, cot_ref[:, cols], jnp.zeros((), BF))
            return carry

        lax.fori_loop(0, tiles, body, 0)

    gacc[...] = jnp.zeros_like(gacc)

    def down(src, dst, k, send_sems, recv_sems):
        rows = rows_of(k)
        return pltpu.make_async_remote_copy(
            src_ref=src.at[rows], dst_ref=dst.at[rows], send_sem=send_sems.at[k], recv_sem=recv_sems.at[k],
            device_id={"section": s - 1}, device_id_type=MESH)

    groups = [(0, 3 * CH), (3 * CH, 2 * CH), (5 * CH, CH), (6 * CH, CH), (7 * CH, CH)]
    direct = (2, 3, 4)
    round_z = [nz // 2] + [v for i in range(nz // 2 - 1, 0, -1) for v in (i, nz - i)]

    def late_send(g):
        start, size = groups[g]
        rows = pl.ds(start, size)

        def send(yy, zz):
            pltpu.make_async_remote_copy(
                src_ref=gpv.at[rows, pl.ds(pl.multiple_of(zz * cols_z, cols_z), cols_z)], dst_ref=gpg.at[q0, rows],
                send_sem=late_s.at[g], recv_sem=late_r.at[g], device_id=device(yy, zz, c), device_id_type=MESH).start()

        for i in round_z:
            send(y, lax.rem(z + i, nz))
        if g in direct:
            @pl.when(encoder)
            def _():
                for i in round_z + [0]:
                    send(1 - y, lax.rem(z + i, nz))

    def late_done(g, count):
        start, size = groups[g]
        ref = gpg.at[pl.ds(0, count), pl.ds(start, size)]
        return pltpu.make_async_remote_copy(
            src_ref=ref, dst_ref=ref, send_sem=late_s.at[g], recv_sem=late_r.at[g],
            device_id={"dp": q0 * 2 + 1 - c}, device_id_type=MESH)

    def late_recv(g):
        if g not in direct:
            late_done(g, nz - 1).wait_recv()
            return

        @pl.when(encoder)
        def _():
            late_done(g, nq - 1).wait_recv()

        @pl.when(decoder)
        def _():
            late_done(g, nz - 1).wait_recv()

    def late_pass(g):
        start, size = groups[g]
        ref = gpg.at[pl.ds(pl.multiple_of(y * nz, nz), nz), pl.ds(start, size)]
        return pltpu.make_async_remote_copy(
            src_ref=ref, dst_ref=ref, send_sem=pass_s.at[g], recv_sem=pass_r.at[g],
            device_id=device(1 - y, z, c), device_id_type=MESH)

    def term(k):
        rows = rows_of(k)
        up = gbuf[rows, :].astype(F32)
        grad_gate = (up * act[rows, :]).astype(BF)
        for t in range(tiles):
            cols = slice(t * TILE, (t + 1) * TILE)
            ts[:, cols] = jnp.dot(grad_gate, mwt[:, cols], preferred_element_type=F32)

        @pl.when(s < n_sec - 1)
        def _():
            down(tsend, tbuf, k, t_s, t_r).wait_recv()
            tsend[rows, :] = (ts[...] + tbuf[rows, :].astype(F32)).astype(BF)

        @pl.when(s == n_sec - 1)
        def _():
            tsend[rows, :] = ts[...].astype(BF)

    passing = [(0, 3, 0), (0, 7, 1), (1, 1, 0), (1, 3, 1), (1, 6, 2), (2, 1, 1), (2, 4, 2), (2, 6, 3),
               (3, 1, 2), (3, 4, 3), (3, 6, 4)]

    def own_rows(g):
        rows = pl.ds(groups[g][0], groups[g][1])
        gpg[q0, rows, :] = gpv[rows, mine_z]

    def chunk(k, carry):
        rows = rows_of(k)

        @pl.when(s < n_sec - 1)
        def _():
            down(gin_ref, gbuf, k, g_s, g_r).wait_recv()

        @pl.when(s == half)
        def _():
            term(k)
            down(tsend, gbuf, k, t_s, g_r).start()

        gpv[rows, :] = (gbuf[rows, :].astype(F32) * slope[rows, :]).astype(BF)
        grad_pre = gpv[rows, :]
        total = jnp.zeros((CH, 128), F32)
        for t in range(tiles):
            cols = slice(t * TILE, (t + 1) * TILE)
            p = jnp.dot(grad_pre, wt[:, cols], preferred_element_type=F32)
            both = p * normed[rows, cols]
            gacc[:, cols] += both
            h = p * gain_ref[:, cols]
            gs[:, cols] = h
            weighted = both * gain_ref[:, cols]
            for i in range(TILE // 128):
                total = total + weighted[:, i * 128:(i + 1) * 128]
        center = jnp.sum(total, axis=1, keepdims=True) * (1.0 / feats)
        scale = inv[rows, 0:1]
        for t in range(tiles):
            cols = slice(t * TILE, (t + 1) * TILE)
            gin_ref[rows, cols] = (
                gbuf[rows, cols].astype(F32) + scale * (gs[:, cols] - normed[rows, cols] * center)
            ).astype(BF)

        @pl.when((s > 0) & (s != half))
        def _():
            down(gin_ref, gbuf, k, g_s, g_r).start()

        @pl.when(s > half)
        def _():
            term(k)
            down(tsend, tbuf, k, t_s, t_r).start()

        for g, (start, size) in enumerate(groups[:-1]):
            @pl.when(k == (start + size) // CH - 1)
            def _(g=g):
                late_send(g)
                own_rows(g)

        @pl.when(encoder & (k == 3))
        def _():
            sag.pair_step(last_pair - 2)
            sag.pair_step(last_pair - 1)

        for g, at in ((0, 5), (1, 6)):
            @pl.when(encoder & (k == at))
            def _(g=g):
                late_recv(g)
                late_pass(g).start()

        for up, at in ((0, 2), (1, 0)):
            @pl.when(decoder & (above == up) & (k == at))
            def _():
                sag.begin_other(crossing)

        for up, at, i in passing:
            @pl.when(decoder & (above == up) & (k == at))
            def _(i=i):
                sag.pair_step(i)

        return carry

    lax.fori_loop(0, n_ch, chunk, 0)

    late_send(len(groups) - 1)
    part = gacc[...]
    for q in range(nq):
        gnv[q] = part[0:8, q * 128:(q + 1) * 128] + part[8:16, q * 128:(q + 1) * 128]

    def gain_send(i, carry):
        q = lax.rem(q0 + i, nq)
        pltpu.make_async_remote_copy(
            src_ref=gnv.at[q], dst_ref=gng.at[q0], send_sem=tail_s.at[2], recv_sem=tail_r.at[2],
            device_id={"dp": q * 2 + c}, device_id_type=MESH).start()
        return carry

    lax.fori_loop(1, nq, gain_send, 0)
    gng[q0] = gnv[q0]
    store_gin = load(gin_ref, gin_hbm, 5)

    own_rows(len(groups) - 1)

    @pl.when(decoder)
    def _():
        for i in range(2, last_pair):
            @pl.when(i >= 2 + above)
            def _(i=i):
                sag.pair_step(i)

            if 3 <= i:
                late_recv(i - 3)
                late_pass(i - 3).start()
        for g in range(len(groups)):
            late_pass(g).wait_recv()

    @pl.when(encoder)
    def _():
        late_recv(2)
        late_recv(3)
        late_pass(0).wait_recv()
        late_pass(1).wait_recv()

    most = toks - CH
    kk = nq * most
    parts = width // TILE
    gpt[:, 0:kk] = gpg[:, 0:most, :].reshape(kk, cols_z).T

    def product(t, carry):
        cols = cols_of(t)
        dwt[:, cols] = jnp.dot(gpt[:, 0:kk], sg[:, 0:most, cols].reshape(kk, TILE), preferred_element_type=F32)
        return carry

    lax.fori_loop(0, parts, product, 0, unroll=2)

    @pl.when(encoder)
    def _():
        late_recv(len(groups) - 1)

    gpt[:, kk:nq * toks] = gpg[:, most:toks, :].reshape(nq * CH, cols_z).T

    other = {"dp": q0 * 2 + 1 - c}
    per = TILE // (2 * rw)
    first_part = z // per

    def swap(t):
        spots = pl.ds(t * per, per)
        return pltpu.make_async_remote_copy(
            src_ref=dws.at[spots, 1 - c], dst_ref=dwp.at[spots], send_sem=swap_s.at[t], recv_sem=swap_r.at[t],
            device_id=other, device_id_type=MESH)

    turns = [parts // 2] + [v for i in range(parts // 2 - 1, 0, -1) for v in (i, parts - i)] + [0]

    def finish(i):
        t = lax.rem(first_part + i, parts)
        cols = cols_of(t)
        p = dwt[:, cols] + jnp.dot(
            gpt[:, kk:nq * toks], sg[:, most:toks, cols].reshape(nq * CH, TILE), preferred_element_type=F32)
        dws[pl.ds(t * per, per)] = p.T.astype(BF).reshape(per, 2, rw, cols_z)
        swap(t).start()

    for i in turns:
        finish(i)

    def deliver(i):
        t = lax.rem(first_part + i, parts)
        swap(t).wait_recv()
        for e in range(per):
            zz = t * per + e
            dwo[zz] = (dws[zz, c].astype(F32) + dwp[zz].astype(F32)).astype(BF)

            @pl.when(zz != z)
            def _(zz=zz):
                pltpu.make_async_remote_copy(
                    src_ref=dwo.at[zz], dst_ref=og.at[z], send_sem=tail_s.at[1], recv_sem=tail_r.at[1],
                    device_id=device(y, zz, c), device_id_type=MESH).start()

    for i in turns:
        deliver(i)
    store_own = load(dwo.at[z], og.at[z], 0)

    gain_all = pltpu.make_async_remote_copy(
        src_ref=gng.at[pl.ds(0, nq - 1)], dst_ref=gng.at[pl.ds(0, nq - 1)], send_sem=tail_s.at[2],
        recv_sem=tail_r.at[2], device_id=other, device_id_type=MESH)
    gain_all.wait()
    gnl[...] = jnp.sum(gng[...], axis=0)
    gain_copy = pltpu.make_async_remote_copy(
        src_ref=gnl, dst_ref=gnp, send_sem=tail_s.at[0], recv_sem=tail_r.at[0], device_id=other, device_id_type=MESH)
    gain_copy.start()

    for g in range(len(groups)):
        if g not in direct:
            late_done(g, nz - 1).wait_send()
            late_pass(g).wait_send()
            continue

        @pl.when(encoder)
        def _(g=g):
            late_done(g, nq - 1).wait_send()

        @pl.when(decoder)
        def _(g=g):
            late_done(g, nz - 1).wait_send()
            late_pass(g).wait_send()
    for k in range(n_ch):
        @pl.when((s > 0) & (s != half))
        def _(k=k):
            down(gin_ref, gbuf, k, g_s, g_r).wait_send()

        @pl.when(decoder)
        def _(k=k):
            down(tsend, tbuf, k, t_s, t_r).wait_send()

    sag.sent(crossing)

    @pl.when(decoder)
    def _():
        wag.sent()
        relay.up(True).wait_send()

    @pl.when(encoder)
    def _():
        relay.sent()

    for t in range(parts):
        swap(t).wait_send()
    store_gin.wait()
    gain_copy.wait()
    gains = jnp.sum(gnl[...] + gnp[...], axis=0, keepdims=True) * (1.0 / n_dp)
    gg_ref[...] = jnp.where(c == 0, gains[:, 0:rw], gains[:, rw:2 * rw])

    whole = pltpu.make_async_remote_copy(
        src_ref=dwo.at[pl.ds(0, nz - 1)], dst_ref=og.at[pl.ds(0, nz - 1)], send_sem=tail_s.at[1],
        recv_sem=tail_r.at[1], device_id=other, device_id_type=MESH)
    store_own.wait()
    whole.wait()


def publish_kernel(n_dp, gin_ref, blocks_ref, gain_ref, gin_out, dw_out, gain_out):
    gin_out[...] = gin_ref[...]
    nz, _, cols_z = blocks_ref.shape
    for zz in range(nz):
        dw_out[:, zz * cols_z:(zz + 1) * cols_z] = blocks_ref[zz].astype(F32) * (1.0 / n_dp)
    gain_out[...] = gain_ref[...]


def local(section_inputs, section_weights, memory_weights, norm_gains, memory, cotangent, lengths):
    n_sec, n_dp = lax.axis_size("section"), lax.axis_size("dp")
    toks, feats = section_inputs.shape[1:]
    rw = memory_weights.shape[1]
    nq = n_dp // 2
    nz = nq // 2
    n_ch = toks // CH
    vmem = pl.BlockSpec(memory_space=pltpu.VMEM)
    hbm = pl.BlockSpec(memory_space=pl.ANY)
    square = pltpu.VMEM((feats, feats), BF)
    wide = pltpu.VMEM((toks, feats), F32)
    narrow = pltpu.VMEM((toks, feats), BF)
    cols_z = feats // nz
    blocks = pltpu.VMEM((nz, rw, cols_z), BF)
    dma = pltpu.SemaphoreType.DMA
    gin, dw, gg = pl.pallas_call(
        functools.partial(relay_kernel, n_sec, n_dp),
        out_shape=(
            jax.ShapeDtypeStruct((toks, feats), BF),
            jax.ShapeDtypeStruct((nz, rw, cols_z), BF),
            jax.ShapeDtypeStruct((1, rw), F32),
        ),
        in_specs=[hbm, hbm, hbm, vmem, hbm, hbm, pl.BlockSpec(memory_space=pltpu.SMEM)],
        out_specs=(hbm, hbm, vmem),
        scratch_shapes=[
            narrow, narrow, narrow, narrow,
            square, square, square, square, narrow,
            pltpu.VMEM((nq, toks, feats // 2), BF),
            wide, wide, wide, wide,
            pltpu.VMEM((cols_z, feats // 2), F32),
            pltpu.VMEM((toks, 128), F32),
            narrow, narrow, narrow,
            narrow,
            pltpu.VMEM((CH, feats), F32),
            pltpu.VMEM((CH, feats), F32),
            pltpu.VMEM((CH, feats), F32),
            pltpu.VMEM((nq, toks, cols_z), BF),
            pltpu.VMEM((cols_z, nq * toks), BF),
            pltpu.VMEM((nz, 2, rw, cols_z), BF),
            blocks, blocks,
            pltpu.VMEM((nq, 8, 128), F32),
            pltpu.VMEM((nq, 8, 128), F32),
            pltpu.VMEM((8, 128), F32),
            pltpu.VMEM((8, 128), F32),
            dma((6,)),
            dma((Gather.count(nz),)), dma((Gather.count(nz),)),
            dma((Relay.count(nz),)), dma((Relay.count(nz),)),
            dma((HalfGather.count(nz),)), dma((HalfGather.count(nz),)),
            dma((n_ch,)), dma((n_ch,)), dma((n_ch,)), dma((n_ch,)),
            dma((5,)), dma((5,)),
            dma((5,)), dma((5,)),
            dma((feats // 2 // TILE,)), dma((feats // 2 // TILE,)),
            dma((3,)), dma((3,)),
        ],
        compiler_params=pltpu.CompilerParams(
            collective_id=0, has_side_effects=True, vmem_limit_bytes=60 * 1024 * 1024
        ),
    )(
        section_inputs[0], section_weights[0], memory_weights[0], norm_gains, memory, cotangent,
        lengths,
    )
    gin, dw, gg = pl.pallas_call(
        functools.partial(publish_kernel, n_dp),
        out_shape=(
            jax.ShapeDtypeStruct((toks, feats), BF),
            jax.ShapeDtypeStruct((rw, feats), F32),
            jax.ShapeDtypeStruct((1, rw), F32),
        ),
        in_specs=[vmem] * 3,
        out_specs=(vmem,) * 3,
    )(gin, dw, gg)
    return gin[None], dw[None], gg


def solution(mesh):
    return jax.shard_map(
        local,
        mesh=mesh,
        in_specs=(
            P("section", "dp", None),
            P("section", None, None),
            P("section", "dp", None),
            P("section", None),
            P("dp", None),
            P("dp", None),
            P("dp"),
        ),
        out_specs=(P("section", "dp", None), P("section", "dp", None), P("section", "dp")),
        check_vma=False,
    )
```

```python
import functools

import jax
import jax.numpy as jnp
from jax import lax
from jax.experimental import pallas as pl
from jax.experimental.pallas import tpu as pltpu
from jax.sharding import PartitionSpec as P

epsilon = 1e-06
BF = jnp.bfloat16
F32 = jnp.float32
CH = 16
TILE = 256


def arrived(ref, sem, dev):
    pltpu.make_async_remote_copy(
        src_ref=ref, dst_ref=ref, send_sem=sem, recv_sem=sem, device_id=dev,
        device_id_type=pl.DeviceIdType.MESH).wait_recv()


def left(ref, sem, dev):
    pltpu.make_async_remote_copy(
        src_ref=ref, dst_ref=ref, send_sem=sem, recv_sem=sem, device_id=dev,
        device_id_type=pl.DeviceIdType.MESH).wait_send()


class Gather:
    def __init__(self, buf, rows, place, send_sem, recv_sems, lane=None):
        self.buf, self.rows, self.place = buf, rows, place
        self.y, self.z, self.c, self.nz, self.device = place
        self.lane = self.c if lane is None else lane
        self.far = self.nz // 2
        self.ss, self.rs = send_sem, recv_sems
        self.mate = self.device(self.y, self.z, 1 - self.c)

    @staticmethod
    def count(nz):
        return 5 * (nz // 2) + 3

    def block(self, q, start, size):
        return self.buf.at[pl.ds(pl.multiple_of((q * 2 + self.lane) * self.rows + start, 16), size)]

    def copy(self, q, start, size, ident, dev):
        ref = self.block(q, start, size)
        return pltpu.make_async_remote_copy(
            src_ref=ref, dst_ref=ref, send_sem=self.ss.at[0], recv_sem=self.rs.at[ident],
            device_id=dev, device_id_type=pl.DeviceIdType.MESH)

    def await_rows(self, rows, ident):
        arrived(self.buf.at[pl.ds(0, rows)], self.rs.at[ident], self.mate)

    def turn(self, z):
        return lax.rem(z + 2 * self.nz, self.nz)

    def source(self, way, d):
        return self.turn(self.z - (1 - 2 * way) * d)

    def ways(self, d, m=0):
        return (0,) if d == 0 or (d == self.far and m == 1) else (0, 1)

    def span(self, way, d, m):
        half, quarter = self.rows // 2, self.rows // 4
        if m in (1, 3):
            return (half if m == 1 else half + quarter), quarter
        return (way * quarter, quarter) if d == self.far else (0, half)

    def z_copy(self, way, d, m):
        y = 1 - self.y if m == 2 else self.y
        start, size = self.span(way, d, m)
        dev = self.device(self.y, self.turn(self.z + 1 - 2 * way), self.c)
        return self.copy(y * self.nz + self.source(way, d - 1), start, size, 3 * (d - 1) + m, dev)

    def y_copy(self, way, d):
        start, size = self.span(way, d, 1)
        dev = self.device(1 - self.y, self.z, self.c)
        return self.copy(self.y * self.nz + self.source(way, d), start, size, 3 * self.far + d, dev)

    def first_copy(self):
        dev = self.device(1 - self.y, self.z, self.c)
        return self.copy(self.y * self.nz + self.z, 0, self.rows // 2, 4 * self.far + 1, dev)

    def hand(self, kind, args):
        ident = 4 * self.far + 2
        if kind in ("own", "first"):
            y = self.y if kind == "own" else 1 - self.y
            self.copy(y * self.nz + self.z, 0, self.size(kind, args), ident, self.mate).start()
            return
        way, d, m = args
        start, size = self.span(way, d, 3 if kind == "back" else m)
        y = {"z": 1 - self.y if m == 2 else self.y, "back": 1 - self.y if m else self.y, "y": 1 - self.y}[kind]
        self.copy(y * self.nz + self.source(way, d), start, size, ident + d, self.mate).start()

    def size(self, kind, args):
        if kind in ("own", "first"):
            return self.rows if kind == "own" else self.rows // 2
        way, d, m = args
        return self.span(way, d, 3 if kind == "back" else m)[1]

    def begin(self):
        self.first_copy().start()
        for m in (1, 0):
            for way in (0, 1):
                self.z_copy(way, 1, m).start()
        self.y_copy(0, 0).start()
        self.hand("own", ())

    def begin_other(self):
        self.await_rows(self.rows // 2, 4 * self.far + 1)
        for way in (0, 1):
            self.z_copy(way, 1, 2).start()
        self.hand("first", ())

    def pair_step(self, i):
        d, m = i // 3 + 1, (1, 0, 2)[i % 3]
        self.await_rows(sum(self.span(way, d, m)[1] for way in self.ways(d, m)), 3 * (d - 1) + m)
        if d < self.far:
            for way in self.ways(d + 1, m):
                self.z_copy(way, d + 1, m).start()
        for way in self.ways(d, m):
            if m == 1:
                self.y_copy(way, d).start()
            self.hand("z", (way, d, m))

    def backs(self, d):
        if d == 0:
            return [(0, 0, 1)]
        return [(0, d, 0), (1, d, 1)] if d == self.far else [(way, d, m) for m in (0, 1) for way in (0, 1)]

    def crossed(self, d):
        return [(way, d, 1) for way in self.ways(d, 1)]

    def handed(self, d):
        if d == 0:
            came = [("own", ()), ("first", ())]
        else:
            came = [("z", (way, d, m)) for m in (0, 1, 2) for way in self.ways(d, m)]
        return came + [("back", args) for args in self.backs(d)] + [("y", args) for args in self.crossed(d)]

    def pass_backs(self, d, relay):
        relay.await_back(d)
        for args in self.backs(d):
            self.hand("back", args)
        self.await_rows(sum(self.size("y", args) for args in self.crossed(d)), 3 * self.far + d)
        for args in self.crossed(d):
            self.hand("y", args)

    def collect(self, d):
        self.await_rows(sum(self.size(*h) for h in self.handed(d)), 4 * self.far + 2 + d)

    def sent(self):
        total = self.rows // 2
        for d in range(self.far + 1):
            total += sum(self.size("y", args) for args in self.crossed(d))
            total += sum(self.size(*h) * (2 if h[0] == "z" else 1) for h in self.handed(d))
        left(self.buf.at[pl.ds(0, total)], self.ss.at[0], self.mate)

    def sources(self, d):
        spots = {0: (0,), self.far: (self.far,)}.get(d, (d, -d))
        return [y * self.nz + self.turn(self.z + o) for o in spots for y in (0, 1)]


class Relay:
    def __init__(self, gather, section, half, sems):
        self.g, self.ss, self.rs = gather, *sems
        g = gather
        self.quarter = g.rows // 4
        self.partner = {
            "section": jnp.where(section >= half, section - half, section + half),
            "dp": ((1 - g.y) * g.nz + g.z) * 2 + g.c,
        }

    @staticmethod
    def count(nz):
        return 3 + 3 * (nz // 2)

    def copy(self, y, src, ident, dev):
        g = self.g
        start, size = g.span(0, 1, 3)
        ref = g.block(y * g.nz + src, start, size)
        return pltpu.make_async_remote_copy(
            src_ref=ref, dst_ref=ref, send_sem=self.ss.at[0], recv_sem=self.rs.at[ident],
            device_id=dev, device_id_type=pl.DeviceIdType.MESH)

    def await_quarters(self, number, ident):
        arrived(self.g.buf.at[pl.ds(0, number * self.quarter)], self.rs.at[ident], self.partner)

    def await_back(self, d):
        self.await_quarters(len(self.g.backs(d)), 2 + 2 * self.g.far + d)

    def up(self):
        return self.copy(self.g.y, self.g.z, 0, self.partner)

    def ring(self, way, d, m):
        g = self.g
        dev = g.device(g.y, g.turn(g.z + 1 - 2 * way), g.c)
        return self.copy(g.y if m else 1 - g.y, g.source(way, d - 1), 2 + 2 * (d - 1) + m, dev)

    def back(self, way, d, m):
        g = self.g
        return self.copy(g.y if m else 1 - g.y, g.source(way, d), 2 + 2 * g.far + d, self.partner)

    def begin(self):
        g = self.g
        self.await_quarters(1, 0)
        self.copy(1 - g.y, g.z, 1, g.device(1 - g.y, g.z, g.c)).start()
        for way in (0, 1):
            self.ring(way, 1, 0).start()

    def begin_other(self):
        self.await_quarters(1, 1)
        for way in (0, 1):
            self.ring(way, 1, 1).start()
        self.back(0, 0, 1).start()

    def step(self, d):
        g = self.g
        for m in (0, 1):
            came = [args for args in g.backs(d) if args[2] == m]
            self.await_quarters(len(came), 2 + 2 * (d - 1) + m)
            for way, _, _ in came:
                if d < g.far and (way, d + 1, m) in g.backs(d + 1):
                    self.ring(way, d + 1, m).start()
                self.back(way, d, m).start()

    def sent(self, encoder):
        number = 2 + 2 * sum(len(self.g.backs(d)) for d in range(1, self.g.far + 1)) if encoder else 1
        left(self.g.buf.at[pl.ds(0, number * self.quarter)], self.ss.at[0], self.partner)


class HalfGather:
    def __init__(self, buf, place, send_sem, recv_sems):
        self.buf, self.ss, self.rs = buf, send_sem, recv_sems
        self.y, self.z, self.c, self.nz, self.device = place
        self.far = self.nz // 2
        self.rows = buf.shape[1]
        self.mate = self.device(self.y, self.z, 1 - self.c)

    @staticmethod
    def count(nz):
        return 1 + 2 * (nz // 2)

    def turn(self, z):
        return lax.rem(z + 2 * self.nz, self.nz)

    def cross(self, src):
        return pltpu.make_async_remote_copy(
            src_ref=src, dst_ref=self.buf.at[self.y * self.nz + self.z], send_sem=self.ss.at[0],
            recv_sem=self.rs.at[0], device_id=self.device(1 - self.y, self.z, self.c),
            device_id_type=pl.DeviceIdType.MESH)

    def z_copy(self, way, d, m):
        sign = 1 - 2 * way
        src = self.turn(self.z - sign * (d - 1))
        y = 1 - self.y if m else self.y
        size = self.rows // 2 if d == self.far else self.rows
        ref = self.buf.at[y * self.nz + src, pl.ds(way * size if d == self.far else 0, size)]
        return pltpu.make_async_remote_copy(
            src_ref=ref, dst_ref=ref, send_sem=self.ss.at[0], recv_sem=self.rs.at[1 + 2 * (d - 1) + m],
            device_id=self.device(self.y, self.turn(self.z + sign), self.c), device_id_type=pl.DeviceIdType.MESH)

    def begin(self):
        for way in (0, 1):
            self.z_copy(way, 1, 0).start()

    def begin_other(self):
        arrived(self.buf.at[0], self.rs.at[0], self.mate)
        for way in (0, 1):
            self.z_copy(way, 1, 1).start()

    def pair_step(self, i):
        d, m = i // 2 + 1, i % 2
        arrived(self.buf.at[pl.ds(0, 1 if d == self.far else 2)], self.rs.at[1 + i], self.mate)
        if d < self.far:
            for way in (0, 1):
                self.z_copy(way, d + 1, m).start()

    def sent(self):
        left(self.buf.at[pl.ds(0, 2 * self.nz - 1)], self.ss.at[0], self.mate)


def relay_kernel(n_sec, n_dp,
                 x_hbm, w_hbm, mw_hbm, gain_ref, mem_hbm, cot_hbm, len_ref,
                 gin_hbm, og, gg_ref,
                 x_ref, mem_ref, cot_ref, gin_ref,
                 wv, wt, mwv, mwt, sc, sg, normed, slope, act, gate, dwt, inv, gbuf, tbuf, tsend,
                 gpv, gacc, gs, ts, gpg, gpt, dws, dwp, dwo, gnv, gng, gnl, gnp,
                 load_sem, wag_s, wag_r, rel_s, rel_r, sag_s, sag_r, g_s, g_r, t_s, t_r, late_s, late_r, pass_s, pass_r, swap_s, swap_r,
                 tail_s, tail_r):
    s = lax.axis_index("section")
    j = lax.axis_index("dp")
    half = n_sec // 2
    nq = n_dp // 2
    nz = nq // 2
    c = lax.rem(j, 2)
    q0 = j // 2
    y, z = q0 // nz, lax.rem(q0, nz)
    toks, feats = x_ref.shape
    rw = mw_hbm.shape[0]
    n_ch = toks // CH
    tiles = feats // TILE
    decoder = s >= half
    encoder = s < half
    above = n_sec - 1 - s
    MESH = pl.DeviceIdType.MESH

    def device(yy, zz, cc):
        return {"dp": (yy * nz + zz) * 2 + cc}

    def load(src, dst, i):
        copy = pltpu.make_async_copy(src, dst, load_sem.at[i])
        copy.start()
        return copy

    barrier = pltpu.get_barrier_semaphore()

    def greet(i, carry):
        q = lax.rem(q0 + i, nq)
        pl.semaphore_signal(barrier, inc=1, device_id={"dp": q * 2 + c}, device_id_type=MESH)
        return carry

    lax.fori_loop(1, nq, greet, 0)
    pl.semaphore_signal(barrier, inc=1, device_id={"dp": q0 * 2 + 1 - c}, device_id_type=MESH)

    @pl.when(s > 0)
    def _():
        pl.semaphore_signal(barrier, inc=1, device_id={"section": s - 1}, device_id_type=MESH)

    @pl.when(s < n_sec - 1)
    def _():
        pl.semaphore_signal(barrier, inc=1, device_id={"section": s + 1}, device_id_type=MESH)

    load_m = pltpu.make_async_copy(
        mw_hbm, mwv.at[pl.ds(pl.multiple_of(j * rw, rw), rw)], load_sem.at[1])

    @pl.when(decoder)
    def _():
        load_m.start()

    load_x = load(x_hbm, x_ref, 2)
    load_w = load(w_hbm, wv, 0)
    load_mem = load(mem_hbm, mem_ref, 3)
    load_cot = load(cot_hbm, cot_ref, 4)

    pl.semaphore_signal(
        barrier, inc=1, device_id={"section": lax.rem(s + half, n_sec), "dp": ((1 - y) * nz + z) * 2 + c},
        device_id_type=MESH)
    ends = (s == 0) | (s == n_sec - 1)
    pl.semaphore_wait(barrier, nq + jnp.where(ends, 2, 3))

    place = (y, z, c, nz, device)

    wag = Gather(mwv, rw, place, wag_s, wag_r)
    relay = Relay(wag, s, half, (rel_s, rel_r))
    sag = HalfGather(sg, place, sag_s, sag_r)
    far = wag.far
    last_pair = 2 * far
    width = feats // 2
    cols_z = feats // nz
    mine, theirs = (pl.ds(pl.multiple_of(v * width, width), width) for v in (y, 1 - y))
    crossing = sc.at[:, theirs]
    mine_z = pl.ds(pl.multiple_of(z * cols_z, cols_z), cols_z)

    @pl.when(decoder)
    def _():
        load_m.wait()
        relay.up().start()
        wag.begin()

    def rows_of(k):
        return pl.ds(pl.multiple_of(k * CH, CH), CH)

    def norm_rows(k, carry):
        rows = rows_of(k)
        wide = x_ref[rows, :].astype(F32)
        scale = lax.rsqrt(jnp.mean(wide * wide, axis=1, keepdims=True) + epsilon)
        inv[rows, :] = jnp.broadcast_to(scale, (CH, 128))
        value = wide * scale
        normed[rows, :] = value
        sc[rows, :] = (value * gain_ref[...]).astype(BF)
        sg[q0, rows, :] = sc[rows, mine]
        return carry

    load_x.wait()
    lax.fori_loop(0, n_ch, norm_rows, 0)

    @pl.when(encoder)
    def _():
        sag.cross(crossing).start()
        relay.begin()

    load_w.wait()

    def cols_of(t):
        return pl.ds(pl.multiple_of(t * TILE, TILE), TILE)

    def preact_tile(t, carry):
        cols = cols_of(t)
        p = jnp.dot(sc[...], wv[:, cols], preferred_element_type=F32)
        sig = jax.nn.sigmoid(p)
        act[:, cols] = p * sig
        slope[:, cols] = sig * (1.0 + p * (1.0 - sig))
        return carry

    lax.fori_loop(0, tiles // 2, preact_tile, 0)

    @pl.when(encoder)
    def _():
        relay.begin_other()
        relay.step(1)

    lax.fori_loop(tiles // 2, tiles, preact_tile, 0)
    load_mem.wait()
    load_cot.wait()

    def turn_w(piece, pieces):
        def body(i, carry):
            a, b = i // tiles, lax.rem(i, tiles)
            wt[cols_of(b), cols_of(a)] = wv[cols_of(a), cols_of(b)].T
            return carry

        size = tiles * tiles // pieces
        lax.fori_loop(piece * size, (piece + 1) * size, body, 0, unroll=4)

    def chip_rows(q):
        return pl.ds(pl.multiple_of(q * 2 * rw, 2 * rw), 2 * rw)

    def turn_m(d):
        spots = [chip_rows(q) for q in wag.sources(d)]

        def body(t, carry):
            for at in spots:
                mwt[cols_of(t), at] = mwv[at, cols_of(t)].T
            return carry

        lax.fori_loop(0, tiles, body, 0, unroll=2)

    def gate_part(d):
        spots = [chip_rows(q) for q in wag.sources(d)]
        left = jnp.concatenate([mem_ref[:, at] for at in spots], axis=1)

        def body(t, carry):
            cols = cols_of(t)
            right = jnp.concatenate([mwv[at, cols] for at in spots], axis=0)
            p = jnp.dot(left, right, preferred_element_type=F32)
            if d == 0:
                gate[:, cols] = p
            elif d < far:
                gate[:, cols] += p
            else:
                slope[:, cols] = slope[:, cols] * (gate[:, cols] + p)
            return carry

        lax.fori_loop(0, tiles, body, 0, unroll=4)

    @pl.when(decoder)
    def _():
        wag.begin_other()
        wag.pair_step(0)
        turn_w(0, 4)
        wag.pair_step(1)
        turn_w(1, 4)
        wag.pair_step(2)
        turn_w(2, 4)
        wag.pair_step(3)
        turn_w(3, 4)
        wag.pair_step(4)
        wag.pass_backs(0, relay)
        wag.pair_step(5)
        sag.cross(crossing).start()
        wag.collect(0)
        gate_part(0)
        turn_m(0)
        wag.pair_step(6)
        wag.pass_backs(1, relay)
        wag.pair_step(7)
        wag.collect(1)
        gate_part(1)
        wag.pair_step(8)
        turn_m(1)
        wag.pass_backs(2, relay)
        wag.pair_step(9)
        wag.collect(2)
        gate_part(2)
        wag.pair_step(10)
        turn_m(2)
        wag.pair_step(11)
        wag.pass_backs(3, relay)
        wag.pass_backs(4, relay)
        wag.collect(3)
        gate_part(3)
        turn_m(3)
        wag.collect(4)
        gate_part(4)
        sag.begin()
        turn_m(4)

        @pl.when(above >= 2)
        def _():
            sag.begin_other()
            sag.pair_step(0)

        @pl.when(above >= 3)
        def _():
            sag.pair_step(1)

    @pl.when(encoder)
    def _():
        relay.step(2)
        turn_w(0, 4)
        relay.step(3)
        turn_w(1, 4)
        relay.step(4)
        sag.begin()
        sag.begin_other()
        turn_w(2, 4)
        turn_w(3, 4)
        for i in range(last_pair - 2):
            sag.pair_step(i)

    @pl.when(s == n_sec - 1)
    def _():
        live = lax.broadcasted_iota(jnp.int32, (toks, TILE), 0) < len_ref[0]

        def body(t, carry):
            cols = cols_of(t)
            gbuf[:, cols] = jnp.where(live, cot_ref[:, cols], jnp.zeros((), BF))
            return carry

        lax.fori_loop(0, tiles, body, 0)

    gacc[...] = jnp.zeros_like(gacc)

    def down(src, dst, k, send_sems, recv_sems):
        rows = rows_of(k)
        return pltpu.make_async_remote_copy(
            src_ref=src.at[rows], dst_ref=dst.at[rows], send_sem=send_sems.at[0], recv_sem=recv_sems.at[k],
            device_id={"section": s - 1}, device_id_type=MESH)

    groups = [(0, 3 * CH), (3 * CH, 2 * CH), (5 * CH, CH), (6 * CH, CH), (7 * CH, CH)]
    direct = (2, 3, 4)
    round_z = [nz // 2] + [v for i in range(nz // 2 - 1, 0, -1) for v in (i, nz - i)]

    def late_send(g):
        start, size = groups[g]
        rows = pl.ds(start, size)

        def send(yy, zz):
            pltpu.make_async_remote_copy(
                src_ref=gpv.at[rows, pl.ds(pl.multiple_of(zz * cols_z, cols_z), cols_z)], dst_ref=gpg.at[q0, rows],
                send_sem=late_s.at[0], recv_sem=late_r.at[g], device_id=device(yy, zz, c), device_id_type=MESH).start()

        for i in round_z:
            send(y, lax.rem(z + i, nz))
        if g in direct:
            @pl.when(encoder)
            def _():
                for i in round_z + [0]:
                    send(1 - y, lax.rem(z + i, nz))

    def late_done(g, count):
        start, size = groups[g]
        ref = gpg.at[pl.ds(0, count), pl.ds(start, size)]
        return pltpu.make_async_remote_copy(
            src_ref=ref, dst_ref=ref, send_sem=late_s.at[0], recv_sem=late_r.at[g],
            device_id={"dp": q0 * 2 + 1 - c}, device_id_type=MESH)

    def late_recv(g):
        if g not in direct:
            late_done(g, nz - 1).wait_recv()
            return

        @pl.when(encoder)
        def _():
            late_done(g, nq - 1).wait_recv()

        @pl.when(decoder)
        def _():
            late_done(g, nz - 1).wait_recv()

    def late_pass(g):
        start, size = groups[g]
        ref = gpg.at[pl.ds(pl.multiple_of(y * nz, nz), nz), pl.ds(start, size)]
        return pltpu.make_async_remote_copy(
            src_ref=ref, dst_ref=ref, send_sem=pass_s.at[0], recv_sem=pass_r.at[g],
            device_id=device(1 - y, z, c), device_id_type=MESH)

    def term(k):
        rows = rows_of(k)
        up = gbuf[rows, :].astype(F32)
        grad_gate = (up * act[rows, :]).astype(BF)
        for t in range(tiles):
            cols = slice(t * TILE, (t + 1) * TILE)
            ts[:, cols] = jnp.dot(grad_gate, mwt[:, cols], preferred_element_type=F32)

        @pl.when(s < n_sec - 1)
        def _():
            down(tsend, tbuf, k, t_s, t_r).wait_recv()
            tsend[rows, :] = (ts[...] + tbuf[rows, :].astype(F32)).astype(BF)

        @pl.when(s == n_sec - 1)
        def _():
            tsend[rows, :] = ts[...].astype(BF)

    passing = [(0, 3, 0), (0, 7, 1), (1, 1, 0), (1, 3, 1), (1, 6, 2), (2, 1, 1), (2, 4, 2), (2, 6, 3),
               (3, 1, 2), (3, 4, 3), (3, 6, 4)]

    def own_rows(g):
        rows = pl.ds(groups[g][0], groups[g][1])
        gpg[q0, rows, :] = gpv[rows, mine_z]

    def chunk(k, carry):
        rows = rows_of(k)

        @pl.when(s < n_sec - 1)
        def _():
            down(gin_ref, gbuf, k, g_s, g_r).wait_recv()

        @pl.when(s == half)
        def _():
            term(k)
            down(tsend, gbuf, k, t_s, g_r).start()

        gpv[rows, :] = (gbuf[rows, :].astype(F32) * slope[rows, :]).astype(BF)
        grad_pre = gpv[rows, :]
        total = jnp.zeros((CH, 128), F32)
        for t in range(tiles):
            cols = slice(t * TILE, (t + 1) * TILE)
            p = jnp.dot(grad_pre, wt[:, cols], preferred_element_type=F32)
            both = p * normed[rows, cols]
            gacc[:, cols] += both
            h = p * gain_ref[:, cols]
            gs[:, cols] = h
            weighted = both * gain_ref[:, cols]
            for i in range(TILE // 128):
                total = total + weighted[:, i * 128:(i + 1) * 128]
        center = jnp.sum(total, axis=1, keepdims=True) * (1.0 / feats)
        scale = inv[rows, 0:1]
        for t in range(tiles):
            cols = slice(t * TILE, (t + 1) * TILE)
            gin_ref[rows, cols] = (
                gbuf[rows, cols].astype(F32) + scale * (gs[:, cols] - normed[rows, cols] * center)
            ).astype(BF)

        @pl.when((s > 0) & (s != half))
        def _():
            down(gin_ref, gbuf, k, g_s, g_r).start()

        @pl.when(s > half)
        def _():
            term(k)
            down(tsend, tbuf, k, t_s, t_r).start()

        for g, (start, size) in enumerate(groups[:-1]):
            @pl.when(k == (start + size) // CH - 1)
            def _(g=g):
                late_send(g)
                own_rows(g)

        @pl.when(encoder & (k == 3))
        def _():
            sag.pair_step(last_pair - 2)
            sag.pair_step(last_pair - 1)

        for g, at in ((0, 5), (1, 6)):
            @pl.when(encoder & (k == at))
            def _(g=g):
                late_recv(g)
                late_pass(g).start()

        for up, at in ((0, 2), (1, 0)):
            @pl.when(decoder & (above == up) & (k == at))
            def _():
                sag.begin_other()

        for up, at, i in passing:
            @pl.when(decoder & (above == up) & (k == at))
            def _(i=i):
                sag.pair_step(i)

        return carry

    lax.fori_loop(0, n_ch, chunk, 0)

    late_send(len(groups) - 1)
    part = gacc[...]
    for q in range(nq):
        gnv[q] = part[0:8, q * 128:(q + 1) * 128] + part[8:16, q * 128:(q + 1) * 128]

    def gain_send(i, carry):
        q = lax.rem(q0 + i, nq)
        pltpu.make_async_remote_copy(
            src_ref=gnv.at[q], dst_ref=gng.at[q0], send_sem=tail_s.at[2], recv_sem=tail_r.at[2],
            device_id={"dp": q * 2 + c}, device_id_type=MESH).start()
        return carry

    lax.fori_loop(1, nq, gain_send, 0)
    gng[q0] = gnv[q0]
    store_gin = load(gin_ref, gin_hbm, 5)

    own_rows(len(groups) - 1)

    @pl.when(decoder)
    def _():
        for i in range(2, last_pair):
            @pl.when(i >= 2 + above)
            def _(i=i):
                sag.pair_step(i)

            if 3 <= i:
                late_recv(i - 3)
                late_pass(i - 3).start()
        for g in range(len(groups)):
            late_pass(g).wait_recv()

    @pl.when(encoder)
    def _():
        late_recv(2)
        late_pass(0).wait_recv()
        late_pass(1).wait_recv()

    most = toks - 2 * CH
    kk = nq * most
    parts = width // TILE
    gpt[:, 0:kk] = gpg[:, 0:most, :].reshape(kk, cols_z).T

    def product(t, carry):
        cols = cols_of(t)
        dwt[:, cols] = jnp.dot(gpt[:, 0:kk], sg[:, 0:most, cols].reshape(kk, TILE), preferred_element_type=F32)
        return carry

    lax.fori_loop(0, parts, product, 0, unroll=2)

    @pl.when(encoder)
    def _():
        late_recv(3)
        late_recv(4)

    gpt[:, kk:nq * toks] = gpg[:, most:toks, :].reshape(nq * 2 * CH, cols_z).T

    other = {"dp": q0 * 2 + 1 - c}
    per = TILE // (2 * rw)
    first_part = z // per

    def swap(t):
        spots = pl.ds(t * per, per)
        return pltpu.make_async_remote_copy(
            src_ref=dws.at[spots, 1 - c], dst_ref=dwp.at[spots], send_sem=swap_s.at[0], recv_sem=swap_r.at[t],
            device_id=other, device_id_type=MESH)

    turns = [parts // 2] + [v for i in range(parts // 2 - 1, 0, -1) for v in (i, parts - i)] + [0]

    def finish(i):
        t = lax.rem(first_part + i, parts)
        cols = cols_of(t)
        p = dwt[:, cols] + jnp.dot(
            gpt[:, kk:nq * toks], sg[:, most:toks, cols].reshape(nq * 2 * CH, TILE), preferred_element_type=F32)
        dws[pl.ds(t * per, per)] = p.T.astype(BF).reshape(per, 2, rw, cols_z)
        swap(t).start()

    for i in turns:
        finish(i)

    def deliver(i):
        t = lax.rem(first_part + i, parts)
        swap(t).wait_recv()
        for e in range(per):
            zz = t * per + e
            dwo[zz] = (dws[zz, c].astype(F32) + dwp[zz].astype(F32)).astype(BF)

            @pl.when(zz != z)
            def _(zz=zz):
                pltpu.make_async_remote_copy(
                    src_ref=dwo.at[zz], dst_ref=og.at[z], send_sem=tail_s.at[1], recv_sem=tail_r.at[1],
                    device_id=device(y, zz, c), device_id_type=MESH).start()

    for i in turns:
        deliver(i)
    store_own = load(dwo.at[z], og.at[z], 0)

    gain_all = pltpu.make_async_remote_copy(
        src_ref=gng.at[pl.ds(0, nq - 1)], dst_ref=gng.at[pl.ds(0, nq - 1)], send_sem=tail_s.at[2],
        recv_sem=tail_r.at[2], device_id=other, device_id_type=MESH)
    gain_all.wait()
    gnl[...] = jnp.sum(gng[...], axis=0)
    gain_copy = pltpu.make_async_remote_copy(
        src_ref=gnl, dst_ref=gnp, send_sem=tail_s.at[0], recv_sem=tail_r.at[0], device_id=other, device_id_type=MESH)
    gain_copy.start()

    near = sum(size for g, (_, size) in enumerate(groups) if g not in direct)
    both = toks - near

    @pl.when(encoder)
    def _():
        left(gpg.at[pl.ds(0, (near * (nz - 1) + both * (nq - 1)) // toks)], late_s.at[0], other)
        left(gpg.at[pl.ds(0, near * nz // toks)], pass_s.at[0], other)

    @pl.when(decoder)
    def _():
        left(gpg.at[pl.ds(0, nz - 1)], late_s.at[0], other)
        left(gpg.at[pl.ds(0, nz)], pass_s.at[0], other)

    @pl.when((s > 0) & (s != half))
    def _():
        left(gin_ref, g_s.at[0], other)

    @pl.when(decoder)
    def _():
        left(tsend, t_s.at[0], other)

    sag.sent()

    @pl.when(decoder)
    def _():
        wag.sent()
        relay.sent(False)

    @pl.when(encoder)
    def _():
        relay.sent(True)

    left(dwp, swap_s.at[0], other)
    store_gin.wait()
    gain_copy.wait()
    gains = jnp.sum(gnl[...] + gnp[...], axis=0, keepdims=True) * (1.0 / n_dp)
    gg_ref[...] = jnp.where(c == 0, gains[:, 0:rw], gains[:, rw:2 * rw])

    whole = pltpu.make_async_remote_copy(
        src_ref=dwo.at[pl.ds(0, nz - 1)], dst_ref=og.at[pl.ds(0, nz - 1)], send_sem=tail_s.at[1],
        recv_sem=tail_r.at[1], device_id=other, device_id_type=MESH)
    store_own.wait()
    whole.wait()


def publish_kernel(n_dp, gin_ref, blocks_ref, gain_ref, gin_out, dw_out, gain_out):
    gin_out[...] = gin_ref[...]
    nz, _, cols_z = blocks_ref.shape
    for zz in range(nz):
        dw_out[:, zz * cols_z:(zz + 1) * cols_z] = blocks_ref[zz].astype(F32) * (1.0 / n_dp)
    gain_out[...] = gain_ref[...]


def local(section_inputs, section_weights, memory_weights, norm_gains, memory, cotangent, lengths):
    n_sec, n_dp = lax.axis_size("section"), lax.axis_size("dp")
    toks, feats = section_inputs.shape[1:]
    rw = memory_weights.shape[1]
    nq = n_dp // 2
    nz = nq // 2
    n_ch = toks // CH
    vmem = pl.BlockSpec(memory_space=pltpu.VMEM)
    hbm = pl.BlockSpec(memory_space=pl.ANY)
    square = pltpu.VMEM((feats, feats), BF)
    wide = pltpu.VMEM((toks, feats), F32)
    narrow = pltpu.VMEM((toks, feats), BF)
    cols_z = feats // nz
    blocks = pltpu.VMEM((nz, rw, cols_z), BF)
    dma = pltpu.SemaphoreType.DMA
    gin, dw, gg = pl.pallas_call(
        functools.partial(relay_kernel, n_sec, n_dp),
        out_shape=(
            jax.ShapeDtypeStruct((toks, feats), BF),
            jax.ShapeDtypeStruct((nz, rw, cols_z), BF),
            jax.ShapeDtypeStruct((1, rw), F32),
        ),
        in_specs=[hbm, hbm, hbm, vmem, hbm, hbm, pl.BlockSpec(memory_space=pltpu.SMEM)],
        out_specs=(hbm, hbm, vmem),
        scratch_shapes=[
            narrow, narrow, narrow, narrow,
            square, square, square, square, narrow,
            pltpu.VMEM((nq, toks, feats // 2), BF),
            wide, wide, wide, wide,
            pltpu.VMEM((cols_z, feats // 2), F32),
            pltpu.VMEM((toks, 128), F32),
            narrow, narrow, narrow,
            narrow,
            pltpu.VMEM((CH, feats), F32),
            pltpu.VMEM((CH, feats), F32),
            pltpu.VMEM((CH, feats), F32),
            pltpu.VMEM((nq, toks, cols_z), BF),
            pltpu.VMEM((cols_z, nq * toks), BF),
            pltpu.VMEM((nz, 2, rw, cols_z), BF),
            blocks, blocks,
            pltpu.VMEM((nq, 8, 128), F32),
            pltpu.VMEM((nq, 8, 128), F32),
            pltpu.VMEM((8, 128), F32),
            pltpu.VMEM((8, 128), F32),
            dma((6,)),
            dma((1,)), dma((Gather.count(nz),)),
            dma((1,)), dma((Relay.count(nz),)),
            dma((1,)), dma((HalfGather.count(nz),)),
            dma((1,)), dma((n_ch,)), dma((1,)), dma((n_ch,)),
            dma((1,)), dma((5,)),
            dma((1,)), dma((5,)),
            dma((1,)), dma((feats // 2 // TILE,)),
            dma((3,)), dma((3,)),
        ],
        compiler_params=pltpu.CompilerParams(
            collective_id=0, has_side_effects=True, vmem_limit_bytes=60 * 1024 * 1024
        ),
    )(
        section_inputs[0], section_weights[0], memory_weights[0], norm_gains, memory, cotangent,
        lengths,
    )
    gin, dw, gg = pl.pallas_call(
        functools.partial(publish_kernel, n_dp),
        out_shape=(
            jax.ShapeDtypeStruct((toks, feats), BF),
            jax.ShapeDtypeStruct((rw, feats), F32),
            jax.ShapeDtypeStruct((1, rw), F32),
        ),
        in_specs=[vmem] * 3,
        out_specs=(vmem,) * 3,
    )(gin, dw, gg)
    return gin[None], dw[None], gg


def solution(mesh):
    return jax.shard_map(
        local,
        mesh=mesh,
        in_specs=(
            P("section", "dp", None),
            P("section", None, None),
            P("section", "dp", None),
            P("section", None),
            P("dp", None),
            P("dp", None),
            P("dp"),
        ),
        out_specs=(P("section", "dp", None), P("section", "dp", None), P("section", "dp")),
        check_vma=False,
    )
```

```python
import functools

import jax
import jax.numpy as jnp
from jax import lax
from jax.experimental import pallas as pl
from jax.experimental.pallas import tpu as pltpu
from jax.sharding import PartitionSpec as P

epsilon = 1e-06
BF = jnp.bfloat16
F32 = jnp.float32
CH = 16
TILE = 256


def arrived(ref, sem, dev):
    pltpu.make_async_remote_copy(
        src_ref=ref, dst_ref=ref, send_sem=sem, recv_sem=sem, device_id=dev,
        device_id_type=pl.DeviceIdType.MESH).wait_recv()


def left(ref, sem, dev):
    pltpu.make_async_remote_copy(
        src_ref=ref, dst_ref=ref, send_sem=sem, recv_sem=sem, device_id=dev,
        device_id_type=pl.DeviceIdType.MESH).wait_send()


class Gather:
    def __init__(self, buf, rows, place, send_sem, recv_sems, lane=None):
        self.buf, self.rows, self.place = buf, rows, place
        self.y, self.z, self.c, self.nz, self.device = place
        self.lane = self.c if lane is None else lane
        self.far = self.nz // 2
        self.ss, self.rs = send_sem, recv_sems
        self.mate = self.device(self.y, self.z, 1 - self.c)

    @staticmethod
    def count(nz):
        return 5 * (nz // 2) + 3

    def block(self, q, start, size):
        return self.buf.at[pl.ds(pl.multiple_of((q * 2 + self.lane) * self.rows + start, 16), size)]

    def copy(self, q, start, size, ident, dev):
        ref = self.block(q, start, size)
        return pltpu.make_async_remote_copy(
            src_ref=ref, dst_ref=ref, send_sem=self.ss.at[0], recv_sem=self.rs.at[ident],
            device_id=dev, device_id_type=pl.DeviceIdType.MESH)

    def await_rows(self, rows, ident):
        arrived(self.buf.at[pl.ds(0, rows)], self.rs.at[ident], self.mate)

    def turn(self, z):
        return lax.rem(z + 2 * self.nz, self.nz)

    def source(self, way, d):
        return self.turn(self.z - (1 - 2 * way) * d)

    def ways(self, d, m=0):
        return (0,) if d == 0 or (d == self.far and m == 1) else (0, 1)

    def span(self, way, d, m):
        half, quarter = self.rows // 2, self.rows // 4
        if m in (1, 3):
            return (half if m == 1 else half + quarter), quarter
        return (way * quarter, quarter) if d == self.far else (0, half)

    def z_copy(self, way, d, m):
        y = 1 - self.y if m == 2 else self.y
        start, size = self.span(way, d, m)
        dev = self.device(self.y, self.turn(self.z + 1 - 2 * way), self.c)
        return self.copy(y * self.nz + self.source(way, d - 1), start, size, 3 * (d - 1) + m, dev)

    def y_copy(self, way, d):
        start, size = self.span(way, d, 1)
        dev = self.device(1 - self.y, self.z, self.c)
        return self.copy(self.y * self.nz + self.source(way, d), start, size, 3 * self.far + d, dev)

    def first_copy(self):
        dev = self.device(1 - self.y, self.z, self.c)
        return self.copy(self.y * self.nz + self.z, 0, self.rows // 2, 4 * self.far + 1, dev)

    def hand(self, kind, args):
        ident = 4 * self.far + 2
        if kind in ("own", "first"):
            y = self.y if kind == "own" else 1 - self.y
            self.copy(y * self.nz + self.z, 0, self.size(kind, args), ident, self.mate).start()
            return
        way, d, m = args
        start, size = self.span(way, d, 3 if kind == "back" else m)
        y = {"z": 1 - self.y if m == 2 else self.y, "back": 1 - self.y if m else self.y, "y": 1 - self.y}[kind]
        self.copy(y * self.nz + self.source(way, d), start, size, ident + d, self.mate).start()

    def size(self, kind, args):
        if kind in ("own", "first"):
            return self.rows if kind == "own" else self.rows // 2
        way, d, m = args
        return self.span(way, d, 3 if kind == "back" else m)[1]

    def begin(self):
        self.first_copy().start()
        for m in (1, 0):
            for way in (0, 1):
                self.z_copy(way, 1, m).start()
        self.y_copy(0, 0).start()
        self.hand("own", ())

    def begin_other(self):
        self.await_rows(self.rows // 2, 4 * self.far + 1)
        for way in (0, 1):
            self.z_copy(way, 1, 2).start()
        self.hand("first", ())

    def pair_step(self, i):
        d, m = i // 3 + 1, (1, 0, 2)[i % 3]
        self.await_rows(sum(self.span(way, d, m)[1] for way in self.ways(d, m)), 3 * (d - 1) + m)
        if d < self.far:
            for way in self.ways(d + 1, m):
                self.z_copy(way, d + 1, m).start()
        for way in self.ways(d, m):
            if m == 1:
                self.y_copy(way, d).start()
            self.hand("z", (way, d, m))

    def backs(self, d):
        if d == 0:
            return [(0, 0, 1)]
        return [(0, d, 0), (1, d, 1)] if d == self.far else [(way, d, m) for m in (0, 1) for way in (0, 1)]

    def crossed(self, d):
        return [(way, d, 1) for way in self.ways(d, 1)]

    def handed(self, d):
        if d == 0:
            came = [("own", ()), ("first", ())]
        else:
            came = [("z", (way, d, m)) for m in (0, 1, 2) for way in self.ways(d, m)]
        return came + [("back", args) for args in self.backs(d)] + [("y", args) for args in self.crossed(d)]

    def pass_backs(self, d, relay):
        relay.await_back(d)
        for args in self.backs(d):
            self.hand("back", args)
        self.await_rows(sum(self.size("y", args) for args in self.crossed(d)), 3 * self.far + d)
        for args in self.crossed(d):
            self.hand("y", args)

    def collect(self, d):
        self.await_rows(sum(self.size(*h) for h in self.handed(d)), 4 * self.far + 2 + d)

    def sent(self):
        total = self.rows // 2
        for d in range(self.far + 1):
            total += sum(self.size("y", args) for args in self.crossed(d))
            total += sum(self.size(*h) * (2 if h[0] == "z" else 1) for h in self.handed(d))
        left(self.buf.at[pl.ds(0, total)], self.ss.at[0], self.mate)

    def sources(self, d):
        spots = {0: (0,), self.far: (self.far,)}.get(d, (d, -d))
        return [y * self.nz + self.turn(self.z + o) for o in spots for y in (0, 1)]


class Relay:
    def __init__(self, gather, section, half, sems):
        self.g, self.ss, self.rs = gather, *sems
        g = gather
        self.quarter = g.rows // 4
        self.partner = {
            "section": jnp.where(section >= half, section - half, section + half),
            "dp": ((1 - g.y) * g.nz + g.z) * 2 + g.c,
        }

    @staticmethod
    def count(nz):
        return 3 + 3 * (nz // 2)

    def copy(self, y, src, ident, dev):
        g = self.g
        start, size = g.span(0, 1, 3)
        ref = g.block(y * g.nz + src, start, size)
        return pltpu.make_async_remote_copy(
            src_ref=ref, dst_ref=ref, send_sem=self.ss.at[0], recv_sem=self.rs.at[ident],
            device_id=dev, device_id_type=pl.DeviceIdType.MESH)

    def await_quarters(self, number, ident):
        arrived(self.g.buf.at[pl.ds(0, number * self.quarter)], self.rs.at[ident], self.partner)

    def await_back(self, d):
        self.await_quarters(len(self.g.backs(d)), 2 + 2 * self.g.far + d)

    def up(self):
        return self.copy(self.g.y, self.g.z, 0, self.partner)

    def ring(self, way, d, m):
        g = self.g
        dev = g.device(g.y, g.turn(g.z + 1 - 2 * way), g.c)
        return self.copy(g.y if m else 1 - g.y, g.source(way, d - 1), 2 + 2 * (d - 1) + m, dev)

    def back(self, way, d, m):
        g = self.g
        return self.copy(g.y if m else 1 - g.y, g.source(way, d), 2 + 2 * g.far + d, self.partner)

    def begin(self):
        g = self.g
        self.await_quarters(1, 0)
        self.copy(1 - g.y, g.z, 1, g.device(1 - g.y, g.z, g.c)).start()
        for way in (0, 1):
            self.ring(way, 1, 0).start()

    def begin_other(self):
        self.await_quarters(1, 1)
        for way in (0, 1):
            self.ring(way, 1, 1).start()
        self.back(0, 0, 1).start()

    def step(self, d, m):
        g = self.g
        came = [args for args in g.backs(d) if args[2] == m]
        self.await_quarters(len(came), 2 + 2 * (d - 1) + m)
        for way, _, _ in came:
            if d < g.far and (way, d + 1, m) in g.backs(d + 1):
                self.ring(way, d + 1, m).start()
            self.back(way, d, m).start()

    def sent(self, encoder):
        number = 2 + 2 * sum(len(self.g.backs(d)) for d in range(1, self.g.far + 1)) if encoder else 1
        left(self.g.buf.at[pl.ds(0, number * self.quarter)], self.ss.at[0], self.partner)


class HalfGather:
    def __init__(self, buf, place, send_sem, recv_sems):
        self.buf, self.ss, self.rs = buf, send_sem, recv_sems
        self.y, self.z, self.c, self.nz, self.device = place
        self.far = self.nz // 2
        self.rows = buf.shape[1]
        self.mate = self.device(self.y, self.z, 1 - self.c)

    @staticmethod
    def count(nz):
        return 1 + 2 * (nz // 2)

    def turn(self, z):
        return lax.rem(z + 2 * self.nz, self.nz)

    def cross(self, src):
        return pltpu.make_async_remote_copy(
            src_ref=src, dst_ref=self.buf.at[self.y * self.nz + self.z], send_sem=self.ss.at[0],
            recv_sem=self.rs.at[0], device_id=self.device(1 - self.y, self.z, self.c),
            device_id_type=pl.DeviceIdType.MESH)

    def z_copy(self, way, d, m):
        sign = 1 - 2 * way
        src = self.turn(self.z - sign * (d - 1))
        y = 1 - self.y if m else self.y
        size = self.rows // 2 if d == self.far else self.rows
        ref = self.buf.at[y * self.nz + src, pl.ds(way * size if d == self.far else 0, size)]
        return pltpu.make_async_remote_copy(
            src_ref=ref, dst_ref=ref, send_sem=self.ss.at[0], recv_sem=self.rs.at[1 + 2 * (d - 1) + m],
            device_id=self.device(self.y, self.turn(self.z + sign), self.c), device_id_type=pl.DeviceIdType.MESH)

    def begin(self):
        for way in (0, 1):
            self.z_copy(way, 1, 0).start()

    def begin_other(self):
        arrived(self.buf.at[0], self.rs.at[0], self.mate)
        for way in (0, 1):
            self.z_copy(way, 1, 1).start()

    def pair_step(self, i):
        d, m = i // 2 + 1, i % 2
        arrived(self.buf.at[pl.ds(0, 1 if d == self.far else 2)], self.rs.at[1 + i], self.mate)
        if d < self.far:
            for way in (0, 1):
                self.z_copy(way, d + 1, m).start()

    def sent(self):
        left(self.buf.at[pl.ds(0, 2 * self.nz - 1)], self.ss.at[0], self.mate)


def relay_kernel(n_sec, n_dp,
                 x_hbm, w_hbm, mw_hbm, gain_ref, mem_hbm, cot_hbm, len_ref,
                 gin_hbm, og, gg_ref,
                 x_ref, mem_ref, cot_ref, gin_ref,
                 wv, wt, mwv, mwt, sc, sg, normed, slope, act, gate, dwt, inv, gbuf, tbuf, tsend,
                 gpv, gacc, gs, ts, gpg, gpt, dws, dwp, dwo, gnv, gng, gnl, gnp,
                 load_sem, wag_s, wag_r, rel_s, rel_r, sag_s, sag_r, g_s, g_r, t_s, t_r, late_s, late_r, pass_s, pass_r, swap_s, swap_r,
                 tail_s, tail_r):
    s = lax.axis_index("section")
    j = lax.axis_index("dp")
    half = n_sec // 2
    nq = n_dp // 2
    nz = nq // 2
    c = lax.rem(j, 2)
    q0 = j // 2
    y, z = q0 // nz, lax.rem(q0, nz)
    toks, feats = x_ref.shape
    rw = mw_hbm.shape[0]
    n_ch = toks // CH
    tiles = feats // TILE
    decoder = s >= half
    encoder = s < half
    above = n_sec - 1 - s
    MESH = pl.DeviceIdType.MESH

    def device(yy, zz, cc):
        return {"dp": (yy * nz + zz) * 2 + cc}

    def load(src, dst, i):
        copy = pltpu.make_async_copy(src, dst, load_sem.at[i])
        copy.start()
        return copy

    barrier = pltpu.get_barrier_semaphore()

    def greet(i, carry):
        q = lax.rem(q0 + i, nq)
        pl.semaphore_signal(barrier, inc=1, device_id={"dp": q * 2 + c}, device_id_type=MESH)
        return carry

    lax.fori_loop(1, nq, greet, 0)
    pl.semaphore_signal(barrier, inc=1, device_id={"dp": q0 * 2 + 1 - c}, device_id_type=MESH)

    @pl.when(s > 0)
    def _():
        pl.semaphore_signal(barrier, inc=1, device_id={"section": s - 1}, device_id_type=MESH)

    @pl.when(s < n_sec - 1)
    def _():
        pl.semaphore_signal(barrier, inc=1, device_id={"section": s + 1}, device_id_type=MESH)

    load_m = pltpu.make_async_copy(
        mw_hbm, mwv.at[pl.ds(pl.multiple_of(j * rw, rw), rw)], load_sem.at[1])

    @pl.when(decoder)
    def _():
        load_m.start()

    load_x = load(x_hbm, x_ref, 2)
    load_w = load(w_hbm, wv, 0)
    load_mem = load(mem_hbm, mem_ref, 3)
    load_cot = load(cot_hbm, cot_ref, 4)

    pl.semaphore_signal(
        barrier, inc=1, device_id={"section": lax.rem(s + half, n_sec), "dp": ((1 - y) * nz + z) * 2 + c},
        device_id_type=MESH)
    ends = (s == 0) | (s == n_sec - 1)
    pl.semaphore_wait(barrier, nq + jnp.where(ends, 2, 3))

    place = (y, z, c, nz, device)

    wag = Gather(mwv, rw, place, wag_s, wag_r)
    relay = Relay(wag, s, half, (rel_s, rel_r))
    sag = HalfGather(sg, place, sag_s, sag_r)
    far = wag.far
    last_pair = 2 * far
    width = feats // 2
    cols_z = feats // nz
    mine, theirs = (pl.ds(pl.multiple_of(v * width, width), width) for v in (y, 1 - y))
    crossing = sc.at[:, theirs]
    mine_z = pl.ds(pl.multiple_of(z * cols_z, cols_z), cols_z)

    @pl.when(decoder)
    def _():
        load_m.wait()
        relay.up().start()
        wag.begin()

    def rows_of(k):
        return pl.ds(pl.multiple_of(k * CH, CH), CH)

    def norm_rows(k, carry):
        rows = rows_of(k)
        wide = x_ref[rows, :].astype(F32)
        scale = lax.rsqrt(jnp.mean(wide * wide, axis=1, keepdims=True) + epsilon)
        inv[rows, :] = jnp.broadcast_to(scale, (CH, 128))
        value = wide * scale
        normed[rows, :] = value
        sc[rows, :] = (value * gain_ref[...]).astype(BF)
        sg[q0, rows, :] = sc[rows, mine]
        return carry

    load_x.wait()
    lax.fori_loop(0, n_ch, norm_rows, 0)

    @pl.when(encoder)
    def _():
        sag.cross(crossing).start()
        relay.begin()
        relay.step(1, 0)
        relay.begin_other()
        for d in range(2, far + 1):
            relay.step(d, 0)
            relay.step(d - 1, 1)
        relay.step(far, 1)
        sag.begin()
        sag.begin_other()

    load_w.wait()

    def cols_of(t):
        return pl.ds(pl.multiple_of(t * TILE, TILE), TILE)

    def preact_tile(t, carry):
        cols = cols_of(t)
        p = jnp.dot(sc[...], wv[:, cols], preferred_element_type=F32)
        sig = jax.nn.sigmoid(p)
        act[:, cols] = p * sig
        slope[:, cols] = sig * (1.0 + p * (1.0 - sig))
        return carry

    lax.fori_loop(0, tiles, preact_tile, 0)
    load_mem.wait()
    load_cot.wait()

    def turn_w(piece, pieces):
        def body(i, carry):
            a, b = i // tiles, lax.rem(i, tiles)
            wt[cols_of(b), cols_of(a)] = wv[cols_of(a), cols_of(b)].T
            return carry

        size = tiles * tiles // pieces
        lax.fori_loop(piece * size, (piece + 1) * size, body, 0, unroll=4)

    def chip_rows(q):
        return pl.ds(pl.multiple_of(q * 2 * rw, 2 * rw), 2 * rw)

    def turn_m(d):
        spots = [chip_rows(q) for q in wag.sources(d)]

        def body(t, carry):
            for at in spots:
                mwt[cols_of(t), at] = mwv[at, cols_of(t)].T
            return carry

        lax.fori_loop(0, tiles, body, 0, unroll=2)

    def gate_part(d):
        spots = [chip_rows(q) for q in wag.sources(d)]
        left = jnp.concatenate([mem_ref[:, at] for at in spots], axis=1)

        def body(t, carry):
            cols = cols_of(t)
            right = jnp.concatenate([mwv[at, cols] for at in spots], axis=0)
            p = jnp.dot(left, right, preferred_element_type=F32)
            if d == 0:
                gate[:, cols] = p
            elif d < far:
                gate[:, cols] += p
            else:
                slope[:, cols] = slope[:, cols] * (gate[:, cols] + p)
            return carry

        lax.fori_loop(0, tiles, body, 0, unroll=4)

    @pl.when(decoder)
    def _():
        wag.begin_other()
        wag.pair_step(0)
        turn_w(0, 4)
        wag.pair_step(1)
        turn_w(1, 4)
        wag.pair_step(2)
        turn_w(2, 4)
        wag.pair_step(3)
        turn_w(3, 4)
        wag.pair_step(4)
        wag.pass_backs(0, relay)
        wag.pair_step(5)
        sag.cross(crossing).start()
        wag.collect(0)
        gate_part(0)
        turn_m(0)
        wag.pair_step(6)
        wag.pass_backs(1, relay)
        wag.pair_step(7)
        wag.collect(1)
        gate_part(1)
        wag.pair_step(8)
        turn_m(1)
        wag.pass_backs(2, relay)
        wag.pair_step(9)
        wag.collect(2)
        gate_part(2)
        wag.pair_step(10)
        turn_m(2)
        wag.pair_step(11)
        wag.pass_backs(3, relay)
        wag.pass_backs(4, relay)
        wag.collect(3)
        gate_part(3)
        turn_m(3)
        wag.collect(4)
        gate_part(4)
        sag.begin()
        turn_m(4)

        @pl.when(above >= 2)
        def _():
            sag.begin_other()
            sag.pair_step(0)

        @pl.when(above >= 3)
        def _():
            sag.pair_step(1)

    @pl.when(encoder)
    def _():
        for piece in range(4):
            turn_w(piece, 4)
        for i in range(last_pair - 2):
            sag.pair_step(i)

    @pl.when(s == n_sec - 1)
    def _():
        live = lax.broadcasted_iota(jnp.int32, (toks, TILE), 0) < len_ref[0]

        def body(t, carry):
            cols = cols_of(t)
            gbuf[:, cols] = jnp.where(live, cot_ref[:, cols], jnp.zeros((), BF))
            return carry

        lax.fori_loop(0, tiles, body, 0)

    gacc[...] = jnp.zeros_like(gacc)

    def down(src, dst, k, send_sems, recv_sems):
        rows = rows_of(k)
        return pltpu.make_async_remote_copy(
            src_ref=src.at[rows], dst_ref=dst.at[rows], send_sem=send_sems.at[0], recv_sem=recv_sems.at[k],
            device_id={"section": s - 1}, device_id_type=MESH)

    groups = [(0, 3 * CH), (3 * CH, 2 * CH), (5 * CH, CH), (6 * CH, CH), (7 * CH, CH)]
    direct = (2, 3, 4)
    round_z = [nz // 2] + [v for i in range(nz // 2 - 1, 0, -1) for v in (i, nz - i)]

    def late_send(g):
        start, size = groups[g]
        rows = pl.ds(start, size)

        def send(yy, zz):
            pltpu.make_async_remote_copy(
                src_ref=gpv.at[rows, pl.ds(pl.multiple_of(zz * cols_z, cols_z), cols_z)], dst_ref=gpg.at[q0, rows],
                send_sem=late_s.at[0], recv_sem=late_r.at[g], device_id=device(yy, zz, c), device_id_type=MESH).start()

        for i in round_z:
            send(y, lax.rem(z + i, nz))
        if g in direct:
            @pl.when(encoder)
            def _():
                for i in round_z + [0]:
                    send(1 - y, lax.rem(z + i, nz))

    def late_done(g, count):
        start, size = groups[g]
        ref = gpg.at[pl.ds(0, count), pl.ds(start, size)]
        return pltpu.make_async_remote_copy(
            src_ref=ref, dst_ref=ref, send_sem=late_s.at[0], recv_sem=late_r.at[g],
            device_id={"dp": q0 * 2 + 1 - c}, device_id_type=MESH)

    def late_recv(g):
        if g not in direct:
            late_done(g, nz - 1).wait_recv()
            return

        @pl.when(encoder)
        def _():
            late_done(g, nq - 1).wait_recv()

        @pl.when(decoder)
        def _():
            late_done(g, nz - 1).wait_recv()

    def late_pass(g):
        start, size = groups[g]
        ref = gpg.at[pl.ds(pl.multiple_of(y * nz, nz), nz), pl.ds(start, size)]
        return pltpu.make_async_remote_copy(
            src_ref=ref, dst_ref=ref, send_sem=pass_s.at[0], recv_sem=pass_r.at[g],
            device_id=device(1 - y, z, c), device_id_type=MESH)

    def term(k):
        rows = rows_of(k)
        up = gbuf[rows, :].astype(F32)
        grad_gate = (up * act[rows, :]).astype(BF)
        for t in range(tiles):
            cols = slice(t * TILE, (t + 1) * TILE)
            ts[:, cols] = jnp.dot(grad_gate, mwt[:, cols], preferred_element_type=F32)

        @pl.when(s < n_sec - 1)
        def _():
            down(tsend, tbuf, k, t_s, t_r).wait_recv()
            tsend[rows, :] = (ts[...] + tbuf[rows, :].astype(F32)).astype(BF)

        @pl.when(s == n_sec - 1)
        def _():
            tsend[rows, :] = ts[...].astype(BF)

    passing = [(0, 3, 0), (0, 7, 1), (1, 1, 0), (1, 3, 1), (1, 6, 2), (2, 1, 1), (2, 4, 2), (2, 6, 3),
               (3, 1, 2), (3, 4, 3), (3, 6, 4)]

    def own_rows(g):
        rows = pl.ds(groups[g][0], groups[g][1])
        gpg[q0, rows, :] = gpv[rows, mine_z]

    def chunk(k, carry):
        rows = rows_of(k)

        @pl.when(s < n_sec - 1)
        def _():
            down(gin_ref, gbuf, k, g_s, g_r).wait_recv()

        @pl.when(s == half)
        def _():
            term(k)
            down(tsend, gbuf, k, t_s, g_r).start()

        gpv[rows, :] = (gbuf[rows, :].astype(F32) * slope[rows, :]).astype(BF)
        grad_pre = gpv[rows, :]
        total = jnp.zeros((CH, 128), F32)
        for t in range(tiles):
            cols = slice(t * TILE, (t + 1) * TILE)
            p = jnp.dot(grad_pre, wt[:, cols], preferred_element_type=F32)
            both = p * normed[rows, cols]
            gacc[:, cols] += both
            h = p * gain_ref[:, cols]
            gs[:, cols] = h
            weighted = both * gain_ref[:, cols]
            for i in range(TILE // 128):
                total = total + weighted[:, i * 128:(i + 1) * 128]
        center = jnp.sum(total, axis=1, keepdims=True) * (1.0 / feats)
        scale = inv[rows, 0:1]
        for t in range(tiles):
            cols = slice(t * TILE, (t + 1) * TILE)
            gin_ref[rows, cols] = (
                gbuf[rows, cols].astype(F32) + scale * (gs[:, cols] - normed[rows, cols] * center)
            ).astype(BF)

        @pl.when((s > 0) & (s != half))
        def _():
            down(gin_ref, gbuf, k, g_s, g_r).start()

        @pl.when(s > half)
        def _():
            term(k)
            down(tsend, tbuf, k, t_s, t_r).start()

        @pl.when(encoder)
        def _():
            for g, (start, size) in enumerate(groups[:-1]):
                @pl.when(k == (start + size) // CH - 1)
                def _(g=g):
                    late_send(g)
                    own_rows(g)

            @pl.when(k == 3)
            def _():
                sag.pair_step(last_pair - 2)
                sag.pair_step(last_pair - 1)

            for g, at in ((0, 5), (1, 6)):
                @pl.when(k == at)
                def _(g=g):
                    late_recv(g)
                    late_pass(g).start()

        for up in range(half):
            @pl.when(above == up)
            def _(up=up):
                for at in {0: (2,), 1: (0,)}.get(up, ()):
                    @pl.when(k == at)
                    def _():
                        sag.begin_other()

                for at, i in [(at, i) for v, at, i in passing if v == up]:
                    @pl.when(k == at)
                    def _(i=i):
                        sag.pair_step(i)

        return carry

    lax.fori_loop(0, n_ch, chunk, 0)

    @pl.when(decoder)
    def _():
        for g in range(len(groups) - 1):
            late_send(g)
            own_rows(g)

    late_send(len(groups) - 1)
    part = gacc[...]
    for q in range(nq):
        gnv[q] = part[0:8, q * 128:(q + 1) * 128] + part[8:16, q * 128:(q + 1) * 128]

    def gain_send(i, carry):
        q = lax.rem(q0 + i, nq)
        pltpu.make_async_remote_copy(
            src_ref=gnv.at[q], dst_ref=gng.at[q0], send_sem=tail_s.at[2], recv_sem=tail_r.at[2],
            device_id={"dp": q * 2 + c}, device_id_type=MESH).start()
        return carry

    lax.fori_loop(1, nq, gain_send, 0)
    gng[q0] = gnv[q0]
    store_gin = load(gin_ref, gin_hbm, 5)

    own_rows(len(groups) - 1)

    @pl.when(decoder)
    def _():
        for i in range(2, last_pair):
            @pl.when(i >= 2 + above)
            def _(i=i):
                sag.pair_step(i)

            if 3 <= i:
                late_recv(i - 3)
                late_pass(i - 3).start()
        for g in range(len(groups)):
            late_pass(g).wait_recv()

    @pl.when(encoder)
    def _():
        late_recv(2)
        late_pass(0).wait_recv()
        late_pass(1).wait_recv()

    most = toks - 2 * CH
    kk = nq * most
    parts = width // TILE
    gpt[:, 0:kk] = gpg[:, 0:most, :].reshape(kk, cols_z).T

    def product(t, carry):
        cols = cols_of(t)
        dwt[:, cols] = jnp.dot(gpt[:, 0:kk], sg[:, 0:most, cols].reshape(kk, TILE), preferred_element_type=F32)
        return carry

    lax.fori_loop(0, parts, product, 0, unroll=2)

    @pl.when(encoder)
    def _():
        late_recv(3)
        late_recv(4)

    gpt[:, kk:nq * toks] = gpg[:, most:toks, :].reshape(nq * 2 * CH, cols_z).T

    other = {"dp": q0 * 2 + 1 - c}
    per = TILE // (2 * rw)
    first_part = z // per

    def swap(t):
        spots = pl.ds(t * per, per)
        return pltpu.make_async_remote_copy(
            src_ref=dws.at[spots, 1 - c], dst_ref=dwp.at[spots], send_sem=swap_s.at[0], recv_sem=swap_r.at[t],
            device_id=other, device_id_type=MESH)

    turns = [parts // 2] + [v for i in range(parts // 2 - 1, 0, -1) for v in (i, parts - i)] + [0]

    def finish(i):
        t = lax.rem(first_part + i, parts)
        cols = cols_of(t)
        p = dwt[:, cols] + jnp.dot(
            gpt[:, kk:nq * toks], sg[:, most:toks, cols].reshape(nq * 2 * CH, TILE), preferred_element_type=F32)
        dws[pl.ds(t * per, per)] = p.T.astype(BF).reshape(per, 2, rw, cols_z)
        swap(t).start()

    for i in turns:
        finish(i)

    def deliver(i):
        t = lax.rem(first_part + i, parts)
        swap(t).wait_recv()
        for e in range(per):
            zz = t * per + e
            dwo[zz] = (dws[zz, c].astype(F32) + dwp[zz].astype(F32)).astype(BF)

            @pl.when(zz != z)
            def _(zz=zz):
                pltpu.make_async_remote_copy(
                    src_ref=dwo.at[zz], dst_ref=og.at[z], send_sem=tail_s.at[1], recv_sem=tail_r.at[1],
                    device_id=device(y, zz, c), device_id_type=MESH).start()

    for i in turns:
        deliver(i)
    store_own = load(dwo.at[z], og.at[z], 0)

    gain_all = pltpu.make_async_remote_copy(
        src_ref=gng.at[pl.ds(0, nq - 1)], dst_ref=gng.at[pl.ds(0, nq - 1)], send_sem=tail_s.at[2],
        recv_sem=tail_r.at[2], device_id=other, device_id_type=MESH)
    gain_all.wait()
    gnl[...] = jnp.sum(gng[...], axis=0)
    gain_copy = pltpu.make_async_remote_copy(
        src_ref=gnl, dst_ref=gnp, send_sem=tail_s.at[0], recv_sem=tail_r.at[0], device_id=other, device_id_type=MESH)
    gain_copy.start()

    near = sum(size for g, (_, size) in enumerate(groups) if g not in direct)
    both = toks - near

    @pl.when(encoder)
    def _():
        left(gpg.at[pl.ds(0, (near * (nz - 1) + both * (nq - 1)) // toks)], late_s.at[0], other)
        left(gpg.at[pl.ds(0, near * nz // toks)], pass_s.at[0], other)

    @pl.when(decoder)
    def _():
        left(gpg.at[pl.ds(0, nz - 1)], late_s.at[0], other)
        left(gpg.at[pl.ds(0, nz)], pass_s.at[0], other)

    @pl.when((s > 0) & (s != half))
    def _():
        left(gin_ref, g_s.at[0], other)

    @pl.when(decoder)
    def _():
        left(tsend, t_s.at[0], other)

    sag.sent()

    @pl.when(decoder)
    def _():
        wag.sent()
        relay.sent(False)

    @pl.when(encoder)
    def _():
        relay.sent(True)

    left(dwp, swap_s.at[0], other)
    store_gin.wait()
    gain_copy.wait()
    gains = jnp.sum(gnl[...] + gnp[...], axis=0, keepdims=True) * (1.0 / n_dp)
    gg_ref[...] = jnp.where(c == 0, gains[:, 0:rw], gains[:, rw:2 * rw])

    whole = pltpu.make_async_remote_copy(
        src_ref=dwo.at[pl.ds(0, nz - 1)], dst_ref=og.at[pl.ds(0, nz - 1)], send_sem=tail_s.at[1],
        recv_sem=tail_r.at[1], device_id=other, device_id_type=MESH)
    store_own.wait()
    whole.wait()


def publish_kernel(n_dp, gin_ref, blocks_ref, gain_ref, gin_out, dw_out, gain_out):
    gin_out[...] = gin_ref[...]
    nz, _, cols_z = blocks_ref.shape
    for zz in range(nz):
        dw_out[:, zz * cols_z:(zz + 1) * cols_z] = blocks_ref[zz].astype(F32) * (1.0 / n_dp)
    gain_out[...] = gain_ref[...]


def local(section_inputs, section_weights, memory_weights, norm_gains, memory, cotangent, lengths):
    n_sec, n_dp = lax.axis_size("section"), lax.axis_size("dp")
    toks, feats = section_inputs.shape[1:]
    rw = memory_weights.shape[1]
    nq = n_dp // 2
    nz = nq // 2
    n_ch = toks // CH
    vmem = pl.BlockSpec(memory_space=pltpu.VMEM)
    hbm = pl.BlockSpec(memory_space=pl.ANY)
    square = pltpu.VMEM((feats, feats), BF)
    wide = pltpu.VMEM((toks, feats), F32)
    narrow = pltpu.VMEM((toks, feats), BF)
    cols_z = feats // nz
    blocks = pltpu.VMEM((nz, rw, cols_z), BF)
    dma = pltpu.SemaphoreType.DMA
    gin, dw, gg = pl.pallas_call(
        functools.partial(relay_kernel, n_sec, n_dp),
        out_shape=(
            jax.ShapeDtypeStruct((toks, feats), BF),
            jax.ShapeDtypeStruct((nz, rw, cols_z), BF),
            jax.ShapeDtypeStruct((1, rw), F32),
        ),
        in_specs=[hbm, hbm, hbm, vmem, hbm, hbm, pl.BlockSpec(memory_space=pltpu.SMEM)],
        out_specs=(hbm, hbm, vmem),
        scratch_shapes=[
            narrow, narrow, narrow, narrow,
            square, square, square, square, narrow,
            pltpu.VMEM((nq, toks, feats // 2), BF),
            wide, wide, wide, wide,
            pltpu.VMEM((cols_z, feats // 2), F32),
            pltpu.VMEM((toks, 128), F32),
            narrow, narrow, narrow,
            narrow,
            pltpu.VMEM((CH, feats), F32),
            pltpu.VMEM((CH, feats), F32),
            pltpu.VMEM((CH, feats), F32),
            pltpu.VMEM((nq, toks, cols_z), BF),
            pltpu.VMEM((cols_z, nq * toks), BF),
            pltpu.VMEM((nz, 2, rw, cols_z), BF),
            blocks, blocks,
            pltpu.VMEM((nq, 8, 128), F32),
            pltpu.VMEM((nq, 8, 128), F32),
            pltpu.VMEM((8, 128), F32),
            pltpu.VMEM((8, 128), F32),
            dma((6,)),
            dma((1,)), dma((Gather.count(nz),)),
            dma((1,)), dma((Relay.count(nz),)),
            dma((1,)), dma((HalfGather.count(nz),)),
            dma((1,)), dma((n_ch,)), dma((1,)), dma((n_ch,)),
            dma((1,)), dma((5,)),
            dma((1,)), dma((5,)),
            dma((1,)), dma((feats // 2 // TILE,)),
            dma((3,)), dma((3,)),
        ],
        compiler_params=pltpu.CompilerParams(
            collective_id=0, has_side_effects=True, vmem_limit_bytes=60 * 1024 * 1024
        ),
    )(
        section_inputs[0], section_weights[0], memory_weights[0], norm_gains, memory, cotangent,
        lengths,
    )
    gin, dw, gg = pl.pallas_call(
        functools.partial(publish_kernel, n_dp),
        out_shape=(
            jax.ShapeDtypeStruct((toks, feats), BF),
            jax.ShapeDtypeStruct((rw, feats), F32),
            jax.ShapeDtypeStruct((1, rw), F32),
        ),
        in_specs=[vmem] * 3,
        out_specs=(vmem,) * 3,
    )(gin, dw, gg)
    return gin[None], dw[None], gg


def solution(mesh):
    return jax.shard_map(
        local,
        mesh=mesh,
        in_specs=(
            P("section", "dp", None),
            P("section", None, None),
            P("section", "dp", None),
            P("section", None),
            P("dp", None),
            P("dp", None),
            P("dp"),
        ),
        out_specs=(P("section", "dp", None), P("section", "dp", None), P("section", "dp")),
        check_vma=False,
    )
```

```python
import functools

import jax
import jax.numpy as jnp
from jax import lax
from jax.experimental import pallas as pl
from jax.experimental.pallas import tpu as pltpu
from jax.sharding import PartitionSpec as P

epsilon = 1e-06
BF = jnp.bfloat16
F32 = jnp.float32
CH = 16
TILE = 256


def arrived(ref, sem, dev):
    pltpu.make_async_remote_copy(
        src_ref=ref, dst_ref=ref, send_sem=sem, recv_sem=sem, device_id=dev,
        device_id_type=pl.DeviceIdType.MESH).wait_recv()


def left(ref, sem, dev):
    pltpu.make_async_remote_copy(
        src_ref=ref, dst_ref=ref, send_sem=sem, recv_sem=sem, device_id=dev,
        device_id_type=pl.DeviceIdType.MESH).wait_send()


class Gather:
    def __init__(self, buf, rows, place, send_sem, recv_sems, lane=None):
        self.buf, self.rows, self.place = buf, rows, place
        self.y, self.z, self.c, self.nz, self.device = place
        self.lane = self.c if lane is None else lane
        self.far = self.nz // 2
        self.ss, self.rs = send_sem, recv_sems
        self.mate = self.device(self.y, self.z, 1 - self.c)

    @staticmethod
    def count(nz):
        return 5 * (nz // 2) + 3

    def block(self, q, start, size):
        return self.buf.at[pl.ds(pl.multiple_of((q * 2 + self.lane) * self.rows + start, 16), size)]

    def copy(self, q, start, size, ident, dev):
        ref = self.block(q, start, size)
        return pltpu.make_async_remote_copy(
            src_ref=ref, dst_ref=ref, send_sem=self.ss.at[0], recv_sem=self.rs.at[ident],
            device_id=dev, device_id_type=pl.DeviceIdType.MESH)

    def await_rows(self, rows, ident):
        arrived(self.buf.at[pl.ds(0, rows)], self.rs.at[ident], self.mate)

    def turn(self, z):
        return lax.rem(z + 2 * self.nz, self.nz)

    def source(self, way, d):
        return self.turn(self.z - (1 - 2 * way) * d)

    def ways(self, d, m=0):
        return (0,) if d == 0 or (d == self.far and m == 1) else (0, 1)

    def span(self, way, d, m):
        half, quarter = self.rows // 2, self.rows // 4
        if m in (1, 3):
            return (half if m == 1 else half + quarter), quarter
        return (way * quarter, quarter) if d == self.far else (0, half)

    def z_copy(self, way, d, m):
        y = 1 - self.y if m == 2 else self.y
        start, size = self.span(way, d, m)
        dev = self.device(self.y, self.turn(self.z + 1 - 2 * way), self.c)
        return self.copy(y * self.nz + self.source(way, d - 1), start, size, 3 * (d - 1) + m, dev)

    def y_copy(self, way, d):
        start, size = self.span(way, d, 1)
        dev = self.device(1 - self.y, self.z, self.c)
        return self.copy(self.y * self.nz + self.source(way, d), start, size, 3 * self.far + d, dev)

    def first_copy(self):
        dev = self.device(1 - self.y, self.z, self.c)
        return self.copy(self.y * self.nz + self.z, 0, self.rows // 2, 4 * self.far + 1, dev)

    def hand(self, kind, args):
        ident = 4 * self.far + 2
        if kind in ("own", "first"):
            y = self.y if kind == "own" else 1 - self.y
            self.copy(y * self.nz + self.z, 0, self.size(kind, args), ident, self.mate).start()
            return
        way, d, m = args
        start, size = self.span(way, d, 3 if kind == "back" else m)
        y = {"z": 1 - self.y if m == 2 else self.y, "back": 1 - self.y if m else self.y, "y": 1 - self.y}[kind]
        self.copy(y * self.nz + self.source(way, d), start, size, ident + d, self.mate).start()

    def size(self, kind, args):
        if kind in ("own", "first"):
            return self.rows if kind == "own" else self.rows // 2
        way, d, m = args
        return self.span(way, d, 3 if kind == "back" else m)[1]

    def begin(self):
        self.first_copy().start()
        for m in (1, 0):
            for way in (0, 1):
                self.z_copy(way, 1, m).start()
        self.y_copy(0, 0).start()
        self.hand("own", ())

    def begin_other(self):
        self.await_rows(self.rows // 2, 4 * self.far + 1)
        for way in (0, 1):
            self.z_copy(way, 1, 2).start()
        self.hand("first", ())

    def pair_step(self, i):
        d, m = i // 3 + 1, (1, 0, 2)[i % 3]
        self.await_rows(sum(self.span(way, d, m)[1] for way in self.ways(d, m)), 3 * (d - 1) + m)
        if d < self.far:
            for way in self.ways(d + 1, m):
                self.z_copy(way, d + 1, m).start()
        for way in self.ways(d, m):
            if m == 1:
                self.y_copy(way, d).start()
            self.hand("z", (way, d, m))

    def backs(self, d):
        if d == 0:
            return [(0, 0, 1)]
        return [(0, d, 0), (1, d, 1)] if d == self.far else [(way, d, m) for m in (0, 1) for way in (0, 1)]

    def crossed(self, d):
        return [(way, d, 1) for way in self.ways(d, 1)]

    def handed(self, d):
        if d == 0:
            came = [("own", ()), ("first", ())]
        else:
            came = [("z", (way, d, m)) for m in (0, 1, 2) for way in self.ways(d, m)]
        return came + [("back", args) for args in self.backs(d)] + [("y", args) for args in self.crossed(d)]

    def pass_backs(self, d, relay):
        relay.await_back(d)
        for args in self.backs(d):
            self.hand("back", args)
        self.await_rows(sum(self.size("y", args) for args in self.crossed(d)), 3 * self.far + d)
        for args in self.crossed(d):
            self.hand("y", args)

    def collect(self, d):
        self.await_rows(sum(self.size(*h) for h in self.handed(d)), 4 * self.far + 2 + d)

    def sent(self):
        total = self.rows // 2
        for d in range(self.far + 1):
            total += sum(self.size("y", args) for args in self.crossed(d))
            total += sum(self.size(*h) * (2 if h[0] == "z" else 1) for h in self.handed(d))
        left(self.buf.at[pl.ds(0, total)], self.ss.at[0], self.mate)

    def sources(self, d):
        spots = {0: (0,), self.far: (self.far,)}.get(d, (d, -d))
        return [y * self.nz + self.turn(self.z + o) for o in spots for y in (0, 1)]


class Relay:
    def __init__(self, gather, section, half, sems):
        self.g, self.ss, self.rs = gather, *sems
        g = gather
        self.quarter = g.rows // 4
        self.partner = {
            "section": jnp.where(section >= half, section - half, section + half),
            "dp": ((1 - g.y) * g.nz + g.z) * 2 + g.c,
        }

    @staticmethod
    def count(nz):
        return 3 + 3 * (nz // 2)

    def copy(self, y, src, ident, dev):
        g = self.g
        start, size = g.span(0, 1, 3)
        ref = g.block(y * g.nz + src, start, size)
        return pltpu.make_async_remote_copy(
            src_ref=ref, dst_ref=ref, send_sem=self.ss.at[0], recv_sem=self.rs.at[ident],
            device_id=dev, device_id_type=pl.DeviceIdType.MESH)

    def await_quarters(self, number, ident):
        arrived(self.g.buf.at[pl.ds(0, number * self.quarter)], self.rs.at[ident], self.partner)

    def await_back(self, d):
        self.await_quarters(len(self.g.backs(d)), 2 + 2 * self.g.far + d)

    def up(self):
        return self.copy(self.g.y, self.g.z, 0, self.partner)

    def ring(self, way, d, m):
        g = self.g
        dev = g.device(g.y, g.turn(g.z + 1 - 2 * way), g.c)
        return self.copy(g.y if m else 1 - g.y, g.source(way, d - 1), 2 + 2 * (d - 1) + m, dev)

    def back(self, way, d, m):
        g = self.g
        return self.copy(g.y if m else 1 - g.y, g.source(way, d), 2 + 2 * g.far + d, self.partner)

    def begin(self):
        g = self.g
        self.await_quarters(1, 0)
        self.copy(1 - g.y, g.z, 1, g.device(1 - g.y, g.z, g.c)).start()
        for way in (0, 1):
            self.ring(way, 1, 0).start()

    def begin_other(self):
        self.await_quarters(1, 1)
        for way in (0, 1):
            self.ring(way, 1, 1).start()
        self.back(0, 0, 1).start()

    def step(self, d, m):
        g = self.g
        came = [args for args in g.backs(d) if args[2] == m]
        self.await_quarters(len(came), 2 + 2 * (d - 1) + m)
        for way, _, _ in came:
            if d < g.far and (way, d + 1, m) in g.backs(d + 1):
                self.ring(way, d + 1, m).start()
            self.back(way, d, m).start()

    def sent(self, encoder):
        number = 2 + 2 * sum(len(self.g.backs(d)) for d in range(1, self.g.far + 1)) if encoder else 1
        left(self.g.buf.at[pl.ds(0, number * self.quarter)], self.ss.at[0], self.partner)


class HalfGather:
    def __init__(self, buf, place, send_sem, recv_sems):
        self.buf, self.ss, self.rs = buf, send_sem, recv_sems
        self.y, self.z, self.c, self.nz, self.device = place
        self.far = self.nz // 2
        self.rows = buf.shape[1]
        self.mate = self.device(self.y, self.z, 1 - self.c)

    @staticmethod
    def count(nz):
        return 1 + 2 * (nz // 2)

    def turn(self, z):
        return lax.rem(z + 2 * self.nz, self.nz)

    def cross(self, src):
        return pltpu.make_async_remote_copy(
            src_ref=src, dst_ref=self.buf.at[self.y * self.nz + self.z], send_sem=self.ss.at[0],
            recv_sem=self.rs.at[0], device_id=self.device(1 - self.y, self.z, self.c),
            device_id_type=pl.DeviceIdType.MESH)

    def z_copy(self, way, d, m):
        sign = 1 - 2 * way
        src = self.turn(self.z - sign * (d - 1))
        y = 1 - self.y if m else self.y
        size = self.rows // 2 if d == self.far else self.rows
        ref = self.buf.at[y * self.nz + src, pl.ds(way * size if d == self.far else 0, size)]
        return pltpu.make_async_remote_copy(
            src_ref=ref, dst_ref=ref, send_sem=self.ss.at[0], recv_sem=self.rs.at[1 + 2 * (d - 1) + m],
            device_id=self.device(self.y, self.turn(self.z + sign), self.c), device_id_type=pl.DeviceIdType.MESH)

    def begin(self):
        for way in (0, 1):
            self.z_copy(way, 1, 0).start()

    def begin_other(self):
        arrived(self.buf.at[0], self.rs.at[0], self.mate)
        for way in (0, 1):
            self.z_copy(way, 1, 1).start()

    def pair_step(self, i):
        d, m = i // 2 + 1, i % 2
        arrived(self.buf.at[pl.ds(0, 1 if d == self.far else 2)], self.rs.at[1 + i], self.mate)
        if d < self.far:
            for way in (0, 1):
                self.z_copy(way, d + 1, m).start()

    def sent(self):
        left(self.buf.at[pl.ds(0, 2 * self.nz - 1)], self.ss.at[0], self.mate)


def relay_kernel(n_sec, n_dp,
                 x_hbm, w_hbm, mw_hbm, gain_ref, mem_hbm, cot_hbm, len_ref,
                 gin_hbm, og, gg_ref,
                 x_ref, mem_ref, cot_ref, gin_ref,
                 wv, wt, mwv, mwt, sc, sg, normed, slope, act, gate, dwt, inv, gbuf, tbuf, tsend,
                 gpv, gacc, gs, ts, gpg, gpt, dws, dwp, dwo, gnv, gng, gnl, gnp,
                 load_sem, wag_s, wag_r, rel_s, rel_r, sag_s, sag_r, g_s, g_r, t_s, t_r, late_s, late_r, pass_s, pass_r, swap_s, swap_r,
                 tail_s, tail_r):
    s = lax.axis_index("section")
    j = lax.axis_index("dp")
    half = n_sec // 2
    nq = n_dp // 2
    nz = nq // 2
    c = lax.rem(j, 2)
    q0 = j // 2
    y, z = q0 // nz, lax.rem(q0, nz)
    toks, feats = x_ref.shape
    rw = mw_hbm.shape[0]
    n_ch = toks // CH
    tiles = feats // TILE
    decoder = s >= half
    encoder = s < half
    above = n_sec - 1 - s
    MESH = pl.DeviceIdType.MESH

    def device(yy, zz, cc):
        return {"dp": (yy * nz + zz) * 2 + cc}

    def load(src, dst, i):
        copy = pltpu.make_async_copy(src, dst, load_sem.at[i])
        copy.start()
        return copy

    barrier = pltpu.get_barrier_semaphore()

    def greet(i, carry):
        q = lax.rem(q0 + i, nq)
        pl.semaphore_signal(barrier, inc=1, device_id={"dp": q * 2 + c}, device_id_type=MESH)
        return carry

    lax.fori_loop(1, nq, greet, 0)
    pl.semaphore_signal(barrier, inc=1, device_id={"dp": q0 * 2 + 1 - c}, device_id_type=MESH)

    @pl.when(s > 0)
    def _():
        pl.semaphore_signal(barrier, inc=1, device_id={"section": s - 1}, device_id_type=MESH)

    @pl.when(s < n_sec - 1)
    def _():
        pl.semaphore_signal(barrier, inc=1, device_id={"section": s + 1}, device_id_type=MESH)

    load_m = pltpu.make_async_copy(
        mw_hbm, mwv.at[pl.ds(pl.multiple_of(j * rw, rw), rw)], load_sem.at[1])

    @pl.when(decoder)
    def _():
        load_m.start()

    load_x = load(x_hbm, x_ref, 2)
    load_w = load(w_hbm, wv, 0)
    load_mem = load(mem_hbm, mem_ref, 3)
    load_cot = load(cot_hbm, cot_ref, 4)

    pl.semaphore_signal(
        barrier, inc=1, device_id={"section": lax.rem(s + half, n_sec), "dp": ((1 - y) * nz + z) * 2 + c},
        device_id_type=MESH)
    ends = (s == 0) | (s == n_sec - 1)
    pl.semaphore_wait(barrier, nq + jnp.where(ends, 2, 3))

    place = (y, z, c, nz, device)

    wag = Gather(mwv, rw, place, wag_s, wag_r)
    relay = Relay(wag, s, half, (rel_s, rel_r))
    sag = HalfGather(sg, place, sag_s, sag_r)
    far = wag.far
    last_pair = 2 * far
    width = feats // 2
    cols_z = feats // nz
    mine, theirs = (pl.ds(pl.multiple_of(v * width, width), width) for v in (y, 1 - y))
    crossing = sc.at[:, theirs]
    mine_z = pl.ds(pl.multiple_of(z * cols_z, cols_z), cols_z)

    @pl.when(decoder)
    def _():
        load_m.wait()
        relay.up().start()
        wag.begin()

    def rows_of(k):
        return pl.ds(pl.multiple_of(k * CH, CH), CH)

    def norm_rows(k, carry):
        rows = rows_of(k)
        wide = x_ref[rows, :].astype(F32)
        scale = lax.rsqrt(jnp.mean(wide * wide, axis=1, keepdims=True) + epsilon)
        inv[rows, :] = jnp.broadcast_to(scale, (CH, 128))
        value = wide * scale
        normed[rows, :] = value
        sc[rows, :] = (value * gain_ref[...]).astype(BF)
        sg[q0, rows, :] = sc[rows, mine]
        return carry

    load_x.wait()
    lax.fori_loop(0, n_ch, norm_rows, 0)

    @pl.when(encoder)
    def _():
        sag.cross(crossing).start()
        relay.begin()
        relay.step(1, 0)
        relay.begin_other()
        for d in range(2, far + 1):
            relay.step(d, 0)
            relay.step(d - 1, 1)
        relay.step(far, 1)
        sag.begin()
        sag.begin_other()

    load_w.wait()

    def cols_of(t):
        return pl.ds(pl.multiple_of(t * TILE, TILE), TILE)

    def preact_tile(t, carry):
        cols = cols_of(t)
        p = jnp.dot(sc[...], wv[:, cols], preferred_element_type=F32)
        sig = jax.nn.sigmoid(p)
        act[:, cols] = p * sig
        slope[:, cols] = sig * (1.0 + p * (1.0 - sig))
        return carry

    lax.fori_loop(0, tiles, preact_tile, 0)
    load_mem.wait()
    load_cot.wait()

    def turn_w(piece, pieces):
        def body(i, carry):
            a, b = i // tiles, lax.rem(i, tiles)
            wt[cols_of(b), cols_of(a)] = wv[cols_of(a), cols_of(b)].T
            return carry

        size = tiles * tiles // pieces
        lax.fori_loop(piece * size, (piece + 1) * size, body, 0, unroll=4)

    def chip_rows(q):
        return pl.ds(pl.multiple_of(q * 2 * rw, 2 * rw), 2 * rw)

    def turn_m(d):
        spots = [chip_rows(q) for q in wag.sources(d)]

        def body(t, carry):
            for at in spots:
                mwt[cols_of(t), at] = mwv[at, cols_of(t)].T
            return carry

        lax.fori_loop(0, tiles, body, 0, unroll=2)

    def gate_part(d):
        spots = [chip_rows(q) for q in wag.sources(d)]
        left = jnp.concatenate([mem_ref[:, at] for at in spots], axis=1)

        def body(t, carry):
            cols = cols_of(t)
            right = jnp.concatenate([mwv[at, cols] for at in spots], axis=0)
            p = jnp.dot(left, right, preferred_element_type=F32)
            if d == 0:
                gate[:, cols] = p
            elif d < far:
                gate[:, cols] += p
            else:
                slope[:, cols] = slope[:, cols] * (gate[:, cols] + p)
            return carry

        lax.fori_loop(0, tiles, body, 0, unroll=4)

    @pl.when(decoder)
    def _():
        wag.begin_other()
        wag.pair_step(0)
        turn_w(0, 4)
        wag.pair_step(1)
        turn_w(1, 4)
        wag.pair_step(2)
        turn_w(2, 4)
        wag.pair_step(3)
        turn_w(3, 4)
        wag.pair_step(4)
        wag.pass_backs(0, relay)
        wag.pair_step(5)
        sag.cross(crossing).start()
        wag.collect(0)
        gate_part(0)
        turn_m(0)
        wag.pair_step(6)
        wag.pass_backs(1, relay)
        wag.pair_step(7)
        wag.collect(1)
        gate_part(1)
        wag.pair_step(8)
        turn_m(1)
        wag.pass_backs(2, relay)
        wag.pair_step(9)
        wag.collect(2)
        gate_part(2)
        wag.pair_step(10)
        turn_m(2)
        wag.pair_step(11)
        wag.pass_backs(3, relay)
        wag.pass_backs(4, relay)
        wag.collect(3)
        gate_part(3)
        turn_m(3)
        wag.collect(4)
        gate_part(4)
        sag.begin()
        turn_m(4)

        @pl.when(above >= 2)
        def _():
            sag.begin_other()
            sag.pair_step(0)

        @pl.when(above >= 3)
        def _():
            sag.pair_step(1)

    @pl.when(encoder)
    def _():
        for piece in range(4):
            turn_w(piece, 4)
        for i in range(last_pair - 2):
            sag.pair_step(i)

    @pl.when(s == n_sec - 1)
    def _():
        live = lax.broadcasted_iota(jnp.int32, (toks, TILE), 0) < len_ref[0]

        def body(t, carry):
            cols = cols_of(t)
            gbuf[:, cols] = jnp.where(live, cot_ref[:, cols], jnp.zeros((), BF))
            return carry

        lax.fori_loop(0, tiles, body, 0)

    gacc[...] = jnp.zeros_like(gacc)

    def down(src, dst, k, send_sems, recv_sems):
        rows = rows_of(k)
        return pltpu.make_async_remote_copy(
            src_ref=src.at[rows], dst_ref=dst.at[rows], send_sem=send_sems.at[0], recv_sem=recv_sems.at[k],
            device_id={"section": s - 1}, device_id_type=MESH)

    groups = [(0, 3 * CH), (3 * CH, 2 * CH), (5 * CH, CH), (6 * CH, CH), (7 * CH, CH)]
    direct = (2, 3, 4)
    round_z = [nz // 2] + [v for i in range(nz // 2 - 1, 0, -1) for v in (i, nz - i)]

    def late_send(g):
        start, size = groups[g]
        rows = pl.ds(start, size)

        def send(yy, zz):
            pltpu.make_async_remote_copy(
                src_ref=gpv.at[rows, pl.ds(pl.multiple_of(zz * cols_z, cols_z), cols_z)], dst_ref=gpg.at[q0, rows],
                send_sem=late_s.at[0], recv_sem=late_r.at[g], device_id=device(yy, zz, c), device_id_type=MESH).start()

        for i in round_z:
            send(y, lax.rem(z + i, nz))
        if g in direct:
            @pl.when(encoder)
            def _():
                for i in round_z + [0]:
                    send(1 - y, lax.rem(z + i, nz))

    def late_done(g, count):
        start, size = groups[g]
        ref = gpg.at[pl.ds(0, count), pl.ds(start, size)]
        return pltpu.make_async_remote_copy(
            src_ref=ref, dst_ref=ref, send_sem=late_s.at[0], recv_sem=late_r.at[g],
            device_id={"dp": q0 * 2 + 1 - c}, device_id_type=MESH)

    def late_recv(g):
        if g not in direct:
            late_done(g, nz - 1).wait_recv()
            return

        @pl.when(encoder)
        def _():
            late_done(g, nq - 1).wait_recv()

        @pl.when(decoder)
        def _():
            late_done(g, nz - 1).wait_recv()

    def late_pass(g):
        start, size = groups[g]
        ref = gpg.at[pl.ds(pl.multiple_of(y * nz, nz), nz), pl.ds(start, size)]
        return pltpu.make_async_remote_copy(
            src_ref=ref, dst_ref=ref, send_sem=pass_s.at[0], recv_sem=pass_r.at[g],
            device_id=device(1 - y, z, c), device_id_type=MESH)

    def term(k):
        rows = rows_of(k)
        up = gbuf[rows, :].astype(F32)
        grad_gate = (up * act[rows, :]).astype(BF)
        for t in range(tiles):
            cols = slice(t * TILE, (t + 1) * TILE)
            ts[:, cols] = jnp.dot(grad_gate, mwt[:, cols], preferred_element_type=F32)

        @pl.when(s < n_sec - 1)
        def _():
            down(tsend, tbuf, k, t_s, t_r).wait_recv()
            tsend[rows, :] = (ts[...] + tbuf[rows, :].astype(F32)).astype(BF)

        @pl.when(s == n_sec - 1)
        def _():
            tsend[rows, :] = ts[...].astype(BF)

    passing = [(0, 3, 0), (0, 7, 1), (1, 1, 0), (1, 3, 1), (1, 6, 2), (2, 1, 1), (2, 4, 2), (2, 6, 3),
               (3, 1, 2), (3, 4, 3), (3, 6, 4)]

    def own_rows(g):
        rows = pl.ds(groups[g][0], groups[g][1])
        gpg[q0, rows, :] = gpv[rows, mine_z]

    def chunk(k, carry):
        rows = rows_of(k)

        @pl.when(s < n_sec - 1)
        def _():
            down(gin_ref, gbuf, k, g_s, g_r).wait_recv()

        @pl.when(encoder & (k == 6))
        def _():
            late_recv(1)
            late_pass(1).start()

        @pl.when(s == half)
        def _():
            term(k)
            down(tsend, gbuf, k, t_s, g_r).start()

        gpv[rows, :] = (gbuf[rows, :].astype(F32) * slope[rows, :]).astype(BF)
        grad_pre = gpv[rows, :]
        total = jnp.zeros((CH, 128), F32)
        for t in range(tiles):
            cols = slice(t * TILE, (t + 1) * TILE)
            p = jnp.dot(grad_pre, wt[:, cols], preferred_element_type=F32)
            both = p * normed[rows, cols]
            gacc[:, cols] += both
            h = p * gain_ref[:, cols]
            gs[:, cols] = h
            weighted = both * gain_ref[:, cols]
            for i in range(TILE // 128):
                total = total + weighted[:, i * 128:(i + 1) * 128]
        center = jnp.sum(total, axis=1, keepdims=True) * (1.0 / feats)
        scale = inv[rows, 0:1]
        for t in range(tiles):
            cols = slice(t * TILE, (t + 1) * TILE)
            gin_ref[rows, cols] = (
                gbuf[rows, cols].astype(F32) + scale * (gs[:, cols] - normed[rows, cols] * center)
            ).astype(BF)

        @pl.when((s > 0) & (s != half))
        def _():
            down(gin_ref, gbuf, k, g_s, g_r).start()

        @pl.when(s > half)
        def _():
            term(k)
            down(tsend, tbuf, k, t_s, t_r).start()

        @pl.when(encoder)
        def _():
            for g, (start, size) in enumerate(groups[:-1]):
                @pl.when(k == (start + size) // CH - 1)
                def _(g=g):
                    late_send(g)
                    own_rows(g)

            @pl.when(k == 3)
            def _():
                sag.pair_step(last_pair - 2)
                sag.pair_step(last_pair - 1)

            @pl.when(k == 5)
            def _():
                late_recv(0)
                late_pass(0).start()

        for up in range(half):
            @pl.when(above == up)
            def _(up=up):
                for at in {0: (2,), 1: (0,)}.get(up, ()):
                    @pl.when(k == at)
                    def _():
                        sag.begin_other()

                for at, i in [(at, i) for v, at, i in passing if v == up]:
                    @pl.when(k == at)
                    def _(i=i):
                        sag.pair_step(i)

        return carry

    lax.fori_loop(0, n_ch, chunk, 0)

    @pl.when(decoder)
    def _():
        for g in range(len(groups) - 1):
            late_send(g)
            own_rows(g)

    late_send(len(groups) - 1)
    part = gacc[...]
    for q in range(nq):
        gnv[q] = part[0:8, q * 128:(q + 1) * 128] + part[8:16, q * 128:(q + 1) * 128]

    def gain_send(i, carry):
        q = lax.rem(q0 + i, nq)
        pltpu.make_async_remote_copy(
            src_ref=gnv.at[q], dst_ref=gng.at[q0], send_sem=tail_s.at[2], recv_sem=tail_r.at[2],
            device_id={"dp": q * 2 + c}, device_id_type=MESH).start()
        return carry

    lax.fori_loop(1, nq, gain_send, 0)
    gng[q0] = gnv[q0]
    store_gin = load(gin_ref, gin_hbm, 5)

    own_rows(len(groups) - 1)

    @pl.when(decoder)
    def _():
        for i in range(2, last_pair):
            @pl.when(i >= 2 + above)
            def _(i=i):
                sag.pair_step(i)

            if 4 <= i:
                late_recv(i - 4)
                late_pass(i - 4).start()
        late_recv(len(groups) - 1)
        late_pass(len(groups) - 1).start()
        for g in range(len(groups)):
            late_pass(g).wait_recv()

    @pl.when(encoder)
    def _():
        late_recv(2)
        late_pass(0).wait_recv()
        late_pass(1).wait_recv()

    most = toks - 2 * CH
    kk = nq * most
    parts = width // TILE
    gpt[:, 0:kk] = gpg[:, 0:most, :].reshape(kk, cols_z).T

    def product(t, carry):
        cols = cols_of(t)
        dwt[:, cols] = jnp.dot(gpt[:, 0:kk], sg[:, 0:most, cols].reshape(kk, TILE), preferred_element_type=F32)
        return carry

    lax.fori_loop(0, parts, product, 0, unroll=2)

    @pl.when(encoder)
    def _():
        late_recv(3)
        late_recv(4)

    gpt[:, kk:nq * toks] = gpg[:, most:toks, :].reshape(nq * 2 * CH, cols_z).T

    other = {"dp": q0 * 2 + 1 - c}
    per = TILE // (2 * rw)
    first_part = z // per

    def swap(t):
        spots = pl.ds(t * per, per)
        return pltpu.make_async_remote_copy(
            src_ref=dws.at[spots, 1 - c], dst_ref=dwp.at[spots], send_sem=swap_s.at[0], recv_sem=swap_r.at[t],
            device_id=other, device_id_type=MESH)

    turns = [parts // 2] + [v for i in range(parts // 2 - 1, 0, -1) for v in (i, parts - i)] + [0]

    def finish(i):
        t = lax.rem(first_part + i, parts)
        cols = cols_of(t)
        p = dwt[:, cols] + jnp.dot(
            gpt[:, kk:nq * toks], sg[:, most:toks, cols].reshape(nq * 2 * CH, TILE), preferred_element_type=F32)
        dws[pl.ds(t * per, per)] = p.T.astype(BF).reshape(per, 2, rw, cols_z)
        swap(t).start()

    for i in turns:
        finish(i)

    def deliver(i):
        t = lax.rem(first_part + i, parts)
        swap(t).wait_recv()
        for e in range(per):
            zz = t * per + e
            dwo[zz] = (dws[zz, c].astype(F32) + dwp[zz].astype(F32)).astype(BF)

            @pl.when(zz != z)
            def _(zz=zz):
                pltpu.make_async_remote_copy(
                    src_ref=dwo.at[zz], dst_ref=og.at[z], send_sem=tail_s.at[1], recv_sem=tail_r.at[1],
                    device_id=device(y, zz, c), device_id_type=MESH).start()

    for i in turns:
        deliver(i)
    store_own = load(dwo.at[z], og.at[z], 0)

    gain_all = pltpu.make_async_remote_copy(
        src_ref=gng.at[pl.ds(0, nq - 1)], dst_ref=gng.at[pl.ds(0, nq - 1)], send_sem=tail_s.at[2],
        recv_sem=tail_r.at[2], device_id=other, device_id_type=MESH)
    gain_all.wait()
    gnl[...] = jnp.sum(gng[...], axis=0)
    gain_copy = pltpu.make_async_remote_copy(
        src_ref=gnl, dst_ref=gnp, send_sem=tail_s.at[0], recv_sem=tail_r.at[0], device_id=other, device_id_type=MESH)
    gain_copy.start()

    near = sum(size for g, (_, size) in enumerate(groups) if g not in direct)
    both = toks - near

    @pl.when(encoder)
    def _():
        left(gpg.at[pl.ds(0, (near * (nz - 1) + both * (nq - 1)) // toks)], late_s.at[0], other)
        left(gpg.at[pl.ds(0, near * nz // toks)], pass_s.at[0], other)

    @pl.when(decoder)
    def _():
        left(gpg.at[pl.ds(0, nz - 1)], late_s.at[0], other)
        left(gpg.at[pl.ds(0, nz)], pass_s.at[0], other)

    @pl.when((s > 0) & (s != half))
    def _():
        left(gin_ref, g_s.at[0], other)

    @pl.when(decoder)
    def _():
        left(tsend, t_s.at[0], other)

    sag.sent()

    @pl.when(decoder)
    def _():
        wag.sent()
        relay.sent(False)

    @pl.when(encoder)
    def _():
        relay.sent(True)

    left(dwp, swap_s.at[0], other)
    store_gin.wait()
    gain_copy.wait()
    gains = jnp.sum(gnl[...] + gnp[...], axis=0, keepdims=True) * (1.0 / n_dp)
    gg_ref[...] = jnp.where(c == 0, gains[:, 0:rw], gains[:, rw:2 * rw])

    whole = pltpu.make_async_remote_copy(
        src_ref=dwo.at[pl.ds(0, nz - 1)], dst_ref=og.at[pl.ds(0, nz - 1)], send_sem=tail_s.at[1],
        recv_sem=tail_r.at[1], device_id=other, device_id_type=MESH)
    store_own.wait()
    whole.wait()


def publish_kernel(n_dp, gin_ref, blocks_ref, gain_ref, gin_out, dw_out, gain_out):
    gin_out[...] = gin_ref[...]
    nz, _, cols_z = blocks_ref.shape
    for zz in range(nz):
        dw_out[:, zz * cols_z:(zz + 1) * cols_z] = blocks_ref[zz].astype(F32) * (1.0 / n_dp)
    gain_out[...] = gain_ref[...]


def local(section_inputs, section_weights, memory_weights, norm_gains, memory, cotangent, lengths):
    n_sec, n_dp = lax.axis_size("section"), lax.axis_size("dp")
    toks, feats = section_inputs.shape[1:]
    rw = memory_weights.shape[1]
    nq = n_dp // 2
    nz = nq // 2
    n_ch = toks // CH
    vmem = pl.BlockSpec(memory_space=pltpu.VMEM)
    hbm = pl.BlockSpec(memory_space=pl.ANY)
    square = pltpu.VMEM((feats, feats), BF)
    wide = pltpu.VMEM((toks, feats), F32)
    narrow = pltpu.VMEM((toks, feats), BF)
    cols_z = feats // nz
    blocks = pltpu.VMEM((nz, rw, cols_z), BF)
    dma = pltpu.SemaphoreType.DMA
    gin, dw, gg = pl.pallas_call(
        functools.partial(relay_kernel, n_sec, n_dp),
        out_shape=(
            jax.ShapeDtypeStruct((toks, feats), BF),
            jax.ShapeDtypeStruct((nz, rw, cols_z), BF),
            jax.ShapeDtypeStruct((1, rw), F32),
        ),
        in_specs=[hbm, hbm, hbm, vmem, hbm, hbm, pl.BlockSpec(memory_space=pltpu.SMEM)],
        out_specs=(hbm, hbm, vmem),
        scratch_shapes=[
            narrow, narrow, narrow, narrow,
            square, square, square, square, narrow,
            pltpu.VMEM((nq, toks, feats // 2), BF),
            wide, wide, wide, wide,
            pltpu.VMEM((cols_z, feats // 2), F32),
            pltpu.VMEM((toks, 128), F32),
            narrow, narrow, narrow,
            narrow,
            pltpu.VMEM((CH, feats), F32),
            pltpu.VMEM((CH, feats), F32),
            pltpu.VMEM((CH, feats), F32),
            pltpu.VMEM((nq, toks, cols_z), BF),
            pltpu.VMEM((cols_z, nq * toks), BF),
            pltpu.VMEM((nz, 2, rw, cols_z), BF),
            blocks, blocks,
            pltpu.VMEM((nq, 8, 128), F32),
            pltpu.VMEM((nq, 8, 128), F32),
            pltpu.VMEM((8, 128), F32),
            pltpu.VMEM((8, 128), F32),
            dma((6,)),
            dma((1,)), dma((Gather.count(nz),)),
            dma((1,)), dma((Relay.count(nz),)),
            dma((1,)), dma((HalfGather.count(nz),)),
            dma((1,)), dma((n_ch,)), dma((1,)), dma((n_ch,)),
            dma((1,)), dma((5,)),
            dma((1,)), dma((5,)),
            dma((1,)), dma((feats // 2 // TILE,)),
            dma((3,)), dma((3,)),
        ],
        compiler_params=pltpu.CompilerParams(
            collective_id=0, has_side_effects=True, vmem_limit_bytes=60 * 1024 * 1024
        ),
    )(
        section_inputs[0], section_weights[0], memory_weights[0], norm_gains, memory, cotangent,
        lengths,
    )
    gin, dw, gg = pl.pallas_call(
        functools.partial(publish_kernel, n_dp),
        out_shape=(
            jax.ShapeDtypeStruct((toks, feats), BF),
            jax.ShapeDtypeStruct((rw, feats), F32),
            jax.ShapeDtypeStruct((1, rw), F32),
        ),
        in_specs=[vmem] * 3,
        out_specs=(vmem,) * 3,
    )(gin, dw, gg)
    return gin[None], dw[None], gg


def solution(mesh):
    return jax.shard_map(
        local,
        mesh=mesh,
        in_specs=(
            P("section", "dp", None),
            P("section", None, None),
            P("section", "dp", None),
            P("section", None),
            P("dp", None),
            P("dp", None),
            P("dp"),
        ),
        out_specs=(P("section", "dp", None), P("section", "dp", None), P("section", "dp")),
        check_vma=False,
    )
```

```python
import functools

import jax
import jax.numpy as jnp
from jax import lax
from jax.experimental import pallas as pl
from jax.experimental.pallas import tpu as pltpu
from jax.sharding import PartitionSpec as P

epsilon = 1e-06
BF = jnp.bfloat16
F32 = jnp.float32
CH = 16
TILE = 256


def arrived(ref, sem, dev):
    pltpu.make_async_remote_copy(
        src_ref=ref, dst_ref=ref, send_sem=sem, recv_sem=sem, device_id=dev,
        device_id_type=pl.DeviceIdType.MESH).wait_recv()


def left(ref, sem, dev):
    pltpu.make_async_remote_copy(
        src_ref=ref, dst_ref=ref, send_sem=sem, recv_sem=sem, device_id=dev,
        device_id_type=pl.DeviceIdType.MESH).wait_send()


class Gather:
    def __init__(self, buf, rows, place, send_sem, recv_sems, lane=None):
        self.buf, self.rows, self.place = buf, rows, place
        self.y, self.z, self.c, self.nz, self.device = place
        self.lane = self.c if lane is None else lane
        self.far = self.nz // 2
        self.ss, self.rs = send_sem, recv_sems
        self.mate = self.device(self.y, self.z, 1 - self.c)

    @staticmethod
    def count(nz):
        return 5 * (nz // 2) + 3

    def block(self, q, start, size):
        return self.buf.at[pl.ds(pl.multiple_of((q * 2 + self.lane) * self.rows + start, 16), size)]

    def copy(self, q, start, size, ident, dev):
        ref = self.block(q, start, size)
        return pltpu.make_async_remote_copy(
            src_ref=ref, dst_ref=ref, send_sem=self.ss.at[0], recv_sem=self.rs.at[ident],
            device_id=dev, device_id_type=pl.DeviceIdType.MESH)

    def await_rows(self, rows, ident):
        arrived(self.buf.at[pl.ds(0, rows)], self.rs.at[ident], self.mate)

    def turn(self, z):
        return lax.rem(z + 2 * self.nz, self.nz)

    def source(self, way, d):
        return self.turn(self.z - (1 - 2 * way) * d)

    def ways(self, d, m=0):
        return (0,) if d == 0 or (d == self.far and m == 1) else (0, 1)

    def span(self, way, d, m):
        half, quarter = self.rows // 2, self.rows // 4
        if m in (1, 3):
            return (half if m == 1 else half + quarter), quarter
        return (way * quarter, quarter) if d == self.far else (0, half)

    def z_copy(self, way, d, m):
        y = 1 - self.y if m == 2 else self.y
        start, size = self.span(way, d, m)
        dev = self.device(self.y, self.turn(self.z + 1 - 2 * way), self.c)
        return self.copy(y * self.nz + self.source(way, d - 1), start, size, 3 * (d - 1) + m, dev)

    def y_copy(self, way, d):
        start, size = self.span(way, d, 1)
        dev = self.device(1 - self.y, self.z, self.c)
        return self.copy(self.y * self.nz + self.source(way, d), start, size, 3 * self.far + d, dev)

    def first_copy(self):
        dev = self.device(1 - self.y, self.z, self.c)
        return self.copy(self.y * self.nz + self.z, 0, self.rows // 2, 4 * self.far + 1, dev)

    def hand(self, kind, args):
        ident = 4 * self.far + 2
        if kind in ("own", "first"):
            y = self.y if kind == "own" else 1 - self.y
            self.copy(y * self.nz + self.z, 0, self.size(kind, args), ident, self.mate).start()
            return
        way, d, m = args
        start, size = self.span(way, d, 3 if kind == "back" else m)
        y = {"z": 1 - self.y if m == 2 else self.y, "back": 1 - self.y if m else self.y, "y": 1 - self.y}[kind]
        self.copy(y * self.nz + self.source(way, d), start, size, ident + d, self.mate).start()

    def size(self, kind, args):
        if kind in ("own", "first"):
            return self.rows if kind == "own" else self.rows // 2
        way, d, m = args
        return self.span(way, d, 3 if kind == "back" else m)[1]

    def begin(self):
        self.first_copy().start()
        for m in (1, 0):
            for way in (0, 1):
                self.z_copy(way, 1, m).start()
        self.y_copy(0, 0).start()
        self.hand("own", ())

    def begin_other(self):
        self.await_rows(self.rows // 2, 4 * self.far + 1)
        for way in (0, 1):
            self.z_copy(way, 1, 2).start()
        self.hand("first", ())

    def pair_step(self, i):
        d, m = i // 3 + 1, (1, 0, 2)[i % 3]
        self.await_rows(sum(self.span(way, d, m)[1] for way in self.ways(d, m)), 3 * (d - 1) + m)
        if d < self.far:
            for way in self.ways(d + 1, m):
                self.z_copy(way, d + 1, m).start()
        for way in self.ways(d, m):
            if m == 1:
                self.y_copy(way, d).start()
            self.hand("z", (way, d, m))

    def backs(self, d):
        if d == 0:
            return [(0, 0, 1)]
        return [(0, d, 0), (1, d, 1)] if d == self.far else [(way, d, m) for m in (0, 1) for way in (0, 1)]

    def crossed(self, d):
        return [(way, d, 1) for way in self.ways(d, 1)]

    def handed(self, d):
        if d == 0:
            came = [("own", ()), ("first", ())]
        else:
            came = [("z", (way, d, m)) for m in (0, 1, 2) for way in self.ways(d, m)]
        return came + [("back", args) for args in self.backs(d)] + [("y", args) for args in self.crossed(d)]

    def pass_backs(self, d, relay):
        relay.await_back(d)
        for args in self.backs(d):
            self.hand("back", args)
        self.await_rows(sum(self.size("y", args) for args in self.crossed(d)), 3 * self.far + d)
        for args in self.crossed(d):
            self.hand("y", args)

    def collect(self, d):
        self.await_rows(sum(self.size(*h) for h in self.handed(d)), 4 * self.far + 2 + d)

    def sent(self):
        total = self.rows // 2
        for d in range(self.far + 1):
            total += sum(self.size("y", args) for args in self.crossed(d))
            total += sum(self.size(*h) * (2 if h[0] == "z" else 1) for h in self.handed(d))
        left(self.buf.at[pl.ds(0, total)], self.ss.at[0], self.mate)

    def sources(self, d):
        spots = {0: (0,), self.far: (self.far,)}.get(d, (d, -d))
        return [y * self.nz + self.turn(self.z + o) for o in spots for y in (0, 1)]


class Relay:
    def __init__(self, gather, section, half, sems):
        self.g, self.ss, self.rs = gather, *sems
        g = gather
        self.quarter = g.rows // 4
        self.partner = {
            "section": jnp.where(section >= half, section - half, section + half),
            "dp": ((1 - g.y) * g.nz + g.z) * 2 + g.c,
        }

    @staticmethod
    def count(nz):
        return 3 + 3 * (nz // 2)

    def copy(self, y, src, ident, dev):
        g = self.g
        start, size = g.span(0, 1, 3)
        ref = g.block(y * g.nz + src, start, size)
        return pltpu.make_async_remote_copy(
            src_ref=ref, dst_ref=ref, send_sem=self.ss.at[0], recv_sem=self.rs.at[ident],
            device_id=dev, device_id_type=pl.DeviceIdType.MESH)

    def await_quarters(self, number, ident):
        arrived(self.g.buf.at[pl.ds(0, number * self.quarter)], self.rs.at[ident], self.partner)

    def await_back(self, d):
        self.await_quarters(len(self.g.backs(d)), 2 + 2 * self.g.far + d)

    def up(self):
        return self.copy(self.g.y, self.g.z, 0, self.partner)

    def ring(self, way, d, m):
        g = self.g
        dev = g.device(g.y, g.turn(g.z + 1 - 2 * way), g.c)
        return self.copy(g.y if m else 1 - g.y, g.source(way, d - 1), 2 + 2 * (d - 1) + m, dev)

    def back(self, way, d, m):
        g = self.g
        return self.copy(g.y if m else 1 - g.y, g.source(way, d), 2 + 2 * g.far + d, self.partner)

    def begin(self):
        g = self.g
        self.await_quarters(1, 0)
        self.copy(1 - g.y, g.z, 1, g.device(1 - g.y, g.z, g.c)).start()
        for way in (0, 1):
            self.ring(way, 1, 0).start()

    def begin_other(self):
        self.await_quarters(1, 1)
        for way in (0, 1):
            self.ring(way, 1, 1).start()
        self.back(0, 0, 1).start()

    def step(self, d, m):
        g = self.g
        came = [args for args in g.backs(d) if args[2] == m]
        self.await_quarters(len(came), 2 + 2 * (d - 1) + m)
        for way, _, _ in came:
            if d < g.far and (way, d + 1, m) in g.backs(d + 1):
                self.ring(way, d + 1, m).start()
            self.back(way, d, m).start()

    def sent(self, encoder):
        number = 2 + 2 * sum(len(self.g.backs(d)) for d in range(1, self.g.far + 1)) if encoder else 1
        left(self.g.buf.at[pl.ds(0, number * self.quarter)], self.ss.at[0], self.partner)


class HalfGather:
    def __init__(self, buf, place, send_sem, recv_sems):
        self.buf, self.ss, self.rs = buf, send_sem, recv_sems
        self.y, self.z, self.c, self.nz, self.device = place
        self.far = self.nz // 2
        self.rows = buf.shape[1]
        self.mate = self.device(self.y, self.z, 1 - self.c)

    @staticmethod
    def count(nz):
        return 1 + 2 * (nz // 2)

    def turn(self, z):
        return lax.rem(z + 2 * self.nz, self.nz)

    def cross(self, src):
        return pltpu.make_async_remote_copy(
            src_ref=src, dst_ref=self.buf.at[self.y * self.nz + self.z], send_sem=self.ss.at[0],
            recv_sem=self.rs.at[0], device_id=self.device(1 - self.y, self.z, self.c),
            device_id_type=pl.DeviceIdType.MESH)

    def z_copy(self, way, d, m):
        sign = 1 - 2 * way
        src = self.turn(self.z - sign * (d - 1))
        y = 1 - self.y if m else self.y
        size = self.rows // 2 if d == self.far else self.rows
        ref = self.buf.at[y * self.nz + src, pl.ds(way * size if d == self.far else 0, size)]
        return pltpu.make_async_remote_copy(
            src_ref=ref, dst_ref=ref, send_sem=self.ss.at[0], recv_sem=self.rs.at[1 + 2 * (d - 1) + m],
            device_id=self.device(self.y, self.turn(self.z + sign), self.c), device_id_type=pl.DeviceIdType.MESH)

    def begin(self):
        for way in (0, 1):
            self.z_copy(way, 1, 0).start()

    def begin_other(self):
        arrived(self.buf.at[0], self.rs.at[0], self.mate)
        for way in (0, 1):
            self.z_copy(way, 1, 1).start()

    def pair_step(self, i):
        d, m = i // 2 + 1, i % 2
        arrived(self.buf.at[pl.ds(0, 1 if d == self.far else 2)], self.rs.at[1 + i], self.mate)
        if d < self.far:
            for way in (0, 1):
                self.z_copy(way, d + 1, m).start()

    def sent(self):
        left(self.buf.at[pl.ds(0, 2 * self.nz - 1)], self.ss.at[0], self.mate)


def relay_kernel(n_sec, n_dp,
                 x_hbm, w_hbm, mw_hbm, gain_ref, mem_hbm, cot_hbm, len_ref,
                 gin_hbm, og, gg_ref,
                 x_ref, mem_ref, cot_ref, gin_ref,
                 wv, wt, mwv, mwt, sc, sg, normed, slope, act, gate, dwt, inv, gbuf, tbuf, tsend,
                 gpv, gacc, gs, ts, gpg, gpt, dws, dwp, dwo, gnv, gng, gnl, gnp,
                 load_sem, wag_s, wag_r, rel_s, rel_r, sag_s, sag_r, g_s, g_r, t_s, t_r, late_s, late_r, pass_s, pass_r, swap_s, swap_r,
                 tail_s, tail_r):
    s = lax.axis_index("section")
    j = lax.axis_index("dp")
    half = n_sec // 2
    nq = n_dp // 2
    nz = nq // 2
    c = lax.rem(j, 2)
    q0 = j // 2
    y, z = q0 // nz, lax.rem(q0, nz)
    toks, feats = x_ref.shape
    rw = mw_hbm.shape[0]
    n_ch = toks // CH
    tiles = feats // TILE
    decoder = s >= half
    encoder = s < half
    above = n_sec - 1 - s
    MESH = pl.DeviceIdType.MESH

    def device(yy, zz, cc):
        return {"dp": (yy * nz + zz) * 2 + cc}

    def load(src, dst, i):
        copy = pltpu.make_async_copy(src, dst, load_sem.at[i])
        copy.start()
        return copy

    barrier = pltpu.get_barrier_semaphore()

    def greet(i, carry):
        q = lax.rem(q0 + i, nq)
        pl.semaphore_signal(barrier, inc=1, device_id={"dp": q * 2 + c}, device_id_type=MESH)
        return carry

    lax.fori_loop(1, nq, greet, 0)
    pl.semaphore_signal(barrier, inc=1, device_id={"dp": q0 * 2 + 1 - c}, device_id_type=MESH)

    @pl.when(s > 0)
    def _():
        pl.semaphore_signal(barrier, inc=1, device_id={"section": s - 1}, device_id_type=MESH)

    @pl.when(s < n_sec - 1)
    def _():
        pl.semaphore_signal(barrier, inc=1, device_id={"section": s + 1}, device_id_type=MESH)

    load_m = pltpu.make_async_copy(
        mw_hbm, mwv.at[pl.ds(pl.multiple_of(j * rw, rw), rw)], load_sem.at[1])

    @pl.when(decoder)
    def _():
        load_m.start()

    load_x = load(x_hbm, x_ref, 2)
    load_w = load(w_hbm, wv, 0)
    load_mem = load(mem_hbm, mem_ref, 3)
    load_cot = load(cot_hbm, cot_ref, 4)

    pl.semaphore_signal(
        barrier, inc=1, device_id={"section": lax.rem(s + half, n_sec), "dp": ((1 - y) * nz + z) * 2 + c},
        device_id_type=MESH)
    ends = (s == 0) | (s == n_sec - 1)
    pl.semaphore_wait(barrier, nq + jnp.where(ends, 2, 3))

    place = (y, z, c, nz, device)

    wag = Gather(mwv, rw, place, wag_s, wag_r)
    relay = Relay(wag, s, half, (rel_s, rel_r))
    sag = HalfGather(sg, place, sag_s, sag_r)
    far = wag.far
    last_pair = 2 * far
    width = feats // 2
    cols_z = feats // nz
    mine, theirs = (pl.ds(pl.multiple_of(v * width, width), width) for v in (y, 1 - y))
    crossing = sc.at[:, theirs]
    mine_z = pl.ds(pl.multiple_of(z * cols_z, cols_z), cols_z)

    @pl.when(decoder)
    def _():
        load_m.wait()
        relay.up().start()
        wag.begin()

    def rows_of(k):
        return pl.ds(pl.multiple_of(k * CH, CH), CH)

    def norm_rows(k, carry):
        rows = rows_of(k)
        wide = x_ref[rows, :].astype(F32)
        scale = lax.rsqrt(jnp.mean(wide * wide, axis=1, keepdims=True) + epsilon)
        inv[rows, :] = jnp.broadcast_to(scale, (CH, 128))
        value = wide * scale
        normed[rows, :] = value
        sc[rows, :] = (value * gain_ref[...]).astype(BF)
        sg[q0, rows, :] = sc[rows, mine]
        return carry

    load_x.wait()
    lax.fori_loop(0, n_ch, norm_rows, 0)

    @pl.when(encoder)
    def _():
        sag.cross(crossing).start()
        relay.begin()
        relay.step(1, 0)
        relay.begin_other()
        for d in range(2, far + 1):
            relay.step(d, 0)
            relay.step(d - 1, 1)
        relay.step(far, 1)
        sag.begin()
        sag.begin_other()

    load_w.wait()

    def cols_of(t):
        return pl.ds(pl.multiple_of(t * TILE, TILE), TILE)

    def preact_tile(t, carry):
        cols = cols_of(t)
        p = jnp.dot(sc[...], wv[:, cols], preferred_element_type=F32)
        sig = jax.nn.sigmoid(p)
        act[:, cols] = p * sig
        slope[:, cols] = sig * (1.0 + p * (1.0 - sig))
        return carry

    lax.fori_loop(0, tiles, preact_tile, 0)
    load_mem.wait()
    load_cot.wait()

    def turn_w(piece, pieces):
        def body(i, carry):
            a, b = i // tiles, lax.rem(i, tiles)
            wt[cols_of(b), cols_of(a)] = wv[cols_of(a), cols_of(b)].T
            return carry

        size = tiles * tiles // pieces
        lax.fori_loop(piece * size, (piece + 1) * size, body, 0, unroll=4)

    def chip_rows(q):
        return pl.ds(pl.multiple_of(q * 2 * rw, 2 * rw), 2 * rw)

    def turn_m(d):
        spots = [chip_rows(q) for q in wag.sources(d)]

        def body(t, carry):
            for at in spots:
                mwt[cols_of(t), at] = mwv[at, cols_of(t)].T
            return carry

        lax.fori_loop(0, tiles, body, 0, unroll=2)

    def gate_part(d):
        spots = [chip_rows(q) for q in wag.sources(d)]
        left = jnp.concatenate([mem_ref[:, at] for at in spots], axis=1)

        def body(t, carry):
            cols = cols_of(t)
            right = jnp.concatenate([mwv[at, cols] for at in spots], axis=0)
            p = jnp.dot(left, right, preferred_element_type=F32)
            if d == 0:
                gate[:, cols] = p
            elif d < far:
                gate[:, cols] += p
            else:
                slope[:, cols] = slope[:, cols] * (gate[:, cols] + p)
            return carry

        lax.fori_loop(0, tiles, body, 0, unroll=4)

    @pl.when(decoder)
    def _():
        wag.begin_other()
        wag.pair_step(0)
        turn_w(0, 4)
        wag.pair_step(1)
        turn_w(1, 4)
        wag.pair_step(2)
        turn_w(2, 4)
        wag.pair_step(3)
        turn_w(3, 4)
        wag.pair_step(4)
        wag.pass_backs(0, relay)
        wag.pair_step(5)
        sag.cross(crossing).start()
        wag.collect(0)
        gate_part(0)
        turn_m(0)
        wag.pair_step(6)
        wag.pass_backs(1, relay)
        wag.pair_step(7)
        wag.collect(1)
        gate_part(1)
        wag.pair_step(8)
        turn_m(1)
        wag.pass_backs(2, relay)
        wag.pair_step(9)
        wag.collect(2)
        gate_part(2)
        wag.pair_step(10)
        turn_m(2)
        wag.pair_step(11)
        wag.pass_backs(3, relay)
        wag.pass_backs(4, relay)
        wag.collect(3)
        gate_part(3)
        turn_m(3)
        wag.collect(4)
        gate_part(4)
        sag.begin()
        turn_m(4)

        @pl.when(above >= 2)
        def _():
            sag.begin_other()
            sag.pair_step(0)

        @pl.when(above >= 3)
        def _():
            sag.pair_step(1)

    @pl.when(encoder)
    def _():
        for piece in range(4):
            turn_w(piece, 4)
        for i in range(last_pair - 2):
            sag.pair_step(i)

    @pl.when(s == n_sec - 1)
    def _():
        live = lax.broadcasted_iota(jnp.int32, (toks, TILE), 0) < len_ref[0]

        def body(t, carry):
            cols = cols_of(t)
            gbuf[:, cols] = jnp.where(live, cot_ref[:, cols], jnp.zeros((), BF))
            return carry

        lax.fori_loop(0, tiles, body, 0)

    gacc[...] = jnp.zeros_like(gacc)

    def down(src, dst, k, send_sems, recv_sems):
        rows = rows_of(k)
        return pltpu.make_async_remote_copy(
            src_ref=src.at[rows], dst_ref=dst.at[rows], send_sem=send_sems.at[0], recv_sem=recv_sems.at[k],
            device_id={"section": s - 1}, device_id_type=MESH)

    groups = [(0, 3 * CH)] + [(i * CH, CH) for i in range(3, n_ch)]
    direct = (2, 3, 4, 5)
    round_z = [nz // 2] + [v for i in range(nz // 2 - 1, 0, -1) for v in (i, nz - i)]

    def late_send(g):
        start, size = groups[g]
        rows = pl.ds(start, size)

        def send(yy, zz):
            pltpu.make_async_remote_copy(
                src_ref=gpv.at[rows, pl.ds(pl.multiple_of(zz * cols_z, cols_z), cols_z)], dst_ref=gpg.at[q0, rows],
                send_sem=late_s.at[0], recv_sem=late_r.at[g], device_id=device(yy, zz, c), device_id_type=MESH).start()

        for i in round_z:
            send(y, lax.rem(z + i, nz))
        if g in direct:
            @pl.when(encoder)
            def _():
                for i in round_z + [0]:
                    send(1 - y, lax.rem(z + i, nz))

    def late_done(g, count):
        start, size = groups[g]
        ref = gpg.at[pl.ds(0, count), pl.ds(start, size)]
        return pltpu.make_async_remote_copy(
            src_ref=ref, dst_ref=ref, send_sem=late_s.at[0], recv_sem=late_r.at[g],
            device_id={"dp": q0 * 2 + 1 - c}, device_id_type=MESH)

    def late_recv(g):
        if g not in direct:
            late_done(g, nz - 1).wait_recv()
            return

        @pl.when(encoder)
        def _():
            late_done(g, nq - 1).wait_recv()

        @pl.when(decoder)
        def _():
            late_done(g, nz - 1).wait_recv()

    def late_pass(g):
        start, size = groups[g]
        ref = gpg.at[pl.ds(pl.multiple_of(y * nz, nz), nz), pl.ds(start, size)]
        return pltpu.make_async_remote_copy(
            src_ref=ref, dst_ref=ref, send_sem=pass_s.at[0], recv_sem=pass_r.at[g],
            device_id=device(1 - y, z, c), device_id_type=MESH)

    def term(k):
        rows = rows_of(k)
        up = gbuf[rows, :].astype(F32)
        grad_gate = (up * act[rows, :]).astype(BF)
        for t in range(tiles):
            cols = slice(t * TILE, (t + 1) * TILE)
            ts[:, cols] = jnp.dot(grad_gate, mwt[:, cols], preferred_element_type=F32)

        @pl.when(s < n_sec - 1)
        def _():
            down(tsend, tbuf, k, t_s, t_r).wait_recv()
            tsend[rows, :] = (ts[...] + tbuf[rows, :].astype(F32)).astype(BF)

        @pl.when(s == n_sec - 1)
        def _():
            tsend[rows, :] = ts[...].astype(BF)

    passing = [(0, 3, 0), (0, 7, 1), (1, 1, 0), (1, 3, 1), (1, 6, 2), (2, 1, 1), (2, 4, 2), (2, 6, 3),
               (3, 1, 2), (3, 4, 3), (3, 6, 4)]

    def own_rows(g):
        rows = pl.ds(groups[g][0], groups[g][1])
        gpg[q0, rows, :] = gpv[rows, mine_z]

    def chunk(k, carry):
        rows = rows_of(k)

        @pl.when(s < n_sec - 1)
        def _():
            down(gin_ref, gbuf, k, g_s, g_r).wait_recv()

        @pl.when(s == half)
        def _():
            term(k)
            down(tsend, gbuf, k, t_s, g_r).start()

        gpv[rows, :] = (gbuf[rows, :].astype(F32) * slope[rows, :]).astype(BF)
        grad_pre = gpv[rows, :]
        total = jnp.zeros((CH, 128), F32)
        for t in range(tiles):
            cols = slice(t * TILE, (t + 1) * TILE)
            p = jnp.dot(grad_pre, wt[:, cols], preferred_element_type=F32)
            both = p * normed[rows, cols]
            gacc[:, cols] += both
            h = p * gain_ref[:, cols]
            gs[:, cols] = h
            weighted = both * gain_ref[:, cols]
            for i in range(TILE // 128):
                total = total + weighted[:, i * 128:(i + 1) * 128]
        center = jnp.sum(total, axis=1, keepdims=True) * (1.0 / feats)
        scale = inv[rows, 0:1]
        for t in range(tiles):
            cols = slice(t * TILE, (t + 1) * TILE)
            gin_ref[rows, cols] = (
                gbuf[rows, cols].astype(F32) + scale * (gs[:, cols] - normed[rows, cols] * center)
            ).astype(BF)

        @pl.when((s > 0) & (s != half))
        def _():
            down(gin_ref, gbuf, k, g_s, g_r).start()

        @pl.when(s > half)
        def _():
            term(k)
            down(tsend, tbuf, k, t_s, t_r).start()

        @pl.when(encoder)
        def _():
            for g, (start, size) in enumerate(groups[:-1]):
                @pl.when(k == (start + size) // CH - 1)
                def _(g=g):
                    late_send(g)
                    own_rows(g)

            @pl.when(k == 3)
            def _():
                sag.pair_step(last_pair - 2)
                sag.pair_step(last_pair - 1)

            for g, at in ((0, 5), (1, 6)):
                @pl.when(k == at)
                def _(g=g):
                    late_recv(g)
                    late_pass(g).start()

        for up in range(half):
            @pl.when(above == up)
            def _(up=up):
                for at in {0: (2,), 1: (0,)}.get(up, ()):
                    @pl.when(k == at)
                    def _():
                        sag.begin_other()

                for at, i in [(at, i) for v, at, i in passing if v == up]:
                    @pl.when(k == at)
                    def _(i=i):
                        sag.pair_step(i)

        return carry

    lax.fori_loop(0, n_ch, chunk, 0)

    @pl.when(decoder)
    def _():
        for g in range(len(groups) - 1):
            late_send(g)
            own_rows(g)

    late_send(len(groups) - 1)
    part = gacc[...]
    for q in range(nq):
        gnv[q] = part[0:8, q * 128:(q + 1) * 128] + part[8:16, q * 128:(q + 1) * 128]

    def gain_send(i, carry):
        q = lax.rem(q0 + i, nq)
        pltpu.make_async_remote_copy(
            src_ref=gnv.at[q], dst_ref=gng.at[q0], send_sem=tail_s.at[2], recv_sem=tail_r.at[2],
            device_id={"dp": q * 2 + c}, device_id_type=MESH).start()
        return carry

    lax.fori_loop(1, nq, gain_send, 0)
    gng[q0] = gnv[q0]
    store_gin = load(gin_ref, gin_hbm, 5)

    own_rows(len(groups) - 1)

    @pl.when(decoder)
    def _():
        for i in range(2, last_pair):
            @pl.when(i >= 2 + above)
            def _(i=i):
                sag.pair_step(i)

            if 3 <= i:
                late_recv(i - 3)
                late_pass(i - 3).start()
        late_recv(len(groups) - 1)
        late_pass(len(groups) - 1).start()
        for g in range(len(groups)):
            late_pass(g).wait_recv()

    @pl.when(encoder)
    def _():
        late_recv(2)
        late_recv(3)
        late_pass(0).wait_recv()
        late_pass(1).wait_recv()

    most = toks - 2 * CH
    kk = nq * most
    parts = width // TILE
    gpt[:, 0:kk] = gpg[:, 0:most, :].reshape(kk, cols_z).T

    def product(t, carry):
        cols = cols_of(t)
        dwt[:, cols] = jnp.dot(gpt[:, 0:kk], sg[:, 0:most, cols].reshape(kk, TILE), preferred_element_type=F32)
        return carry

    lax.fori_loop(0, parts, product, 0, unroll=2)

    @pl.when(encoder)
    def _():
        late_recv(4)
        late_recv(5)

    gpt[:, kk:nq * toks] = gpg[:, most:toks, :].reshape(nq * 2 * CH, cols_z).T

    other = {"dp": q0 * 2 + 1 - c}
    per = TILE // (2 * rw)
    first_part = z // per

    def swap(t):
        spots = pl.ds(t * per, per)
        return pltpu.make_async_remote_copy(
            src_ref=dws.at[spots, 1 - c], dst_ref=dwp.at[spots], send_sem=swap_s.at[0], recv_sem=swap_r.at[t],
            device_id=other, device_id_type=MESH)

    turns = [parts // 2] + [v for i in range(parts // 2 - 1, 0, -1) for v in (i, parts - i)] + [0]

    def finish(i):
        t = lax.rem(first_part + i, parts)
        cols = cols_of(t)
        p = dwt[:, cols] + jnp.dot(
            gpt[:, kk:nq * toks], sg[:, most:toks, cols].reshape(nq * 2 * CH, TILE), preferred_element_type=F32)
        dws[pl.ds(t * per, per)] = p.T.astype(BF).reshape(per, 2, rw, cols_z)
        swap(t).start()

    for i in turns:
        finish(i)

    def deliver(i):
        t = lax.rem(first_part + i, parts)
        swap(t).wait_recv()
        for e in range(per):
            zz = t * per + e
            dwo[zz] = (dws[zz, c].astype(F32) + dwp[zz].astype(F32)).astype(BF)

            @pl.when(zz != z)
            def _(zz=zz):
                pltpu.make_async_remote_copy(
                    src_ref=dwo.at[zz], dst_ref=og.at[z], send_sem=tail_s.at[1], recv_sem=tail_r.at[1],
                    device_id=device(y, zz, c), device_id_type=MESH).start()

    for i in turns:
        deliver(i)
    store_own = load(dwo.at[z], og.at[z], 0)

    gain_all = pltpu.make_async_remote_copy(
        src_ref=gng.at[pl.ds(0, nq - 1)], dst_ref=gng.at[pl.ds(0, nq - 1)], send_sem=tail_s.at[2],
        recv_sem=tail_r.at[2], device_id=other, device_id_type=MESH)
    gain_all.wait()
    gnl[...] = jnp.sum(gng[...], axis=0)
    gain_copy = pltpu.make_async_remote_copy(
        src_ref=gnl, dst_ref=gnp, send_sem=tail_s.at[0], recv_sem=tail_r.at[0], device_id=other, device_id_type=MESH)
    gain_copy.start()

    near = sum(size for g, (_, size) in enumerate(groups) if g not in direct)
    both = toks - near

    @pl.when(encoder)
    def _():
        left(gpg.at[pl.ds(0, (near * (nz - 1) + both * (nq - 1)) // toks)], late_s.at[0], other)
        left(gpg.at[pl.ds(0, near * nz // toks)], pass_s.at[0], other)

    @pl.when(decoder)
    def _():
        left(gpg.at[pl.ds(0, nz - 1)], late_s.at[0], other)
        left(gpg.at[pl.ds(0, nz)], pass_s.at[0], other)

    @pl.when((s > 0) & (s != half))
    def _():
        left(gin_ref, g_s.at[0], other)

    @pl.when(decoder)
    def _():
        left(tsend, t_s.at[0], other)

    sag.sent()

    @pl.when(decoder)
    def _():
        wag.sent()
        relay.sent(False)

    @pl.when(encoder)
    def _():
        relay.sent(True)

    left(dwp, swap_s.at[0], other)
    store_gin.wait()
    gain_copy.wait()
    gains = jnp.sum(gnl[...] + gnp[...], axis=0, keepdims=True) * (1.0 / n_dp)
    gg_ref[...] = jnp.where(c == 0, gains[:, 0:rw], gains[:, rw:2 * rw])

    whole = pltpu.make_async_remote_copy(
        src_ref=dwo.at[pl.ds(0, nz - 1)], dst_ref=og.at[pl.ds(0, nz - 1)], send_sem=tail_s.at[1],
        recv_sem=tail_r.at[1], device_id=other, device_id_type=MESH)
    store_own.wait()
    whole.wait()


def publish_kernel(n_dp, gin_ref, blocks_ref, gain_ref, gin_out, dw_out, gain_out):
    gin_out[...] = gin_ref[...]
    nz, _, cols_z = blocks_ref.shape
    for zz in range(nz):
        dw_out[:, zz * cols_z:(zz + 1) * cols_z] = blocks_ref[zz].astype(F32) * (1.0 / n_dp)
    gain_out[...] = gain_ref[...]


def local(section_inputs, section_weights, memory_weights, norm_gains, memory, cotangent, lengths):
    n_sec, n_dp = lax.axis_size("section"), lax.axis_size("dp")
    toks, feats = section_inputs.shape[1:]
    rw = memory_weights.shape[1]
    nq = n_dp // 2
    nz = nq // 2
    n_ch = toks // CH
    vmem = pl.BlockSpec(memory_space=pltpu.VMEM)
    hbm = pl.BlockSpec(memory_space=pl.ANY)
    square = pltpu.VMEM((feats, feats), BF)
    wide = pltpu.VMEM((toks, feats), F32)
    narrow = pltpu.VMEM((toks, feats), BF)
    cols_z = feats // nz
    blocks = pltpu.VMEM((nz, rw, cols_z), BF)
    dma = pltpu.SemaphoreType.DMA
    gin, dw, gg = pl.pallas_call(
        functools.partial(relay_kernel, n_sec, n_dp),
        out_shape=(
            jax.ShapeDtypeStruct((toks, feats), BF),
            jax.ShapeDtypeStruct((nz, rw, cols_z), BF),
            jax.ShapeDtypeStruct((1, rw), F32),
        ),
        in_specs=[hbm, hbm, hbm, vmem, hbm, hbm, pl.BlockSpec(memory_space=pltpu.SMEM)],
        out_specs=(hbm, hbm, vmem),
        scratch_shapes=[
            narrow, narrow, narrow, narrow,
            square, square, square, square, narrow,
            pltpu.VMEM((nq, toks, feats // 2), BF),
            wide, wide, wide, wide,
            pltpu.VMEM((cols_z, feats // 2), F32),
            pltpu.VMEM((toks, 128), F32),
            narrow, narrow, narrow,
            narrow,
            pltpu.VMEM((CH, feats), F32),
            pltpu.VMEM((CH, feats), F32),
            pltpu.VMEM((CH, feats), F32),
            pltpu.VMEM((nq, toks, cols_z), BF),
            pltpu.VMEM((cols_z, nq * toks), BF),
            pltpu.VMEM((nz, 2, rw, cols_z), BF),
            blocks, blocks,
            pltpu.VMEM((nq, 8, 128), F32),
            pltpu.VMEM((nq, 8, 128), F32),
            pltpu.VMEM((8, 128), F32),
            pltpu.VMEM((8, 128), F32),
            dma((6,)),
            dma((1,)), dma((Gather.count(nz),)),
            dma((1,)), dma((Relay.count(nz),)),
            dma((1,)), dma((HalfGather.count(nz),)),
            dma((1,)), dma((n_ch,)), dma((1,)), dma((n_ch,)),
            dma((1,)), dma((6,)),
            dma((1,)), dma((6,)),
            dma((1,)), dma((feats // 2 // TILE,)),
            dma((3,)), dma((3,)),
        ],
        compiler_params=pltpu.CompilerParams(
            collective_id=0, has_side_effects=True, vmem_limit_bytes=60 * 1024 * 1024
        ),
    )(
        section_inputs[0], section_weights[0], memory_weights[0], norm_gains, memory, cotangent,
        lengths,
    )
    gin, dw, gg = pl.pallas_call(
        functools.partial(publish_kernel, n_dp),
        out_shape=(
            jax.ShapeDtypeStruct((toks, feats), BF),
            jax.ShapeDtypeStruct((rw, feats), F32),
            jax.ShapeDtypeStruct((1, rw), F32),
        ),
        in_specs=[vmem] * 3,
        out_specs=(vmem,) * 3,
    )(gin, dw, gg)
    return gin[None], dw[None], gg


def solution(mesh):
    return jax.shard_map(
        local,
        mesh=mesh,
        in_specs=(
            P("section", "dp", None),
            P("section", None, None),
            P("section", "dp", None),
            P("section", None),
            P("dp", None),
            P("dp", None),
            P("dp"),
        ),
        out_specs=(P("section", "dp", None), P("section", "dp", None), P("section", "dp")),
        check_vma=False,
    )
```
